256 devices in a mesh: dp: 256 (over z, y, x, core).
Axes of the slice: x: 4, y: 4, z: 8, core: 2. Of those that a mesh axis runs over, the one named last changes fastest.
Arguments:
- inputs: bfloat16 [98304, 1024], P('dp'), may hold values from -8 to 8
- grad_out: bfloat16 [98304, 1024], P('dp'), may hold values from -0.019042969 to 0.019042969
- norm_gain: float32 [1024], replicated, may hold values from 0.5 to 1.5
- master: float32 [1024, 4096], P('dp'), may hold values from -0.25 to 0.25
- projector: bfloat16 [1024, 256], P('dp'), may hold values from -0.1875 to 0.1875
- moment_first: float32 [256, 4096], P('dp'), may hold values from -0.6 to 0.6
- moment_second: float32 [256, 4096], P('dp'), may hold values from 0.001 to 0.01
- doc_lengths: int32 [256, 4], P('dp'), may hold values from 1 to 192, 384 in all within a row
Outputs:
- new_master: float32 [1024, 4096], P('dp')
- new_first: float32 [256, 4096], P('dp')
- new_second: float32 [256, 4096], P('dp')
The draws below stay inside these ranges and needn't reach their ends.
All inputs are finite; a program needn't handle non-finite values.
Results may differ from the reference program's by a relative error of at most 0.0025.
Values may be sent and summed in bfloat16 or wider, within the bound.
A program may use at most 128 MiB of HBM per device.

```python
import math
import jax
import jax.numpy as jnp
import numpy as np
from jax import lax

D = 1024
DH = 64
HEADS = 16
RANK = 256
TOK_DEV = 384
DOCS = 4
DOC_MOST = 192
TOKENS = 98304
N_DP = 256


def gain_values(key):
    noise = jax.random.normal(jax.random.fold_in(key, 7002), (D,), jnp.float32)
    return 1.0 + 0.1 * jnp.clip(noise, -5.0, 5.0)


def draw_norm_gain(key, part):
    return gain_values(key)


def draw_inputs(key, part):
    own_key = jax.random.fold_in(key, 21)
    noise = jax.random.normal(jax.random.fold_in(own_key, 1), (TOKENS, D), jnp.float32)
    values = jnp.clip(noise, -6.0, 6.0)
    return values.astype(jnp.bfloat16)


def draw_master(key, part):
    own_key = jax.random.fold_in(key, 31)
    width = 4 * HEADS * DH
    natural = jnp.clip(jax.random.normal(own_key, (D, width), jnp.float32), -6.0, 6.0) * D ** (-0.5)
    return natural


def levels(key, extent, cuts, least, high):
    loudness = 1.0
    for axis_at, parts in cuts:
        heights = jax.random.uniform(jax.random.fold_in(jax.random.fold_in(key, 6), axis_at), (parts,), jnp.float32, least / len(cuts), high / len(cuts))
        loudness = loudness * jnp.repeat(jnp.exp(heights), extent[axis_at] // parts).reshape((-1,) + (1,) * (len(extent) - 1 - axis_at))
    return loudness


def length_profile(count, total, reach, slope):
    loads = [(1 << 20) // math.isqrt(standing ** slope) + 1 for standing in range(2, count + 1)]
    rest, given = total - reach - (count - 1), [1] * (count - 1)
    while rest > 0:
        movable = [i for i in range(count - 1) if given[i] < reach]
        whole, remaining = sum([loads[i] for i in movable]), rest
        for i in movable:
            more = min(reach - given[i], max(1, remaining * loads[i] // whole), rest)
            given[i] = given[i] + more
            rest = rest - more
    return np.array([reach] + given)


def ragged_sizes(rng, amount, total, bound, slope):
    if amount == 2:
        one = jax.random.randint(rng, (), max(1, total - bound), min(bound, total - 1) + 1)
        return jnp.stack([one, total - one])
    tallies = jnp.asarray(length_profile(amount, total, bound, slope), jnp.int32)
    twos = (amount - 1) // 2
    donor, taker = tallies[1:1 + 2 * twos:2], tallies[2:2 + 2 * twos:2]
    room = jnp.minimum(donor - 1, bound - taker)
    passed = jax.random.randint(jax.random.fold_in(rng, 1), (twos,), 0, 1 << 20) % (room + 1)
    tallies = tallies.at[1:1 + 2 * twos:2].set(donor - passed).at[2:2 + 2 * twos:2].set(taker + passed)
    return tallies[jax.random.permutation(jax.random.fold_in(rng, 2), amount)]


def bell_draw(rng, extent, deviation, reach, cuts=(), kind=jnp.bfloat16):
    result = jax.random.normal(rng, extent, jnp.float32) * deviation
    if len(cuts) > 0:
        result = levels(rng, extent, cuts, -0.22, 0.18) * result
    return jnp.clip(result, min=-reach, max=reach).astype(kind)


def setup_inputs(seed: int = 0) -> dict:
    keys = jax.random.split(jax.random.key(seed), 9)
    inputs = draw_inputs(jax.random.fold_in(keys[8], 71), 0)
    grad_out = bell_draw(keys[1], (TOKENS, D), ((TOK_DEV * N_DP) ** -0.5), 0.019042969, ((0, 256),))
    norm_gain = draw_norm_gain(jax.random.fold_in(keys[8], 71), 0)
    master = draw_master(jax.random.fold_in(keys[8], 71), 0)
    projector = bell_draw(keys[4], (D, RANK), D ** -0.5, 0.1875, ((0, 256),))
    moment_first = bell_draw(keys[5], (RANK, 4 * HEADS * DH), 0.1, 0.6, ((0, 256),), jnp.float32)
    moment_second = jnp.clip(jnp.exp(math.log(0.01) - 2.30258502 * jax.random.uniform(keys[6], (RANK, 4 * HEADS * DH), jnp.float32) ** levels(keys[6], (RANK, 4 * HEADS * DH), ((0, 256),), -0.2, 0.2)), 0.001, 0.01)
    doc_lengths = jax.vmap(lambda own: ragged_sizes(own, DOCS, TOK_DEV, DOC_MOST, 2))(jax.random.split(keys[7], N_DP)).reshape((N_DP, DOCS)).astype(jnp.int32)
    return dict(inputs=inputs, grad_out=grad_out, norm_gain=norm_gain, master=master, projector=projector, moment_first=moment_first, moment_second=moment_second, doc_lengths=doc_lengths)


beta_one = 0.9
beta_two = 0.999
adam_eps = 1e-08
adam_step = 10.0
learn_rate = 0.01
galore_scale = 0.25
norm_eps = 1e-05

def doc_mask(lengths_row, count):
    position = jnp.arange(count, dtype=jnp.int32)
    bounds = jnp.cumsum(lengths_row).astype(jnp.int32)
    segment = lax.optimization_barrier(jnp.sum((position[:, None] >= bounds[None, :]).astype(jnp.int32), axis=1))
    return (segment[:, None] == segment[None, :]) & (position[:, None] >= position[None, :])

def attend(queries, key_rows, value_rows, grad_head, visible):
    highest = lax.Precision.HIGHEST
    factor = queries.shape[1] ** (-0.5)
    scores = jnp.dot(queries, key_rows.T, preferred_element_type=jnp.float32) * factor
    scores = jnp.where(visible, scores, jnp.float32(-1e+30))
    row_max = lax.optimization_barrier(jnp.max(scores, axis=1, keepdims=True))
    lifted = jnp.exp(scores - row_max)
    probs = lifted / lax.optimization_barrier(jnp.sum(lifted, axis=1, keepdims=True))
    attended = jnp.dot(probs.astype(jnp.bfloat16), value_rows, preferred_element_type=jnp.float32).astype(jnp.bfloat16)
    grad_values = jnp.dot(probs.T, grad_head, precision=highest)
    grad_probs = jnp.dot(grad_head, value_rows.astype(jnp.float32).T, precision=highest)
    grad_scores = probs * (grad_probs - lax.optimization_barrier(jnp.sum(probs * grad_probs, axis=1, keepdims=True)))
    grad_queries = jnp.dot(grad_scores, key_rows.astype(jnp.float32), precision=highest) * factor
    grad_keys = jnp.dot(grad_scores.T, queries.astype(jnp.float32), precision=highest) * factor
    return (attended, grad_queries, grad_keys, grad_values)

def attend_heads(projected, grad_head, lengths_row, head_size):
    count = projected.shape[0]
    width = grad_head.shape[1]
    heads = width // head_size
    visible = doc_mask(lengths_row, count)
    queries = projected[:, :width].reshape(count, heads, head_size)
    key_rows = projected[:, width:2 * width].reshape(count, heads, head_size)
    value_rows = projected[:, 2 * width:].reshape(count, heads, head_size)
    grad_rows = grad_head.reshape(count, heads, head_size)
    per_head = jax.vmap(attend, in_axes=(1, 1, 1, 1, None), out_axes=1)
    attended, grad_queries, grad_keys, grad_values = per_head(queries, key_rows, value_rows, grad_rows, visible)
    grad_projected = jnp.concatenate([grad_queries.reshape(count, width), grad_keys.reshape(count, width), grad_values.reshape(count, width)], axis=1).astype(jnp.bfloat16)
    return (attended.reshape(count, width), grad_projected)

def normalize(inputs, norm_gain):
    values = inputs.astype(jnp.float32)
    scale = lax.rsqrt(lax.optimization_barrier(jnp.mean(values * values, axis=1, keepdims=True)) + norm_eps)
    return (values * scale * norm_gain[None, :]).astype(jnp.bfloat16)

def adam_update(low, moment_first, moment_second):
    new_first = beta_one * moment_first + (1.0 - beta_one) * low
    new_second = beta_two * moment_second + (1.0 - beta_two) * low * low
    direction = new_first / (1.0 - beta_one ** adam_step) / (jnp.sqrt(new_second / (1.0 - beta_two ** adam_step)) + adam_eps)
    return (new_first, new_second, direction)

def reference(inputs, grad_out, norm_gain, master, projector, moment_first, moment_second, doc_lengths):
    highest = lax.Precision.HIGHEST
    width = HEADS * DH
    weights = master.astype(jnp.bfloat16)
    inner_weights = weights[:, :3 * width]
    outer_weights = weights[:, 3 * width:]
    contract = (((0,), (0,)), ((), ()))
    input_blocks = inputs.reshape(N_DP, TOK_DEV, D)
    grad_blocks = grad_out.reshape(N_DP, TOK_DEV, D)

    def one_block(total, packed):
        block_in, block_grad, lengths_row = packed
        normed = normalize(block_in, norm_gain)
        projected = jnp.dot(normed, inner_weights, preferred_element_type=jnp.float32).astype(jnp.bfloat16)
        grad_head = jnp.dot(block_grad, outer_weights, preferred_element_type=jnp.float32)
        attended, grad_projected = attend_heads(projected, grad_head, lengths_row, DH)
        grad_inner = lax.dot_general(normed, grad_projected, contract, preferred_element_type=jnp.float32)
        grad_outer = lax.dot_general(block_grad, attended, contract, preferred_element_type=jnp.float32)
        return (total + jnp.concatenate([grad_inner, grad_outer], axis=1), None)
    start = jnp.zeros((D, 4 * width), jnp.float32)
    grads, unused = lax.scan(one_block, start, (input_blocks, grad_blocks, doc_lengths))
    proj_float = projector.astype(jnp.float32)
    low = lax.dot_general(proj_float, grads, contract, precision=highest)
    new_first, new_second, direction = adam_update(low, moment_first, moment_second)
    new_master = master - learn_rate * galore_scale * jnp.dot(proj_float, direction, precision=highest)
    return (new_master, new_first, new_second)
```

```python
import jax
import jax.numpy as jnp
import numpy as np
from jax import lax
from jax.experimental import pallas as pl
from jax.experimental.pallas import tpu as pltpu
from jax.sharding import PartitionSpec as P

NZ, NY, NX, NC = 8, 4, 4, 2
SIZE = {"z": NZ, "y": NY, "x": NX}
TOK = 384
WIDTH = 1024
RANK = 256
PART = 384
VMEM_LIMIT = 56 * 1024 * 1024

beta_one = 0.9
beta_two = 0.999
adam_eps = 1e-08
adam_step = 10.0
learn_rate = 0.01
galore_scale = 0.25
norm_eps = 1e-05

F32 = jnp.float32
BF16 = jnp.bfloat16
MESH = pl.DeviceIdType.MESH


def place():
    me = lax.axis_index("dp")
    c = lax.rem(me, NC)
    x = lax.rem(me // NC, NX)
    y = lax.rem(me // (NC * NX), NY)
    z = me // (NC * NX * NY)
    return {"z": z, "y": y, "x": x, "c": c}


def device_at(where, **moved):
    at = dict(where, **moved)
    return ((at["z"] * NY + at["y"]) * NX + at["x"]) * NC + at["c"]


def shifted(where, axis, by):
    n = SIZE[axis]
    return lax.rem(where[axis] + (by + n), n)


class Sender:
    def __init__(self, send_sems, recv_sems):
        self.send_sems, self.recv_sems = send_sems, recv_sems
        self.copies = []

    def send(self, src, dst, device):
        i = len(self.copies)
        copy = pltpu.make_async_remote_copy(
            src_ref=src,
            dst_ref=dst,
            send_sem=self.send_sems.at[i],
            recv_sem=self.recv_sems.at[i],
            device_id=(device,),
            device_id_type=MESH,
        )
        copy.start()
        self.copies.append(copy)
        return copy

    def finish(self):
        for copy in self.copies:
            copy.wait_send()


def greet(devices):
    barrier = pltpu.get_barrier_semaphore()
    for device in devices:
        pl.semaphore_signal(barrier, inc=1, device_id=(device,), device_id_type=MESH)
    pl.semaphore_wait(barrier, len(devices))


def run_together(steps):
    live = list(steps)
    while live:
        still = []
        for step in live:
            try:
                next(step)
                still.append(step)
            except StopIteration:
                pass
        live = still


ORDERS = (("x", "y", "z"), ("y", "z", "x"), ("z", "x", "y"))


def gather_part(part, order, where, sender, piece, w_ref, local_sem, from_sibling):
    c = where["c"]
    sibling = device_at(where, c=1 - c)

    def chunk(stage, value, half=None, core=c):
        index = {}
        for i, axis in enumerate(order):
            if i < stage:
                index[axis] = slice(None)
            elif i == stage:
                index[axis] = value
            else:
                index[axis] = where[axis]
        if half is not None:
            n = SIZE[order[0]] // 2
            index[order[0]] = pl.ds(half * n, n)
        return w_ref.at[part, core, index["z"], index["y"], index["x"]]

    own = w_ref.at[part, c, where["z"], where["y"], where["x"]]
    local = pltpu.make_async_copy(piece.at[part], own, local_sem)
    local.start()
    for stage in range(3):
        axis = order[stage]
        n = SIZE[axis]
        right = device_at(where, **{axis: shifted(where, axis, 1)})
        left = device_at(where, **{axis: shifted(where, axis, -1)})
        last = stage == 2

        def pass_on(ref):
            if last:
                from_sibling.append(sender.send(ref, ref, sibling))

        start = chunk(stage, where[axis])
        src = piece.at[part] if stage == 0 else start
        to_right = sender.send(src, start, right)
        to_left = sender.send(src, start, left)
        pass_on(start)
        for step in range(1, n // 2):
            yield
            end = step == n // 2 - 1
            behind = shifted(where, axis, -step)
            ahead = shifted(where, axis, step)
            to_right.wait_recv()
            got = chunk(stage, behind)
            if not end:
                to_right = sender.send(got, got, right)
            elif stage == 0:
                to_right = sender.send(got, got, right)
            else:
                ref = chunk(stage, behind, 0)
                to_right = sender.send(ref, ref, right)
            pass_on(got)
            to_left.wait_recv()
            got = chunk(stage, ahead)
            if not end:
                to_left = sender.send(got, got, left)
            elif stage == 0:
                to_left = None
            else:
                ref = chunk(stage, ahead, 1)
                to_left = sender.send(ref, ref, left)
            pass_on(got)
        yield
        to_right.wait_recv()
        if to_left is not None:
            to_left.wait_recv()
        pass_on(chunk(stage, shifted(where, axis, n // 2)))
        if stage == 0:
            local.wait()


def weights_kernel(
    master_ref, proj_ref, w_ref, quad_w, quad_p, own_p, rows_w, rows_p, piece,
    local_sems, send_sems, recv_sems
):
    where = place()
    c, x = where["c"], where["x"]
    flip = x + 1 - 2 * lax.rem(x, 2)
    neighbours = [device_at(where, c=1 - c), device_at(where, x=flip, c=1 - c)]
    for axis in "xyz":
        for by in (1, -1):
            neighbours.append(device_at(where, **{axis: shifted(where, axis, by)}))
    greet(neighbours)
    sender = Sender(send_sems, recv_sems)
    own_p[...] = proj_ref[...].astype(F32)
    mine = lax.rem(x, 2) * 2 + c
    quad = []
    for dx, dc in ((0, 1), (1, 0), (1, 1)):
        to_x = flip if dx else x
        to_c = 1 - c if dc else c
        other = lax.rem(to_x, 2) * 2 + to_c
        to = device_at(where, x=to_x, c=to_c)
        columns = pl.ds(pl.multiple_of(other * WIDTH, WIDTH), WIDTH)
        quad.append(sender.send(master_ref.at[:, columns], quad_w.at[mine], to))
        quad.append(sender.send(own_p, quad_p.at[mine], to))
    columns = pl.ds(pl.multiple_of(mine * WIDTH, WIDTH), WIDTH)
    quad_w[mine] = master_ref[:, columns]
    quad_p[mine] = own_p[...]
    for copy in quad:
        copy.wait_recv()
    for i in range(4):
        rows_w[i * 4 : i * 4 + 4, :] = quad_w[i]
        rows_p[i * 4 : i * 4 + 4, :] = quad_p[i]
    piece[0] = rows_w[:, :PART].astype(BF16)
    piece[1] = rows_w[:, PART : 2 * PART].astype(BF16)
    piece[2, :, :256] = rows_w[:, 2 * PART :].astype(BF16)
    halves = jnp.where(c == 0, rows_p[:, :128], rows_p[:, 128:])
    piece[2, :, 256:] = halves.astype(BF16)
    from_sibling = []
    run_together(
        [
            gather_part(
                i, ORDERS[i], where, sender, piece, w_ref, local_sems.at[i], from_sibling
            )
            for i in range(3)
        ]
    )
    for copy in from_sibling:
        copy.wait_recv()
    sender.finish()


def gather_weights(master, proj):
    n_sems = 96
    return pl.pallas_call(
        weights_kernel,
        out_shape=jax.ShapeDtypeStruct((3, NC, NZ, NY, NX, 16, PART), BF16),
        in_specs=[pl.BlockSpec(memory_space=pltpu.VMEM)] * 2,
        out_specs=pl.BlockSpec(memory_space=pl.ANY),
        scratch_shapes=[
            pltpu.VMEM((4, 4, WIDTH), F32),
            pltpu.VMEM((4, 4, RANK), F32),
            pltpu.VMEM((4, RANK), F32),
            pltpu.VMEM((16, WIDTH), F32),
            pltpu.VMEM((16, RANK), F32),
            pltpu.VMEM((3, 16, PART), BF16),
            pltpu.SemaphoreType.DMA((3,)),
            pltpu.SemaphoreType.DMA((n_sems,)),
            pltpu.SemaphoreType.DMA((n_sems,)),
        ],
        compiler_params=pltpu.CompilerParams(
            collective_id=0, has_side_effects=True, vmem_limit_bytes=VMEM_LIMIT
        ),
        name="gather_weights",
    )(master, proj)


def dot(a, b, dims=((1,), (0,))):
    return lax.dot_general(a, b, (dims, ((), ())), preferred_element_type=F32)


ROWS = ((1,), (1,))
COLS = ((0,), (0,))


def split(value):
    high = value.astype(BF16)
    return high, (value - high.astype(F32)).astype(BF16)


def local_kernel(
    len_ref, in_ref, gout_ref, gain_ref, w_ref, low_ref,
    normed, q_s, k_s, v_s, gh_s, low_in, bias, np_t, gp_t
):
    values = in_ref[...].astype(F32)
    scale = lax.rsqrt(jnp.mean(values * values, axis=1, keepdims=True) + norm_eps)
    normed[...] = (values * scale * gain_ref[...]).astype(BF16)

    b0 = len_ref[0, 0]
    b1 = b0 + len_ref[0, 1]
    b2 = b1 + len_ref[0, 2]
    b3 = b2 + len_ref[0, 3]

    def segment(position):
        return sum((position >= b).astype(jnp.int32) for b in (b0, b1, b2, b3))

    row = lax.broadcasted_iota(jnp.int32, (TOK, 1), 0)
    col = lax.broadcasted_iota(jnp.int32, (1, TOK), 1)
    seen = (segment(row) == segment(col)) & (row >= col)
    bias[...] = jnp.where(seen, F32(0.0), F32(-1e30))

    def weight(part, xl, c, lo, hi):
        return w_ref[part, c, :, :, :, xl, :, lo:hi].reshape(WIDTH, hi - lo)

    def project(part, pairs):
        wide = pairs * 128
        for i in range(pairs):
            pass
        res = dot(normed[...], weight(part, 0, 0, 0, wide)).astype(BF16)
        for i in range(pairs):
            q_s[3 * part + i] = res[:, i * 128 : (i + 1) * 128]
        res = dot(normed[...], weight(part, 0, 1, 0, wide)).astype(BF16)
        for i in range(pairs):
            k_s[3 * part + i] = res[:, i * 128 : (i + 1) * 128]
        res = dot(normed[...], weight(part, 1, 0, 0, wide)).astype(BF16)
        for i in range(pairs):
            v_s[3 * part + i] = res[:, i * 128 : (i + 1) * 128]
        res = dot(gout_ref[...], weight(part, 1, 1, 0, wide))
        for i in range(pairs):
            gh_s[3 * part + i] = res[:, i * 128 : (i + 1) * 128]

    @pl.loop(0, 2)
    def _(part):
        project(part, 3)

    project(2, 2)
    for c in range(2):
        proj = weight(2, 0, c, 256, 384)
        rows = slice(c * 128, (c + 1) * 128)
        for src, out in ((normed, np_t), (gout_ref, gp_t)):
            high, rest = split(dot(src[...], proj))
            out[0, :, rows] = high
            out[1, :, rows] = rest

    lane = lax.broadcasted_iota(jnp.int32, (1, 128), 1)
    firsts = (lane < 64).astype(BF16)
    masks = (firsts, 1 - firsts)

    @pl.loop(0, 8)
    def _(pair):
        q, k, v = q_s[pair], k_s[pair], v_s[pair]
        gh_high, gh_rest = split(gh_s[pair])
        v_twice = jnp.concatenate([v, v], axis=1)
        total_q = total_k = total_v = total_a = None
        for mask in masks:
            s = dot(q * mask, k, ROWS) * 0.125 + bias[...]
            e = jnp.exp(s - jnp.max(s, axis=1, keepdims=True))
            p = e / jnp.sum(e, axis=1, keepdims=True)
            p_high, p_rest = split(p)
            a = dot(p_high, v * mask)
            gh_m = gh_high * mask
            gh_both = jnp.concatenate([gh_m, gh_rest * mask], axis=1)
            gv = dot(p_high, gh_both, COLS)
            gv = gv[:, :128] + gv[:, 128:] + dot(p_rest, gh_m, COLS)
            gp = dot(gh_both, v_twice, ROWS)
            gs = p * (gp - jnp.sum(p * gp, axis=1, keepdims=True))
            gs_high, gs_rest = split(gs)
            k_m, q_m = k * mask, q * mask
            gq = dot(gs_high, k_m) + dot(gs_rest, k_m)
            gk = dot(gs_high, q_m, COLS) + dot(gs_rest, q_m, COLS)
            if total_q is None:
                total_q, total_k, total_v, total_a = gq, gk, gv, a
            else:
                total_q, total_k = total_q + gq, total_k + gk
                total_v, total_a = total_v + gv, total_a + a
        grads = jnp.concatenate(
            [
                (total_q * 0.125).astype(BF16),
                (total_k * 0.125).astype(BF16),
                total_v.astype(BF16),
            ],
            axis=1,
        )
        low = dot(np_t[0], grads, COLS) + dot(np_t[1], grads, COLS)
        for i in range(3):
            columns = pl.ds(pl.multiple_of(i * WIDTH + pair * 128, 128), 128)
            low_ref[:, columns] = low[:, i * 128 : (i + 1) * 128]
        attended = total_a.astype(BF16)
        columns = pl.ds(pl.multiple_of(3 * WIDTH + pair * 128, 128), 128)
        low_ref[:, columns] = dot(gp_t[0], attended, COLS) + dot(gp_t[1], attended, COLS)


def local_terms(lengths, inputs, grad_out, gain, weights):
    vmem = pl.BlockSpec(memory_space=pltpu.VMEM)
    return pl.pallas_call(
        local_kernel,
        out_shape=jax.ShapeDtypeStruct((RANK, 4 * WIDTH), F32),
        in_specs=[pl.BlockSpec(memory_space=pltpu.SMEM)] + [vmem] * 4,
        out_specs=vmem,
        scratch_shapes=[
            pltpu.VMEM((TOK, WIDTH), BF16),
            pltpu.VMEM((8, TOK, 128), BF16),
            pltpu.VMEM((8, TOK, 128), BF16),
            pltpu.VMEM((8, TOK, 128), BF16),
            pltpu.VMEM((8, TOK, 128), F32),
            pltpu.VMEM((8, 128), F32),
            pltpu.VMEM((TOK, TOK), F32),
            pltpu.VMEM((2, TOK, RANK), BF16),
            pltpu.VMEM((2, TOK, RANK), BF16),
        ],
        compiler_params=pltpu.CompilerParams(vmem_limit_bytes=VMEM_LIMIT),
        name="local_terms",
    )(lengths, inputs, grad_out, gain, weights)


def update_kernel(
    low_ref, first_ref, second_ref, master_ref, prep_ref,
    new_master, new_first, new_second,
    r0, send_a, send_b, recv_a, recv_b, acc_a, acc_b, recv2_a, recv2_b,
    rows, recv3, dir_rows, tiles, lhs, send_sems, recv_sems
):
    where = place()
    c, x, y, z = where["c"], where["x"], where["y"], where["z"]
    sibling = device_at(where, c=1 - c)

    def peer(axis, by):
        return device_at(where, **{axis: shifted(where, axis, by)})

    greet([sibling] + [peer(a, k) for a in "xyz" for k in range(1, SIZE[a])])
    sender = Sender(send_sems, recv_sems)
    half = 2 * WIDTH
    left, right = slice(0, half), slice(half, 2 * half)

    core = [
        sender.send(low_ref.at[1 - c, :, :, :, part], r0.at[:, :, :, part], sibling)
        for part in (left, right)
    ]
    lane = lax.rem(lax.broadcasted_iota(jnp.int32, (16, 4 * WIDTH), 1), 16)
    diagonal = lane == lax.broadcasted_iota(jnp.int32, (16, 4 * WIDTH), 0)
    for i in range(4):
        line = prep_ref[i : i + 1, :]
        lhs[i * 16 : (i + 1) * 16, :] = jnp.where(diagonal, line, F32(0.0)).astype(BF16)

    core[0].wait_recv()
    sent_a, sent_b = [], []
    for k in (2, 1, 3, 0):
        to = shifted(where, "x", k)
        value = (low_ref[c, to, :, :, left] + r0[to, :, :, left]).reshape(32, half)
        if k:
            send_a[k - 1] = value.astype(BF16)
            sent_a.append(sender.send(send_a.at[k - 1], recv_a.at[k - 1], peer("x", k)))
        else:
            acc_a[...] = value.reshape(NY, 8, half)
    core[1].wait_recv()
    for k in (2, 1, 3, 0):
        to = shifted(where, "y", k)
        value = (low_ref[c, :, to, :, right] + r0[:, to, :, right]).reshape(32, half)
        if k:
            send_b[k - 1] = value.astype(BF16)
            sent_b.append(sender.send(send_b.at[k - 1], recv_b.at[k - 1], peer("y", k)))
        else:
            acc_b[...] = value.reshape(NX, 8, half)
    second = []
    for copies, recv, acc, recv2, axis in (
        (sent_a, recv_a, acc_a, recv2_a, "y"),
        (sent_b, recv_b, acc_b, recv2_b, "x"),
    ):
        for copy in copies:
            copy.wait_recv()
        total = (recv[0].astype(F32) + recv[1].astype(F32)) + recv[2].astype(F32)
        acc[...] = acc[...] + total.reshape(4, 8, half)
        for k in (2, 1, 3):
            to = shifted(where, axis, k)
            second.append(sender.send(acc.at[to], recv2.at[k - 1], peer(axis, k)))
    for copies, acc, recv2, axis, base in (
        (second[:3], acc_a, recv2_a, "y", 0),
        (second[3:], acc_b, recv2_b, "x", half),
    ):
        for copy in copies:
            copy.wait_recv()
        total = acc[where[axis]] + ((recv2[0] + recv2[1]) + recv2[2])
        for i in range(NZ):
            rows[i, :, base : base + half] = total[i : i + 1, :]
    third = []
    for k in (4, 3, 5, 2, 6, 1, 7):
        to = shifted(where, "z", k)
        third.append(sender.send(rows.at[to], recv3.at[k - 1], peer("z", k)))
    low = rows[z]
    for copy in third:
        copy.wait_recv()
    for k in range(NZ - 1):
        low = low + recv3[k]

    first = beta_one * first_ref[...] + (1.0 - beta_one) * low
    second_moment = beta_two * second_ref[...] + (1.0 - beta_two) * low * low
    new_first[...] = first
    new_second[...] = second_moment
    direction = (
        first
        / (1.0 - beta_one**adam_step)
        / (jnp.sqrt(second_moment / (1.0 - beta_two**adam_step)) + adam_eps)
    )
    for a in range(16):
        dir_rows[a : a + 1, :] = direction[:, a * 256 : (a + 1) * 256]
    for p in range(2):
        tiles[p, c, z, y, x] = dir_rows[:, p * 128 : (p + 1) * 128].astype(BF16)

    copies = []
    for k in (4, 3, 5, 2, 6, 1, 7):
        mine = tiles.at[:, c, z, y, x]
        copies.append(sender.send(mine, mine, peer("z", k)))
    for copy in copies:
        copy.wait_recv()
    sent = [[], []]
    for k in (2, 1, 3):
        for p, axis in ((0, "y"), (1, "x")):
            mine = tiles.at[p, c, :, y, x]
            sent[p].append(sender.send(mine, mine, peer(axis, k)))
    final, across = [], []
    for p, axis in ((0, "x"), (1, "y")):
        for copy in sent[p]:
            copy.wait_recv()
        mine = tiles.at[0, c, :, :, x] if p == 0 else tiles.at[1, c, :, y, :]
        for k in (2, 1, 3):
            final.append((p, axis, k, sender.send(mine, mine, peer(axis, k))))
        across.append(sender.send(mine, mine, sibling))
    for p, axis, k, copy in final:
        copy.wait_recv()
        at = shifted(where, axis, -k)
        got = tiles.at[0, c, :, :, at] if p == 0 else tiles.at[1, c, :, at, :]
        across.append(sender.send(got, got, sibling))
    for copy in across:
        copy.wait_recv()
    for p in range(2):
        step = dot(lhs[...], tiles[p].reshape(RANK * 16, 128))
        columns = slice(p * 128, (p + 1) * 128)
        new_master[:, columns] = master_ref[:, columns] - learn_rate * galore_scale * step
    sender.finish()


def update(low, first, second, master, prep):
    vmem = pl.BlockSpec(memory_space=pltpu.VMEM)
    half = 2 * WIDTH
    n_sems = 64
    return pl.pallas_call(
        update_kernel,
        out_shape=(
            jax.ShapeDtypeStruct((64, 256), F32),
            jax.ShapeDtypeStruct((1, 4 * WIDTH), F32),
            jax.ShapeDtypeStruct((1, 4 * WIDTH), F32),
        ),
        in_specs=[vmem] * 5,
        out_specs=(vmem, vmem, vmem),
        scratch_shapes=[
            pltpu.VMEM((NX, NY, 8, 4 * WIDTH), F32),
            pltpu.VMEM((3, 32, half), BF16),
            pltpu.VMEM((3, 32, half), BF16),
            pltpu.VMEM((3, 32, half), BF16),
            pltpu.VMEM((3, 32, half), BF16),
            pltpu.VMEM((NY, 8, half), F32),
            pltpu.VMEM((NX, 8, half), F32),
            pltpu.VMEM((3, 8, half), F32),
            pltpu.VMEM((3, 8, half), F32),
            pltpu.VMEM((NZ, 1, 4 * WIDTH), F32),
            pltpu.VMEM((NZ - 1, 1, 4 * WIDTH), F32),
            pltpu.VMEM((16, 256), F32),
            pltpu.VMEM((2, NC, NZ, NY, NX, 16, 128), BF16),
            pltpu.VMEM((64, 4 * WIDTH), BF16),
            pltpu.SemaphoreType.DMA((n_sems,)),
            pltpu.SemaphoreType.DMA((n_sems,)),
        ],
        compiler_params=pltpu.CompilerParams(
            collective_id=1, has_side_effects=True, vmem_limit_bytes=VMEM_LIMIT
        ),
        name="update",
    )(low, first, second, master, prep)


def projector_orders(projector):
    by_place = projector.reshape(4, NZ, NY, NX, NC)
    rows = by_place.transpose(0, 4, 3, 2, 1).reshape(4, RANK)
    last = by_place.transpose(0, 4, 1, 2, 3).reshape(4, RANK, 1)
    prep = jnp.broadcast_to(last, (4, RANK, 16)).reshape(4, RANK * 16)
    return rows, prep.astype(F32)


def shards(
    inputs, grad_out, norm_gain, master, projector, moment_first, moment_second, doc_lengths
):
    rows, prep = projector_orders(projector)
    weights = gather_weights(master, rows)
    weights = weights.reshape(3, NC, NZ, NY, 2, 2, 16, PART)
    low = local_terms(doc_lengths, inputs, grad_out, norm_gain[None, :], weights)
    low = low.reshape(NC, NX, NY, NZ, 4 * WIDTH)
    new_master, new_first, new_second = update(
        low, moment_first, moment_second, master.reshape(64, 256), prep
    )
    return (new_master.reshape(4, 4 * WIDTH), new_first, new_second)


def solution(mesh):
    return jax.shard_map(
        shards,
        mesh=mesh,
        in_specs=(
            P("dp", None),
            P("dp", None),
            P(),
            P("dp", None),
            P("dp", None),
            P("dp", None),
            P("dp", None),
            P("dp", None),
        ),
        out_specs=(P("dp", None), P("dp", None), P("dp", None)),
        check_vma=False,
    )
```

```python
import jax
import jax.numpy as jnp
import numpy as np
from jax import lax
from jax.experimental import pallas as pl
from jax.experimental.pallas import tpu as pltpu
from jax.sharding import PartitionSpec as P

NZ, NY, NX, NC = 8, 4, 4, 2
SIZE = {"z": NZ, "y": NY, "x": NX}
SHIFTS = {"z": (4, 3, 5, 2, 6, 1, 7), "y": (2, 1, 3), "x": (2, 1, 3)}
GROUPS = 4
UNIT = 256
TOK = 384
WIDTH = 1024
RANK = 256
VMEM_LIMIT = 56 * 1024 * 1024

beta_one = 0.9
beta_two = 0.999
adam_eps = 1e-08
adam_step = 10.0
learn_rate = 0.01
galore_scale = 0.25
norm_eps = 1e-05

F32 = jnp.float32
BF16 = jnp.bfloat16
MESH = pl.DeviceIdType.MESH


def place():
    me = lax.axis_index("dp")
    c = lax.rem(me, NC)
    x = lax.rem(me // NC, NX)
    y = lax.rem(me // (NC * NX), NY)
    z = me // (NC * NX * NY)
    return {"z": z, "y": y, "x": x, "c": c}


def device_at(where, **moved):
    at = dict(where, **moved)
    return ((at["z"] * NY + at["y"]) * NX + at["x"]) * NC + at["c"]


def shifted(where, axis, by):
    n = SIZE[axis]
    return lax.rem(where[axis] + (by + n), n)


class Links:
    def __init__(self, send_sems, recv_sems):
        self.send_sems, self.recv_sems = send_sems, recv_sems
        self.bases = {}
        self.used = 0

    def reserve(self, name, count):
        self.bases[name] = self.used
        self.used += count

    def copy(self, name, i, src, dst, device):
        at = self.bases[name] + i
        return pltpu.make_async_remote_copy(
            src_ref=src,
            dst_ref=dst,
            send_sem=self.send_sems.at[at],
            recv_sem=self.recv_sems.at[at],
            device_id=(device,),
            device_id_type=MESH,
        )


N_SEMS = 160


def start(copies):
    for copy in copies:
        copy.start()


def received(copies):
    for copy in copies:
        copy.wait_recv()


def sent(copies):
    for copy in copies:
        copy.wait_send()


def greet(devices):
    barrier = pltpu.get_barrier_semaphore()
    for device in devices:
        pl.semaphore_signal(barrier, inc=1, device_id=(device,), device_id_type=MESH)
    pl.semaphore_wait(barrier, len(devices))


def dot(a, b, dims=((1,), (0,))):
    return lax.dot_general(a, b, (dims, ((), ())), preferred_element_type=F32)


ROWS = ((1,), (1,))
COLS = ((0,), (0,))


def split(value):
    high = value.astype(BF16)
    return high, (value - high.astype(F32)).astype(BF16)


def adam(low, first, second):
    new_first = beta_one * first + (1.0 - beta_one) * low
    new_second = beta_two * second + (1.0 - beta_two) * low * low
    direction = (
        new_first
        / (1.0 - beta_one**adam_step)
        / (jnp.sqrt(new_second / (1.0 - beta_two**adam_step)) + adam_eps)
    )
    return new_first, new_second, direction


BLOCKS = ((0, 256, 256), (256, 384, 384))


def attend_pair(q, k, v, gh, bias_ref, masks):
    gh_high, gh_rest = split(gh)
    v_twice = jnp.concatenate([v, v], axis=1)
    out_q, out_a, out_k, out_v = [], [], [], []
    for lo, hi, keys in BLOCKS:
        parts = []
        for mask in masks:
            q_m, k_m, v_m = q[lo:hi] * mask, k[:keys] * mask, v[:keys] * mask
            s = dot(q_m, k[:keys], ROWS) * 0.125 + bias_ref[lo:hi, :keys]
            e = jnp.exp(s - jnp.max(s, axis=1, keepdims=True))
            p = e * (1.0 / jnp.sum(e, axis=1, keepdims=True))
            p_high, p_rest = split(p)
            a = dot(p_high, v_m)
            gh_m = gh_high[lo:hi] * mask
            gh_both = jnp.concatenate([gh_m, gh_rest[lo:hi] * mask], axis=1)
            gv = dot(p_high, gh_both, COLS)
            gv = gv[:, :128] + gv[:, 128:] + dot(p_rest, gh_m, COLS)
            gp = dot(gh_both, v_twice[:keys], ROWS)
            gs = p * (gp - jnp.sum(p * gp, axis=1, keepdims=True))
            gs_high, gs_rest = split(gs)
            gq = dot(gs_high, k_m) + dot(gs_rest, k_m)
            gk = dot(gs_high, q_m, COLS) + dot(gs_rest, q_m, COLS)
            parts.append((gq, a, gk, gv))
        gq, a, gk, gv = (one + two for one, two in zip(*parts))
        out_q.append(gq)
        out_a.append(a)
        out_k.append(gk)
        out_v.append(gv)

    def fold(first, second):
        return jnp.concatenate([first + second[:256], second[256:]], axis=0)

    gq = jnp.concatenate(out_q, axis=0)
    a = jnp.concatenate(out_a, axis=0)
    return gq, fold(*out_k), fold(*out_v), a


def main_kernel(
    len_ref, in_ref, gout_ref, gain_ref, master_ref, proj_ref, first_ref, second_ref,
    step_ref, low_out,
    w, quad_w, quad_p, own_p, rows_w, rows_p, order, normed, bias, np_t, gp_t,
    q_s, k_s, v_s, gh_s, low_s, r0, s1, v1, acc, v2, rows, v3, dir_rows, tiles, lhs,
    send_sems, recv_sems
):
    where = place()
    c, x, y, z = where["c"], where["x"], where["y"], where["z"]
    xh, xl = x // 2, lax.rem(x, 2)
    flip = x + 1 - 2 * xl
    sibling = device_at(where, c=1 - c)
    links = Links(send_sems, recv_sems)
    for name, count in (
        ("quad", 6), ("z", 7), ("mid0", 6), ("mid1", 6), ("bulk", 24), ("across", 32),
        ("bulk_p", 3), ("across_p", 4), ("core", 4), ("sum1", 12), ("sum2", 12),
        ("sum3", 7), ("dir_z", 7), ("dir_mid", 6), ("dir_last", 6), ("dir_across", 8),
    ):
        links.reserve(name, count)

    def peer(axis, by):
        return device_at(where, **{axis: shifted(where, axis, by)})

    greet(
        [sibling, device_at(where, x=flip, c=1 - c)]
        + [peer(axis, k) for axis in "xyz" for k in SHIFTS[axis]]
    )

    own_p[...] = proj_ref[...].astype(F32)
    mine = xl * 2 + c
    quad = []
    for i, (dx, dc) in enumerate(((0, 1), (1, 0), (1, 1))):
        to_xl = 1 - xl if dx else xl
        to_c = 1 - c if dc else c
        to = device_at(where, x=xh * 2 + to_xl, c=to_c)
        columns = pl.ds(pl.multiple_of((to_xl * 2 + to_c) * WIDTH, WIDTH), WIDTH)
        quad.append(
            links.copy("quad", 2 * i, master_ref.at[:, columns], quad_w.at[mine], to)
        )
        quad.append(links.copy("quad", 2 * i + 1, own_p, quad_p.at[mine], to))
    start(quad)
    columns = pl.ds(pl.multiple_of(mine * WIDTH, WIDTH), WIDTH)
    quad_w[mine] = master_ref[:, columns]
    quad_p[mine] = own_p[...]

    source = lax.broadcasted_iota(jnp.int32, (RANK, RANK), 0)
    place_to = lax.broadcasted_iota(jnp.int32, (RANK, RANK), 1)
    natural = (
        (place_to & 7) * 32
        + ((place_to >> 3) & 3) * 8
        + ((place_to >> 5) & 3) * 2
        + (place_to >> 7)
    )
    order[...] = (source == natural).astype(F32).astype(BF16)

    received(quad)
    for i in range(4):
        rows_w[i * 4 : i * 4 + 4, :] = quad_w[i]
        rows_p[i * 4 : i * 4 + 4, :] = quad_p[i]
    ordered = dot(rows_p[...].astype(BF16), order[...])
    w[0, 0, c, z, y, xh, xl] = jnp.where(c == 0, ordered[:, :128], ordered[:, 128:]).astype(
        BF16
    )
    w[1, 0, c, z, y, xh, xl] = jnp.zeros((16, 128), BF16)
    for pair in range(8):
        w[pair % 2, 1 + pair // 2, c, z, y, xh, xl] = rows_w[
            :, pair * 128 : (pair + 1) * 128
        ].astype(BF16)

    along_z = []
    for i, k in enumerate(SHIFTS["z"]):
        for_all = w.at[:, :, c, z, y, xh, xl]
        along_z.append(links.copy("z", i, for_all, for_all, peer("z", k)))
    start(along_z)

    values = in_ref[...].astype(F32)
    scale = lax.rsqrt(jnp.mean(values * values, axis=1, keepdims=True) + norm_eps)
    normed[...] = (values * scale * gain_ref[...]).astype(BF16)
    b0 = len_ref[0, 0]
    b1 = b0 + len_ref[0, 1]
    b2 = b1 + len_ref[0, 2]
    b3 = b2 + len_ref[0, 3]

    def segment(position):
        return sum((position >= b).astype(jnp.int32) for b in (b0, b1, b2, b3))

    row = lax.broadcasted_iota(jnp.int32, (TOK, 1), 0)
    col = lax.broadcasted_iota(jnp.int32, (1, TOK), 1)
    seen = (segment(row) == segment(col)) & (row >= col)
    bias[...] = jnp.where(seen, F32(0.0), F32(-1e30))
    received(along_z)

    def middle(name, a_slots, b_slots):
        copies = []
        for i, k in enumerate(SHIFTS["y"]):
            ref = w.at[0, a_slots, c, :, y, xh, xl]
            copies.append(links.copy(name, i, ref, ref, peer("y", k)))
        for i, k in enumerate(SHIFTS["x"]):
            ref = w.at[1, b_slots, c, :, y, xh, xl]
            copies.append(links.copy(name, 3 + i, ref, ref, peer("x", k)))
        return copies

    def along_x(slot, at):
        return w.at[0, slot, c, :, :, at // 2, lax.rem(at, 2)]

    def along_y(slot, at):
        return w.at[1, slot, c, :, at]

    def bulk(g):
        copies = []
        for i, k in enumerate(SHIFTS["x"]):
            ref = along_x(g + 1, x)
            copies.append(links.copy("bulk", g * 6 + i, ref, ref, peer("x", k)))
        for i, k in enumerate(SHIFTS["y"]):
            ref = along_y(g + 1, y)
            copies.append(links.copy("bulk", g * 6 + 3 + i, ref, ref, peer("y", k)))
        return copies

    def bulk_p():
        copies = []
        for i, k in enumerate(SHIFTS["x"]):
            ref = along_x(0, x)
            copies.append(links.copy("bulk_p", i, ref, ref, peer("x", k)))
        return copies

    def across(g):
        refs = [along_x(g + 1, x), along_y(g + 1, y)]
        refs += [along_x(g + 1, shifted(where, "x", -k)) for k in SHIFTS["x"]]
        refs += [along_y(g + 1, shifted(where, "y", -k)) for k in SHIFTS["y"]]
        return [links.copy("across", g * 8 + i, r, r, sibling) for i, r in enumerate(refs)]

    def across_p():
        refs = [along_x(0, x)] + [along_x(0, shifted(where, "x", -k)) for k in SHIFTS["x"]]
        return [links.copy("across_p", i, r, r, sibling) for i, r in enumerate(refs)]

    def open_bulk(g):
        start(bulk(g))
        start(across(g)[:2])

    def forward(g):
        for got, on in zip(bulk(g), across(g)[2:]):
            got.wait_recv()
            on.start()

    early = middle("mid0", pl.ds(0, 2), pl.ds(1, 1))
    late = middle("mid1", pl.ds(2, 3), pl.ds(2, 3))
    start(early)
    start(late)

    spread = lax.broadcasted_iota(jnp.int32, (RANK, 256), 1)
    source = lax.broadcasted_iota(jnp.int32, (RANK, 256), 0)
    diagonal = (spread & 15) == (lax.broadcasted_iota(jnp.int32, (RANK, 256), 0) & 15)
    own_rows = own_p[...].astype(BF16)
    for n in range(16):
        kk = n * 16 + (spread >> 4)
        pick = (source == ((kk & 127) * 2 + (kk >> 7))).astype(F32).astype(BF16)
        line = dot(own_rows, pick)
        for i in range(4):
            lhs[i * 16 : (i + 1) * 16, n * 256 : (n + 1) * 256] = jnp.where(
                diagonal[:16], line[i : i + 1, :], F32(0.0)
            ).astype(BF16)

    received(early)
    open_bulk(0)
    start(bulk_p())
    start(across_p()[:1])
    received(late)
    open_bulk(1)
    forward(0)
    for got, on in zip(bulk_p(), across_p()[1:]):
        got.wait_recv()
        on.start()

    lane = lax.broadcasted_iota(jnp.int32, (1, 128), 1)
    firsts = (lane < 64).astype(F32).astype(BF16)
    masks = (firsts, 1 - firsts)

    def weight(slot, low_x, core):
        halves = [w[a, slot, core, :, :, :, low_x].reshape(WIDTH, 128) for a in range(2)]
        return jnp.concatenate(halves, axis=1)

    def project(g):
        for src, low_x, core, out in (
            (normed, 0, 0, q_s), (normed, 0, 1, k_s), (normed, 1, 0, v_s), (gout_ref, 1, 1, gh_s)
        ):
            res = dot(src[...], weight(g + 1, low_x, core))
            out[0] = res[:, :128].astype(out.dtype)
            out[1] = res[:, 128:].astype(out.dtype)

    def project_rank():
        both = [w[0, 0, core, :, :, :, 0].reshape(WIDTH, 128) for core in range(2)]
        proj = jnp.concatenate(both, axis=1)
        for src, out in ((normed, np_t), (gout_ref, gp_t)):
            high, rest = split(dot(src[...], proj).T)
            out[:, :TOK] = high
            out[:, TOK:] = rest

    def core_copy(g):
        return links.copy("core", g, low_s.at[g, 1 - c], r0.at[g], sibling)

    def sum1(g):
        return [
            links.copy("sum1", g * 3 + i, s1.at[g, i], v1.at[g, i], peer("x", k))
            for i, k in enumerate(SHIFTS["x"])
        ]

    def sum2(g):
        return [
            links.copy(
                "sum2", g * 3 + i, acc.at[g, shifted(where, "y", k)], v2.at[g, i], peer("y", k)
            )
            for i, k in enumerate(SHIFTS["y"])
        ]

    def stage_one(g):
        core_copy(g).wait_recv()
        copies = sum1(g)
        for i, k in enumerate(SHIFTS["x"]):
            to = shifted(where, "x", k)
            value = low_s[g, c, to] + r0[g, to]
            s1[g, i] = value.reshape(32, 4 * UNIT).astype(BF16)
            copies[i].start()
        acc[g] = low_s[g, c, x] + r0[g, x]

    def stage_two(g):
        received(sum1(g))
        total = (v1[g, 0].astype(F32) + v1[g, 1].astype(F32)) + v1[g, 2].astype(F32)
        acc[g] = acc[g] + total.reshape(NY, 8, 4 * UNIT)
        start(sum2(g))

    def stage_three(g):
        received(sum2(g))
        total = acc[g, y] + ((v2[g, 0] + v2[g, 1]) + v2[g, 2])
        for block in range(4):
            columns = pl.ds(pl.multiple_of(block * WIDTH + g * UNIT, UNIT), UNIT)
            for i in range(NZ):
                rows[i, :, columns] = total[i : i + 1, block * UNIT : (block + 1) * UNIT]

    @pl.loop(0, 2 * GROUPS)
    def _(t):
        g, i = t // 2, lax.rem(t, 2)

        @pl.when(i == 0)
        def _():
            received(across(g))
            project(g)

            @pl.when(t == 0)
            def _():
                received(across_p())
                project_rank()

            @pl.when(t > 0)
            def _():
                stage_one(g - 1)

            @pl.when(g < GROUPS - 1)
            def _():
                forward(g + 1)

            @pl.when(g < GROUPS - 2)
            def _():
                open_bulk(g + 2)

        @pl.when((i == 1) & (g > 0))
        def _():
            stage_two(g - 1)

        gq, gk, gv, attended = attend_pair(q_s[i], k_s[i], v_s[i], gh_s[i], bias, masks)
        grads = jnp.concatenate(
            [(gq * 0.125).astype(BF16), (gk * 0.125).astype(BF16), gv.astype(BF16)], axis=1
        )
        low = dot(np_t[...], jnp.concatenate([grads, grads], axis=0))
        attended = attended.astype(BF16)
        outer = dot(gp_t[...], jnp.concatenate([attended, attended], axis=0))
        for block in range(4):
            value = outer if block == 3 else low[:, block * 128 : (block + 1) * 128]
            columns = pl.ds(pl.multiple_of(block * UNIT + i * 128, 128), 128)
            low_s[g, :, :, :, :, columns] = value.reshape(NC, NX, NY, NZ, 128)

        @pl.when(i == 1)
        def _():
            core_copy(g).start()

            @pl.when(g > 0)
            def _():
                stage_three(g - 1)

    stage_one(GROUPS - 1)
    stage_two(GROUPS - 1)
    stage_three(GROUPS - 1)
    third = []
    for i, k in enumerate(SHIFTS["z"]):
        src = rows.at[shifted(where, "z", k)]
        third.append(links.copy("sum3", i, src, v3.at[i], peer("z", k)))
    start(third)
    low = rows[z]
    received(third)
    for i in range(NZ - 1):
        low = low + v3[i]
    low_out[...] = low
    _, _, direction = adam(low, first_ref[...], second_ref[...])
    for a in range(16):
        dir_rows[a : a + 1, :] = direction[:, a * 256 : (a + 1) * 256]
    for p in range(2):
        tiles[p, c, z, y, x] = dir_rows[:, p * 128 : (p + 1) * 128].astype(BF16)

    dir_z = []
    for i, k in enumerate(SHIFTS["z"]):
        own = tiles.at[:, c, z, y, x]
        dir_z.append(links.copy("dir_z", i, own, own, peer("z", k)))
    start(dir_z)
    received(dir_z)

    def lines(p, at):
        return tiles.at[0, c, :, :, at] if p == 0 else tiles.at[1, c, :, at]

    mid, last, over = [], [], []
    for p, axis in ((0, "y"), (1, "x")):
        for i, k in enumerate(SHIFTS[axis]):
            own = tiles.at[p, c, :, y, x]
            mid.append(links.copy("dir_mid", p * 3 + i, own, own, peer(axis, k)))
    start(mid)
    for p, axis in ((0, "x"), (1, "y")):
        received(mid[3 * p : 3 * p + 3])
        own = lines(p, where[axis])
        for i, k in enumerate(SHIFTS[axis]):
            last.append(links.copy("dir_last", p * 3 + i, own, own, peer(axis, k)))
            last[-1].start()
        over.append(links.copy("dir_across", p * 4, own, own, sibling))
        over[-1].start()
    for p, axis in ((0, "x"), (1, "y")):
        for i, k in enumerate(SHIFTS[axis]):
            last[3 * p + i].wait_recv()
            got = lines(p, shifted(where, axis, -k))
            over.append(links.copy("dir_across", p * 4 + 1 + i, got, got, sibling))
            over[-1].start()
    received(over)
    for p in range(2):
        columns = slice(p * 128, (p + 1) * 128)
        step_ref[:, columns] = dot(lhs[...], tiles[p].reshape(RANK * 16, 128))

    sent(quad + along_z + early + late + bulk_p() + across_p())

    @pl.loop(0, GROUPS)
    def _(g):
        sent(bulk(g) + across(g) + [core_copy(g)] + sum1(g) + sum2(g))

    sent(third + dir_z + mid + last + over)


def main(lengths, inputs, grad_out, gain, master, projector, first, second):
    vmem = pl.BlockSpec(memory_space=pltpu.VMEM)
    return pl.pallas_call(
        main_kernel,
        out_shape=(
            jax.ShapeDtypeStruct((64, 256), F32),
            jax.ShapeDtypeStruct((1, 4 * WIDTH), F32),
        ),
        in_specs=[pl.BlockSpec(memory_space=pltpu.SMEM)] + [vmem] * 7,
        out_specs=(vmem, vmem),
        scratch_shapes=[
            pltpu.VMEM((2, 5, NC, NZ, NY, 2, 2, 16, 128), BF16),
            pltpu.VMEM((4, 4, WIDTH), F32),
            pltpu.VMEM((4, 4, RANK), F32),
            pltpu.VMEM((4, RANK), F32),
            pltpu.VMEM((16, WIDTH), F32),
            pltpu.VMEM((16, RANK), F32),
            pltpu.VMEM((RANK, RANK), BF16),
            pltpu.VMEM((TOK, WIDTH), BF16),
            pltpu.VMEM((TOK, TOK), F32),
            pltpu.VMEM((RANK, 2 * TOK), BF16),
            pltpu.VMEM((RANK, 2 * TOK), BF16),
            pltpu.VMEM((2, TOK, 128), BF16),
            pltpu.VMEM((2, TOK, 128), BF16),
            pltpu.VMEM((2, TOK, 128), BF16),
            pltpu.VMEM((2, TOK, 128), F32),
            pltpu.VMEM((GROUPS, NC, NX, NY, NZ, 4 * UNIT), F32),
            pltpu.VMEM((GROUPS, NX, NY, NZ, 4 * UNIT), F32),
            pltpu.VMEM((GROUPS, 3, 32, 4 * UNIT), BF16),
            pltpu.VMEM((GROUPS, 3, 32, 4 * UNIT), BF16),
            pltpu.VMEM((GROUPS, NY, NZ, 4 * UNIT), F32),
            pltpu.VMEM((GROUPS, 3, NZ, 4 * UNIT), F32),
            pltpu.VMEM((NZ, 1, 4 * WIDTH), F32),
            pltpu.VMEM((NZ - 1, 1, 4 * WIDTH), F32),
            pltpu.VMEM((16, 256), F32),
            pltpu.VMEM((2, NC, NZ, NY, NX, 16, 128), BF16),
            pltpu.VMEM((64, 4 * WIDTH), BF16),
            pltpu.SemaphoreType.DMA((N_SEMS,)),
            pltpu.SemaphoreType.DMA((N_SEMS,)),
        ],
        compiler_params=pltpu.CompilerParams(
            collective_id=0, has_side_effects=True, vmem_limit_bytes=VMEM_LIMIT
        ),
        name="galore_step",
    )(lengths, inputs, grad_out, gain, master, projector, first, second)


def finish_kernel(
    step_ref, low_ref, first_ref, second_ref, master_ref, new_master, new_first, new_second
):
    first, second, _ = adam(low_ref[...], first_ref[...], second_ref[...])
    new_first[...] = first
    new_second[...] = second
    for a in range(16):
        columns = slice(a * 256, (a + 1) * 256)
        for i in range(4):
            new_master[i : i + 1, columns] = (
                master_ref[i : i + 1, columns]
                - learn_rate * galore_scale * step_ref[i * 16 + a : i * 16 + a + 1, :]
            )


def finish(step, low, first, second, master):
    vmem = pl.BlockSpec(memory_space=pltpu.VMEM)
    return pl.pallas_call(
        finish_kernel,
        out_shape=(
            jax.ShapeDtypeStruct((4, 4 * WIDTH), F32),
            jax.ShapeDtypeStruct((1, 4 * WIDTH), F32),
            jax.ShapeDtypeStruct((1, 4 * WIDTH), F32),
        ),
        in_specs=[vmem] * 5,
        out_specs=(vmem, vmem, vmem),
        name="outputs",
    )(step, low, first, second, master)


def shards(
    inputs, grad_out, norm_gain, master, projector, moment_first, moment_second, doc_lengths
):
    step, low = main(
        doc_lengths, inputs, grad_out, norm_gain[None, :], master, projector,
        moment_first, moment_second,
    )
    return finish(step, low, moment_first, moment_second, master)


def solution(mesh):
    return jax.shard_map(
        shards,
        mesh=mesh,
        in_specs=(
            P("dp", None),
            P("dp", None),
            P(),
            P("dp", None),
            P("dp", None),
            P("dp", None),
            P("dp", None),
            P("dp", None),
        ),
        out_specs=(P("dp", None), P("dp", None), P("dp", None)),
        check_vma=False,
    )
```

```python
import jax
import jax.numpy as jnp
import numpy as np
from jax import lax
from jax.experimental import pallas as pl
from jax.experimental.pallas import tpu as pltpu
from jax.sharding import PartitionSpec as P

NZ, NY, NX, NC = 8, 4, 4, 2
SIZE = {"z": NZ, "y": NY, "x": NX}
SHIFTS = {"z": (4, 3, 5, 2, 6, 1, 7), "y": (2, 1, 3), "x": (2, 1, 3)}
GROUPS = 4
UNIT = 256
TOK = 384
WIDTH = 1024
RANK = 256
VMEM_LIMIT = 56 * 1024 * 1024

beta_one = 0.9
beta_two = 0.999
adam_eps = 1e-08
adam_step = 10.0
learn_rate = 0.01
galore_scale = 0.25
norm_eps = 1e-05

F32 = jnp.float32
BF16 = jnp.bfloat16
MESH = pl.DeviceIdType.MESH


def place():
    me = lax.axis_index("dp")
    c = lax.rem(me, NC)
    x = lax.rem(me // NC, NX)
    y = lax.rem(me // (NC * NX), NY)
    z = me // (NC * NX * NY)
    return {"z": z, "y": y, "x": x, "c": c}


def device_at(where, **moved):
    at = dict(where, **moved)
    return ((at["z"] * NY + at["y"]) * NX + at["x"]) * NC + at["c"]


def shifted(where, axis, by):
    n = SIZE[axis]
    return lax.rem(where[axis] + (by + n), n)


class Links:
    def __init__(self, send_sems, recv_sems):
        self.send_sems, self.recv_sems = send_sems, recv_sems
        self.bases = {}
        self.used = 0

    def reserve(self, name, count):
        self.bases[name] = self.used
        self.used += count

    def copy(self, name, i, src, dst, device):
        at = self.bases[name] + i
        return pltpu.make_async_remote_copy(
            src_ref=src,
            dst_ref=dst,
            send_sem=self.send_sems.at[at],
            recv_sem=self.recv_sems.at[at],
            device_id=(device,),
            device_id_type=MESH,
        )


N_SEMS = 208


def start(copies):
    for copy in copies:
        copy.start()


def received(copies):
    for copy in copies:
        copy.wait_recv()


def sent(copies):
    for copy in copies:
        copy.wait_send()


def greet(devices):
    barrier = pltpu.get_barrier_semaphore()
    for device in devices:
        pl.semaphore_signal(barrier, inc=1, device_id=(device,), device_id_type=MESH)
    pl.semaphore_wait(barrier, len(devices))


def dot(a, b, dims=((1,), (0,))):
    return lax.dot_general(a, b, (dims, ((), ())), preferred_element_type=F32)


ROWS = ((1,), (1,))
COLS = ((0,), (0,))


def split(value):
    high = value.astype(BF16)
    return high, (value - high.astype(F32)).astype(BF16)


def adam(low, first, second):
    new_first = beta_one * first + (1.0 - beta_one) * low
    new_second = beta_two * second + (1.0 - beta_two) * low * low
    direction = (
        new_first
        / (1.0 - beta_one**adam_step)
        / (jnp.sqrt(new_second / (1.0 - beta_two**adam_step)) + adam_eps)
    )
    return new_first, new_second, direction


BLOCKS = ((0, 256, 256), (256, 384, 384))


def attend_pair(q, k, v, gh, bias_ref, masks):
    gh_high, gh_rest = split(gh)
    v_twice = jnp.concatenate([v, v], axis=1)
    out_q, out_a, out_k, out_v = [], [], [], []
    for lo, hi, keys in BLOCKS:
        parts = []
        for mask in masks:
            q_m, k_m, v_m = q[lo:hi] * mask, k[:keys] * mask, v[:keys] * mask
            s = dot(q_m, k[:keys], ROWS) * 0.125 + bias_ref[lo:hi, :keys]
            e = jnp.exp(s - jnp.max(s, axis=1, keepdims=True))
            p = e * (1.0 / jnp.sum(e, axis=1, keepdims=True))
            p_high, p_rest = split(p)
            a = dot(p_high, v_m)
            gh_m = gh_high[lo:hi] * mask
            gh_both = jnp.concatenate([gh_m, gh_rest[lo:hi] * mask], axis=1)
            gv = dot(p_high, gh_both, COLS)
            gv = gv[:, :128] + gv[:, 128:] + dot(p_rest, gh_m, COLS)
            gp = dot(gh_both, v_twice[:keys], ROWS)
            gs = p * (gp - jnp.sum(p * gp, axis=1, keepdims=True))
            gs_high, gs_rest = split(gs)
            gq = dot(gs_high, k_m) + dot(gs_rest, k_m)
            gk = dot(gs_high, q_m, COLS) + dot(gs_rest, q_m, COLS)
            parts.append((gq, a, gk, gv))
        gq, a, gk, gv = (one + two for one, two in zip(*parts))
        out_q.append(gq)
        out_a.append(a)
        out_k.append(gk)
        out_v.append(gv)

    def fold(first, second):
        return jnp.concatenate([first + second[:256], second[256:]], axis=0)

    gq = jnp.concatenate(out_q, axis=0)
    a = jnp.concatenate(out_a, axis=0)
    return gq, fold(*out_k), fold(*out_v), a


def main_kernel(
    len_ref, in_ref, gout_ref, gain_ref, master_ref, proj_ref, first_ref, second_ref,
    step_ref, low_out,
    w, quad_w, quad_p, own_p, rows_w, rows_p, order, normed, bias, np_t, gp_t,
    q_s, k_s, v_s, gh_s, low_s, r0, s1, v1, acc, v2, rows, v3, dir_rows, tiles, lhs,
    send_sems, recv_sems
):
    where = place()
    c, x, y, z = where["c"], where["x"], where["y"], where["z"]
    xh, xl = x // 2, lax.rem(x, 2)
    flip = x + 1 - 2 * xl
    sibling = device_at(where, c=1 - c)
    links = Links(send_sems, recv_sems)
    for name, count in (
        ("quad", 6), ("z0", 7), ("zp", 7), ("z1", 7), ("mid0", 6), ("midp", 3), ("mid1", 6),
        ("bulk", 24), ("across", 32), ("bulk_p", 3), ("across_p", 4), ("core", 4),
        ("sum1", 12), ("sum2", 12), ("sum3", 14), ("dir_z", 14), ("dir_mid", 12),
        ("dir_last", 12), ("dir_across", 16),
    ):
        links.reserve(name, count)

    def peer(axis, by):
        return device_at(where, **{axis: shifted(where, axis, by)})

    greet(
        [sibling, device_at(where, x=flip, c=1 - c)]
        + [peer(axis, k) for axis in "xyz" for k in SHIFTS[axis]]
    )

    own_p[...] = proj_ref[...].astype(F32)
    mine = xl * 2 + c
    quad = []
    for i, (dx, dc) in enumerate(((0, 1), (1, 0), (1, 1))):
        to_xl = 1 - xl if dx else xl
        to_c = 1 - c if dc else c
        to = device_at(where, x=xh * 2 + to_xl, c=to_c)
        columns = pl.ds(pl.multiple_of((to_xl * 2 + to_c) * WIDTH, WIDTH), WIDTH)
        quad.append(
            links.copy("quad", 2 * i, master_ref.at[:, columns], quad_w.at[mine], to)
        )
        quad.append(links.copy("quad", 2 * i + 1, own_p, quad_p.at[mine], to))
    start(quad)
    columns = pl.ds(pl.multiple_of(mine * WIDTH, WIDTH), WIDTH)
    quad_w[mine] = master_ref[:, columns]
    quad_p[mine] = own_p[...]

    source = lax.broadcasted_iota(jnp.int32, (RANK, RANK), 0)
    place_to = lax.broadcasted_iota(jnp.int32, (RANK, RANK), 1)
    natural = (
        (place_to & 7) * 32
        + ((place_to >> 3) & 3) * 8
        + ((place_to >> 5) & 3) * 2
        + (place_to >> 7)
    )
    order[...] = (source == natural).astype(F32).astype(BF16)

    received(quad)
    for i in range(4):
        rows_w[i * 4 : i * 4 + 4, :] = quad_w[i]
        rows_p[i * 4 : i * 4 + 4, :] = quad_p[i]
    ordered = dot(rows_p[...].astype(BF16), order[...])
    w[0, 4, c, z, y, xh, xl] = jnp.where(c == 0, ordered[:, :128], ordered[:, 128:]).astype(
        BF16
    )
    for pair in range(8):
        w[pair % 2, pair // 2, c, z, y, xh, xl] = rows_w[
            :, pair * 128 : (pair + 1) * 128
        ].astype(BF16)

    def first_step(name, slots, kinds):
        copies = []
        for i, k in enumerate(SHIFTS["z"]):
            ref = w.at[kinds, slots, c, z, y, xh, xl]
            copies.append(links.copy(name, i, ref, ref, peer("z", k)))
        return copies

    z_first = first_step("z0", pl.ds(0, 1), pl.ds(0, 2))
    z_rank = first_step("zp", pl.ds(4, 1), pl.ds(0, 1))
    z_rest = first_step("z1", pl.ds(1, 3), pl.ds(0, 2))
    start(z_first + z_rank + z_rest)

    values = in_ref[...].astype(F32)
    scale = lax.rsqrt(jnp.mean(values * values, axis=1, keepdims=True) + norm_eps)
    normed[...] = (values * scale * gain_ref[...]).astype(BF16)
    b0 = len_ref[0, 0]
    b1 = b0 + len_ref[0, 1]
    b2 = b1 + len_ref[0, 2]
    b3 = b2 + len_ref[0, 3]

    def segment(position):
        return sum((position >= b).astype(jnp.int32) for b in (b0, b1, b2, b3))

    row = lax.broadcasted_iota(jnp.int32, (TOK, 1), 0)
    col = lax.broadcasted_iota(jnp.int32, (1, TOK), 1)
    seen = (segment(row) == segment(col)) & (row >= col)
    bias[...] = jnp.where(seen, F32(0.0), F32(-1e30))
    def middle(name, slots, kinds):
        copies = []
        for kind, axis in kinds:
            for k in SHIFTS[axis]:
                ref = w.at[kind, slots, c, :, y, xh, xl]
                copies.append(links.copy(name, len(copies), ref, ref, peer(axis, k)))
        return copies

    def along_x(slot, at):
        return w.at[0, slot, c, :, :, at // 2, lax.rem(at, 2)]

    def along_y(slot, at):
        return w.at[1, slot, c, :, at]

    def bulk(g):
        copies = []
        for i, k in enumerate(SHIFTS["x"]):
            ref = along_x(g, x)
            copies.append(links.copy("bulk", g * 6 + i, ref, ref, peer("x", k)))
        for i, k in enumerate(SHIFTS["y"]):
            ref = along_y(g, y)
            copies.append(links.copy("bulk", g * 6 + 3 + i, ref, ref, peer("y", k)))
        return copies

    def bulk_p():
        copies = []
        for i, k in enumerate(SHIFTS["x"]):
            ref = along_x(4, x)
            copies.append(links.copy("bulk_p", i, ref, ref, peer("x", k)))
        return copies

    def across(g):
        refs = [along_x(g, x), along_y(g, y)]
        refs += [along_x(g, shifted(where, "x", -k)) for k in SHIFTS["x"]]
        refs += [along_y(g, shifted(where, "y", -k)) for k in SHIFTS["y"]]
        return [links.copy("across", g * 8 + i, r, r, sibling) for i, r in enumerate(refs)]

    def across_p():
        refs = [along_x(4, x)] + [along_x(4, shifted(where, "x", -k)) for k in SHIFTS["x"]]
        return [links.copy("across_p", i, r, r, sibling) for i, r in enumerate(refs)]

    def open_bulk(g):
        start(bulk(g))
        start(across(g)[:2])

    def forward(g):
        for got, on in zip(bulk(g), across(g)[2:]):
            got.wait_recv()
            on.start()

    both = ((0, "y"), (1, "x"))
    mid_first = middle("mid0", pl.ds(0, 1), both)
    mid_rank = middle("midp", pl.ds(4, 1), both[:1])
    mid_rest = middle("mid1", pl.ds(1, 3), both)
    received(z_first)
    start(mid_first)
    received(z_rank)
    start(mid_rank)
    received(mid_first)
    open_bulk(0)
    received(mid_rank)
    start(bulk_p())
    start(across_p()[:1])
    received(z_rest)
    start(mid_rest)

    spread = lax.broadcasted_iota(jnp.int32, (RANK, 256), 1)
    source = lax.broadcasted_iota(jnp.int32, (RANK, 256), 0)
    diagonal = (spread & 15) == (lax.broadcasted_iota(jnp.int32, (RANK, 256), 0) & 15)
    own_rows = own_p[...].astype(BF16)
    for n in range(16):
        kk = n * 16 + (spread >> 4)
        pick = (source == ((kk & 127) * 2 + (kk >> 7))).astype(F32).astype(BF16)
        line = dot(own_rows, pick)
        for i in range(4):
            lhs[i * 16 : (i + 1) * 16, n * 256 : (n + 1) * 256] = jnp.where(
                diagonal[:16], line[i : i + 1, :], F32(0.0)
            ).astype(BF16)

    forward(0)
    received(mid_rest)
    open_bulk(1)
    open_bulk(2)
    open_bulk(3)

    lane = lax.broadcasted_iota(jnp.int32, (1, 128), 1)
    firsts = (lane < 64).astype(F32).astype(BF16)
    masks = (firsts, 1 - firsts)

    def weight(slot, low_x, core):
        halves = [w[a, slot, core, :, :, :, low_x].reshape(WIDTH, 128) for a in range(2)]
        return jnp.concatenate(halves, axis=1)

    def project(g):
        for src, low_x, core, out in (
            (normed, 0, 0, q_s), (normed, 0, 1, k_s), (normed, 1, 0, v_s), (gout_ref, 1, 1, gh_s)
        ):
            res = dot(src[...], weight(g, low_x, core))
            out[0] = res[:, :128].astype(out.dtype)
            out[1] = res[:, 128:].astype(out.dtype)

    def project_rank():
        both = [w[0, 4, core, :, :, :, 0].reshape(WIDTH, 128) for core in range(2)]
        proj = jnp.concatenate(both, axis=1)
        for src, out in ((normed, np_t), (gout_ref, gp_t)):
            high, rest = split(dot(src[...], proj).T)
            out[:, :TOK] = high
            out[:, TOK:] = rest

    def core_copy(g):
        return links.copy("core", g, low_s.at[g, 1 - c], r0.at[g], sibling)

    def sum1(g):
        return [
            links.copy("sum1", g * 3 + i, s1.at[g, i], v1.at[g, i], peer("x", k))
            for i, k in enumerate(SHIFTS["x"])
        ]

    def sum2(g):
        return [
            links.copy(
                "sum2", g * 3 + i, acc.at[g, shifted(where, "y", k)], v2.at[g, i], peer("y", k)
            )
            for i, k in enumerate(SHIFTS["y"])
        ]

    def stage_one(g):
        core_copy(g).wait_recv()
        copies = sum1(g)
        for i, k in enumerate(SHIFTS["x"]):
            to = shifted(where, "x", k)
            value = low_s[g, c, to] + r0[g, to]
            s1[g, i] = value.reshape(32, 4 * UNIT).astype(BF16)
            copies[i].start()
        acc[g] = low_s[g, c, x] + r0[g, x]

    def stage_two(g):
        received(sum1(g))
        total = (v1[g, 0].astype(F32) + v1[g, 1].astype(F32)) + v1[g, 2].astype(F32)
        acc[g] = acc[g] + total.reshape(NY, 8, 4 * UNIT)
        start(sum2(g))

    def stage_three(g):
        received(sum2(g))
        total = acc[g, y] + ((v2[g, 0] + v2[g, 1]) + v2[g, 2])
        h = g // 2
        for block in range(4):
            columns = pl.ds(
                pl.multiple_of(block * 2 * UNIT + lax.rem(g, 2) * UNIT, UNIT), UNIT
            )
            for i in range(NZ):
                rows[h, i, :, columns] = total[i : i + 1, block * UNIT : (block + 1) * UNIT]

    def sum3(h):
        return [
            links.copy(
                "sum3", h * 7 + i, rows.at[h, shifted(where, "z", k)], v3.at[h, i], peer("z", k)
            )
            for i, k in enumerate(SHIFTS["z"])
        ]

    def dir_z(h):
        own = tiles.at[h, c, z, y, x]
        return [
            links.copy("dir_z", h * 7 + i, own, own, peer("z", k))
            for i, k in enumerate(SHIFTS["z"])
        ]

    def summed(h):
        received(sum3(h))
        low = rows[h, z]
        for i in range(NZ - 1):
            low = low + v3[h, i]
        for block in range(4):
            columns = slice(block * WIDTH + h * 512, block * WIDTH + h * 512 + 512)
            part = low[:, block * 512 : (block + 1) * 512]
            low_out[:, columns] = part
            _, _, direction = adam(part, first_ref[:, columns], second_ref[:, columns])
            for a in range(4):
                dir_rows[block * 4 + a : block * 4 + a + 1, :] = direction[
                    :, a * 128 : (a + 1) * 128
                ]
        tiles[h, c, z, y, x] = dir_rows[...].astype(BF16)
        start(dir_z(h))

    paths = ((pl.ds(0, 4), "y", "x"), (pl.ds(4, 4), "x", "y"))

    def dir_mid(h):
        copies = []
        for depth, axis, _ in paths:
            own = tiles.at[h, c, depth, y, x]
            for k in SHIFTS[axis]:
                copies.append(
                    links.copy("dir_mid", h * 6 + len(copies), own, own, peer(axis, k))
                )
        return copies

    def lines(h, p, at):
        depth = paths[p][0]
        return tiles.at[h, c, depth, :, at] if p == 0 else tiles.at[h, c, depth, at]

    def dir_last(h):
        copies = []
        for p, (_, _, axis) in enumerate(paths):
            own = lines(h, p, where[axis])
            for k in SHIFTS[axis]:
                copies.append(
                    links.copy("dir_last", h * 6 + len(copies), own, own, peer(axis, k))
                )
        return copies

    def dir_across(h):
        refs = [lines(h, p, where[paths[p][2]]) for p in range(2)]
        for p, (_, _, axis) in enumerate(paths):
            refs += [lines(h, p, shifted(where, axis, -k)) for k in SHIFTS[axis]]
        return [
            links.copy("dir_across", h * 8 + i, r, r, sibling) for i, r in enumerate(refs)
        ]

    def hand_on(h):
        for got, on in zip(dir_last(h), dir_across(h)[2:]):
            got.wait_recv()
            on.start()

    def step_of(h):
        received(dir_across(h))
        columns = slice(h * 128, (h + 1) * 128)
        step_ref[:, columns] = dot(lhs[...], tiles[h].reshape(RANK * 16, 128))

    @pl.loop(0, 2 * GROUPS)
    def _(t):
        g, i = t // 2, lax.rem(t, 2)

        @pl.when(i == 0)
        def _():
            received(across(g))
            project(g)

            @pl.when(t > 0)
            def _():
                stage_one(g - 1)

        @pl.when(i == 1)
        def _():
            @pl.when(g > 0)
            def _():
                stage_two(g - 1)

            @pl.when(g < GROUPS - 1)
            def _():
                forward(g + 1)

        gq, gk, gv, attended = attend_pair(q_s[i], k_s[i], v_s[i], gh_s[i], bias, masks)

        @pl.when(t == 0)
        def _():
            for got, on in zip(bulk_p(), across_p()[1:]):
                got.wait_recv()
                on.start()
            received(across_p())
            project_rank()

        grads = jnp.concatenate(
            [(gq * 0.125).astype(BF16), (gk * 0.125).astype(BF16), gv.astype(BF16)], axis=1
        )
        low = dot(np_t[...], jnp.concatenate([grads, grads], axis=0))
        attended = attended.astype(BF16)
        outer = dot(gp_t[...], jnp.concatenate([attended, attended], axis=0))
        for block in range(4):
            value = outer if block == 3 else low[:, block * 128 : (block + 1) * 128]
            columns = pl.ds(pl.multiple_of(block * UNIT + i * 128, 128), 128)
            low_s[g, :, :, :, :, columns] = value.reshape(NC, NX, NY, NZ, 128)

        @pl.when(i == 1)
        def _():
            core_copy(g).start()

            @pl.when(g > 0)
            def _():
                stage_three(g - 1)

            @pl.when(g == 2)
            def _():
                start(sum3(0))

        @pl.when(t == 6)
        def _():
            summed(0)

    received(dir_z(0))
    start(dir_mid(0))
    stage_one(GROUPS - 1)
    stage_two(GROUPS - 1)
    received(dir_mid(0))
    start(dir_last(0))
    start(dir_across(0)[:2])
    stage_three(GROUPS - 1)
    start(sum3(1))
    hand_on(0)
    summed(1)
    step_of(0)
    received(dir_z(1))
    start(dir_mid(1))
    received(dir_mid(1))
    start(dir_last(1))
    start(dir_across(1)[:2])
    hand_on(1)
    step_of(1)

    sent(quad + z_first + z_rank + z_rest + mid_first + mid_rank + mid_rest)
    sent(bulk_p() + across_p())

    @pl.loop(0, GROUPS)
    def _(g):
        sent(bulk(g) + across(g) + [core_copy(g)] + sum1(g) + sum2(g))

    for h in range(2):
        sent(sum3(h) + dir_z(h) + dir_mid(h) + dir_last(h) + dir_across(h))


def main(lengths, inputs, grad_out, gain, master, projector, first, second):
    vmem = pl.BlockSpec(memory_space=pltpu.VMEM)
    return pl.pallas_call(
        main_kernel,
        out_shape=(
            jax.ShapeDtypeStruct((64, 256), F32),
            jax.ShapeDtypeStruct((1, 4 * WIDTH), F32),
        ),
        in_specs=[pl.BlockSpec(memory_space=pltpu.SMEM)] + [vmem] * 7,
        out_specs=(vmem, vmem),
        scratch_shapes=[
            pltpu.VMEM((2, 5, NC, NZ, NY, 2, 2, 16, 128), BF16),
            pltpu.VMEM((4, 4, WIDTH), F32),
            pltpu.VMEM((4, 4, RANK), F32),
            pltpu.VMEM((4, RANK), F32),
            pltpu.VMEM((16, WIDTH), F32),
            pltpu.VMEM((16, RANK), F32),
            pltpu.VMEM((RANK, RANK), BF16),
            pltpu.VMEM((TOK, WIDTH), BF16),
            pltpu.VMEM((TOK, TOK), F32),
            pltpu.VMEM((RANK, 2 * TOK), BF16),
            pltpu.VMEM((RANK, 2 * TOK), BF16),
            pltpu.VMEM((2, TOK, 128), BF16),
            pltpu.VMEM((2, TOK, 128), BF16),
            pltpu.VMEM((2, TOK, 128), BF16),
            pltpu.VMEM((2, TOK, 128), F32),
            pltpu.VMEM((GROUPS, NC, NX, NY, NZ, 4 * UNIT), F32),
            pltpu.VMEM((GROUPS, NX, NY, NZ, 4 * UNIT), F32),
            pltpu.VMEM((GROUPS, 3, 32, 4 * UNIT), BF16),
            pltpu.VMEM((GROUPS, 3, 32, 4 * UNIT), BF16),
            pltpu.VMEM((GROUPS, NY, NZ, 4 * UNIT), F32),
            pltpu.VMEM((GROUPS, 3, NZ, 4 * UNIT), F32),
            pltpu.VMEM((2, NZ, 1, 2 * WIDTH), F32),
            pltpu.VMEM((2, NZ - 1, 1, 2 * WIDTH), F32),
            pltpu.VMEM((16, 128), F32),
            pltpu.VMEM((2, NC, NZ, NY, NX, 16, 128), BF16),
            pltpu.VMEM((64, 4 * WIDTH), BF16),
            pltpu.SemaphoreType.DMA((N_SEMS,)),
            pltpu.SemaphoreType.DMA((N_SEMS,)),
        ],
        compiler_params=pltpu.CompilerParams(
            collective_id=0, has_side_effects=True, vmem_limit_bytes=VMEM_LIMIT
        ),
        name="galore_step",
    )(lengths, inputs, grad_out, gain, master, projector, first, second)


def finish_kernel(
    step_ref, low_ref, first_ref, second_ref, master_ref, new_master, new_first, new_second
):
    first, second, _ = adam(low_ref[...], first_ref[...], second_ref[...])
    new_first[...] = first
    new_second[...] = second
    for a in range(16):
        for h in range(2):
            at = (a // 4) * WIDTH + h * 512 + (a % 4) * 128
            columns = slice(at, at + 128)
            for i in range(4):
                row = i * 16 + a
                new_master[i : i + 1, columns] = (
                    master_ref[i : i + 1, columns]
                    - learn_rate * galore_scale * step_ref[row : row + 1, h * 128 : h * 128 + 128]
                )


def finish(step, low, first, second, master):
    vmem = pl.BlockSpec(memory_space=pltpu.VMEM)
    return pl.pallas_call(
        finish_kernel,
        out_shape=(
            jax.ShapeDtypeStruct((4, 4 * WIDTH), F32),
            jax.ShapeDtypeStruct((1, 4 * WIDTH), F32),
            jax.ShapeDtypeStruct((1, 4 * WIDTH), F32),
        ),
        in_specs=[vmem] * 5,
        out_specs=(vmem, vmem, vmem),
        name="outputs",
    )(step, low, first, second, master)


def shards(
    inputs, grad_out, norm_gain, master, projector, moment_first, moment_second, doc_lengths
):
    step, low = main(
        doc_lengths, inputs, grad_out, norm_gain[None, :], master, projector,
        moment_first, moment_second,
    )
    return finish(step, low, moment_first, moment_second, master)


def solution(mesh):
    return jax.shard_map(
        shards,
        mesh=mesh,
        in_specs=(
            P("dp", None),
            P("dp", None),
            P(),
            P("dp", None),
            P("dp", None),
            P("dp", None),
            P("dp", None),
            P("dp", None),
        ),
        out_specs=(P("dp", None), P("dp", None), P("dp", None)),
        check_vma=False,
    )
```

```python
import jax
import jax.numpy as jnp
import numpy as np
from jax import lax
from jax.experimental import pallas as pl
from jax.experimental.pallas import tpu as pltpu
from jax.sharding import PartitionSpec as P

NZ, NY, NX, NC = 8, 4, 4, 2
SIZE = {"z": NZ, "y": NY, "x": NX}
SHIFTS = {"z": (4, 3, 5, 2, 6, 1, 7), "y": (2, 1, 3), "x": (2, 1, 3)}
GROUPS = 4
UNIT = 256
TOK = 384
WIDTH = 1024
RANK = 256
VMEM_LIMIT = 56 * 1024 * 1024

beta_one = 0.9
beta_two = 0.999
adam_eps = 1e-08
adam_step = 10.0
learn_rate = 0.01
galore_scale = 0.25
norm_eps = 1e-05

F32 = jnp.float32
BF16 = jnp.bfloat16
MESH = pl.DeviceIdType.MESH


def place():
    me = lax.axis_index("dp")
    c = lax.rem(me, NC)
    x = lax.rem(me // NC, NX)
    y = lax.rem(me // (NC * NX), NY)
    z = me // (NC * NX * NY)
    return {"z": z, "y": y, "x": x, "c": c}


def device_at(where, **moved):
    at = dict(where, **moved)
    return ((at["z"] * NY + at["y"]) * NX + at["x"]) * NC + at["c"]


def shifted(where, axis, by):
    n = SIZE[axis]
    return lax.rem(where[axis] + (by + n), n)


class Links:
    def __init__(self, send_sems, recv_sems):
        self.send_sems, self.recv_sems = send_sems, recv_sems
        self.bases = {}
        self.used = 0

    def reserve(self, name, count):
        self.bases[name] = self.used
        self.used += count

    def copy(self, name, i, src, dst, device):
        at = self.bases[name] + i
        return pltpu.make_async_remote_copy(
            src_ref=src,
            dst_ref=dst,
            send_sem=self.send_sems.at[at],
            recv_sem=self.recv_sems.at[at],
            device_id=(device,),
            device_id_type=MESH,
        )


N_SEMS = 232


def start(copies):
    for copy in copies:
        copy.start()


def received(copies):
    for copy in copies:
        copy.wait_recv()


def sent(copies):
    for copy in copies:
        copy.wait_send()


def greet(devices):
    barrier = pltpu.get_barrier_semaphore()
    for device in devices:
        pl.semaphore_signal(barrier, inc=1, device_id=(device,), device_id_type=MESH)
    pl.semaphore_wait(barrier, len(devices))


def dot(a, b, dims=((1,), (0,))):
    return lax.dot_general(a, b, (dims, ((), ())), preferred_element_type=F32)


ROWS = ((1,), (1,))
COLS = ((0,), (0,))


def split(value):
    high = value.astype(BF16)
    return high, (value - high.astype(F32)).astype(BF16)


def adam(low, first, second):
    new_first = beta_one * first + (1.0 - beta_one) * low
    new_second = beta_two * second + (1.0 - beta_two) * low * low
    direction = (
        new_first
        / (1.0 - beta_one**adam_step)
        / (jnp.sqrt(new_second / (1.0 - beta_two**adam_step)) + adam_eps)
    )
    return new_first, new_second, direction


def attend_pair(q, k, v, gh, bias_ref, masks, between):
    probs, highs = [], []
    left_v, right_v = [], []
    for mask in masks:
        s = dot(k, q * mask, ROWS) * 0.125 + bias_ref[...]
        e = jnp.exp(s - jnp.max(s, axis=0, keepdims=True))
        p = e * (1.0 / jnp.sum(e, axis=0, keepdims=True))
        probs.append(p)
    between()
    gh_high, gh_rest = split(gh)
    v_twice = jnp.concatenate([v, v], axis=1)
    grads, right_k, left_q = [], [], []
    for p, mask in zip(probs, masks):
        p_high, p_rest = split(p)
        gh_m, gh_r = gh_high * mask, gh_rest * mask
        gp = dot(v_twice, jnp.concatenate([gh_m, gh_r], axis=1), ROWS)
        gs = p * (gp - jnp.sum(p * gp, axis=0, keepdims=True))
        highs.append(p_high)
        left_v += [p_high, p_rest, p_high]
        right_v += [gh_m, gh_m, gh_r]
        grads += list(split(gs))
        right_k += [q * mask] * 2
        left_q += [k * mask] * 2
    gv = dot(jnp.concatenate(left_v, axis=1), jnp.concatenate(right_v, axis=0))
    gk = dot(jnp.concatenate(grads, axis=1), jnp.concatenate(right_k, axis=0))
    gq_t = dot(jnp.concatenate(left_q, axis=0), jnp.concatenate(grads, axis=0), COLS)
    by_head = jnp.concatenate([v * mask for mask in masks], axis=0)
    a_t = dot(by_head, jnp.concatenate(highs, axis=0), COLS)
    return gq_t, gk, gv, a_t


def main_kernel(
    len_ref, in_ref, gout_ref, gain_ref, master_ref, proj_ref, first_ref, second_ref,
    step_ref, low_out,
    w, quad_w, quad_p, own_p, rows_w, rows_p, order, normed, bias, np_t, gp_t,
    q_s, k_s, v_s, gh_s, low_s, r0, s1, v1, acc, v2, rows, v3, dir_rows, tiles, lhs,
    send_sems, recv_sems
):
    where = place()
    c, x, y, z = where["c"], where["x"], where["y"], where["z"]
    xh, xl = x // 2, lax.rem(x, 2)
    flip = x + 1 - 2 * xl
    sibling = device_at(where, c=1 - c)
    links = Links(send_sems, recv_sems)
    for name, count in (
        ("quad", 6), ("z0", 7), ("zp", 7), ("z1", 7), ("mid0", 6), ("midp", 6), ("mid1", 6), ("mid2", 6),
        ("mid3", 6),
        ("bulk", 24), ("across", 32), ("bulk_p", 6), ("across_p", 8), ("core", 4),
        ("sum1", 12), ("sum2", 12), ("sum3", 14), ("dir_z", 14), ("dir_mid", 12),
        ("dir_last", 12), ("dir_across", 16),
    ):
        links.reserve(name, count)

    def peer(axis, by):
        return device_at(where, **{axis: shifted(where, axis, by)})

    greet(
        [sibling, device_at(where, x=flip, c=1 - c)]
        + [peer(axis, k) for axis in "xyz" for k in SHIFTS[axis]]
    )

    own_p[...] = proj_ref[...].astype(F32)
    mine = xl * 2 + c
    quad = []
    for i, (dx, dc) in enumerate(((0, 1), (1, 0), (1, 1))):
        to_xl = 1 - xl if dx else xl
        to_c = 1 - c if dc else c
        to = device_at(where, x=xh * 2 + to_xl, c=to_c)
        columns = pl.ds(pl.multiple_of((to_xl * 2 + to_c) * WIDTH, WIDTH), WIDTH)
        quad.append(
            links.copy("quad", 2 * i, master_ref.at[:, columns], quad_w.at[mine], to)
        )
        quad.append(links.copy("quad", 2 * i + 1, own_p, quad_p.at[mine], to))
    start(quad)
    columns = pl.ds(pl.multiple_of(mine * WIDTH, WIDTH), WIDTH)
    quad_w[mine] = master_ref[:, columns]
    quad_p[mine] = own_p[...]

    source = lax.broadcasted_iota(jnp.int32, (RANK, RANK), 0)
    place_to = lax.broadcasted_iota(jnp.int32, (RANK, RANK), 1)
    natural = (
        (place_to & 7) * 32
        + ((place_to >> 3) & 3) * 8
        + ((place_to >> 5) & 3) * 2
        + (place_to >> 7)
    )
    order[...] = (source == natural).astype(F32).astype(BF16)

    received(quad)
    for i in range(4):
        rows_w[i * 4 : i * 4 + 4, :] = quad_w[i]
        rows_p[i * 4 : i * 4 + 4, :] = quad_p[i]
    ordered = dot(rows_p[...].astype(BF16), order[...])
    w[0, 4, c, z, y, xh, xl] = jnp.where(c == 0, ordered[:, :128], ordered[:, 128:]).astype(
        BF16
    )
    for pair in range(8):
        w[pair % 2, pair // 2, c, z, y, xh, xl] = rows_w[
            :, pair * 128 : (pair + 1) * 128
        ].astype(BF16)

    def first_step(name, slots, kinds):
        copies = []
        for i, k in enumerate(SHIFTS["z"]):
            ref = w.at[kinds, slots, c, z, y, xh, xl]
            copies.append(links.copy(name, i, ref, ref, peer("z", k)))
        return copies

    z_first = first_step("z0", pl.ds(0, 1), pl.ds(0, 2))
    z_rank = first_step("zp", pl.ds(4, 1), pl.ds(0, 1))
    z_rest = first_step("z1", pl.ds(1, 3), pl.ds(0, 2))
    start(z_first + z_rank + z_rest)

    values = in_ref[...].astype(F32)
    scale = lax.rsqrt(jnp.mean(values * values, axis=1, keepdims=True) + norm_eps)
    normed[...] = (values * scale * gain_ref[...]).astype(BF16)
    b0 = len_ref[0, 0]
    b1 = b0 + len_ref[0, 1]
    b2 = b1 + len_ref[0, 2]
    b3 = b2 + len_ref[0, 3]

    def segment(position):
        return sum((position >= b).astype(jnp.int32) for b in (b0, b1, b2, b3))

    key = lax.broadcasted_iota(jnp.int32, (TOK, 1), 0)
    query = lax.broadcasted_iota(jnp.int32, (1, TOK), 1)
    seen = (segment(key) == segment(query)) & (query >= key)
    bias[...] = jnp.where(seen, F32(0.0), F32(-1e30))
    def middle(g):
        copies = []
        for kind, axis in ((0, "y"), (1, "x")):
            for k in SHIFTS[axis]:
                ref = w.at[kind, g, c, :, y, xh, xl]
                copies.append(links.copy("mid%d" % g, len(copies), ref, ref, peer(axis, k)))
        return copies

    depths = (pl.ds(0, 4), pl.ds(4, 4))

    def middle_p():
        copies = []
        for depth, axis in zip(depths, "yx"):
            for k in SHIFTS[axis]:
                ref = w.at[0, 4, c, depth, y, xh, xl]
                copies.append(links.copy("midp", len(copies), ref, ref, peer(axis, k)))
        return copies

    def rank_lines(p, at):
        if p == 0:
            return w.at[0, 4, c, depths[0], :, at // 2, lax.rem(at, 2)]
        return w.at[0, 4, c, depths[1], at]

    def along_x(slot, at):
        return w.at[0, slot, c, :, :, at // 2, lax.rem(at, 2)]

    def along_y(slot, at):
        return w.at[1, slot, c, :, at]

    def bulk(g):
        copies = []
        for i, k in enumerate(SHIFTS["x"]):
            ref = along_x(g, x)
            copies.append(links.copy("bulk", g * 6 + i, ref, ref, peer("x", k)))
        for i, k in enumerate(SHIFTS["y"]):
            ref = along_y(g, y)
            copies.append(links.copy("bulk", g * 6 + 3 + i, ref, ref, peer("y", k)))
        return copies

    def bulk_p():
        copies = []
        for p, axis in enumerate("xy"):
            ref = rank_lines(p, where[axis])
            for k in SHIFTS[axis]:
                copies.append(links.copy("bulk_p", len(copies), ref, ref, peer(axis, k)))
        return copies

    def across(g):
        refs = [along_x(g, x), along_y(g, y)]
        refs += [along_x(g, shifted(where, "x", -k)) for k in SHIFTS["x"]]
        refs += [along_y(g, shifted(where, "y", -k)) for k in SHIFTS["y"]]
        return [links.copy("across", g * 8 + i, r, r, sibling) for i, r in enumerate(refs)]

    def across_p():
        refs = [rank_lines(0, x), rank_lines(1, y)]
        for p, axis in enumerate("xy"):
            refs += [rank_lines(p, shifted(where, axis, -k)) for k in SHIFTS[axis]]
        return [links.copy("across_p", i, r, r, sibling) for i, r in enumerate(refs)]

    def open_bulk(g):
        start(bulk(g))
        start(across(g)[:2])

    def forward(g):
        for got, on in zip(bulk(g), across(g)[2:]):
            got.wait_recv()
            on.start()

    mids = [middle(g) for g in range(GROUPS)]
    mid_rank = middle_p()
    received(z_first)
    start(mids[0])
    received(z_rank)
    start(mid_rank)
    received(mids[0])
    open_bulk(0)
    received(z_rest)
    start(mids[1])
    received(mid_rank)
    start(bulk_p())
    start(across_p()[:2])

    spread = lax.broadcasted_iota(jnp.int32, (RANK, 256), 1)
    source = lax.broadcasted_iota(jnp.int32, (RANK, 256), 0)
    diagonal = (spread & 15) == (lax.broadcasted_iota(jnp.int32, (RANK, 256), 0) & 15)
    own_rows = own_p[...].astype(BF16)
    for n in range(16):
        kk = n * 16 + (spread >> 4)
        pick = (source == ((kk & 127) * 2 + (kk >> 7))).astype(F32).astype(BF16)
        line = dot(own_rows, pick)
        for i in range(4):
            lhs[i * 16 : (i + 1) * 16, n * 256 : (n + 1) * 256] = jnp.where(
                diagonal[:16], line[i : i + 1, :], F32(0.0)
            ).astype(BF16)

    forward(0)
    received(mids[1])
    open_bulk(1)
    start(mids[2])
    start(mids[3])

    lane = lax.broadcasted_iota(jnp.int32, (1, 128), 1)
    firsts = (lane < 64).astype(F32).astype(BF16)
    masks = (firsts, 1 - firsts)

    def weight(slot, low_x, core):
        halves = [w[a, slot, core, :, :, :, low_x].reshape(WIDTH, 128) for a in range(2)]
        return jnp.concatenate(halves, axis=1)

    def project(g):
        for src, low_x, core, out in (
            (normed, 0, 0, q_s), (normed, 0, 1, k_s), (normed, 1, 0, v_s), (gout_ref, 1, 1, gh_s)
        ):
            res = dot(src[...], weight(g, low_x, core))
            out[0] = res[:, :128].astype(out.dtype)
            out[1] = res[:, 128:].astype(out.dtype)

    def project_rank():
        both = [w[0, 4, core, :, :, :, 0].reshape(WIDTH, 128) for core in range(2)]
        proj = jnp.concatenate(both, axis=1)
        for src, out in ((normed, np_t), (gout_ref, gp_t)):
            high, rest = split(dot(src[...], proj).T)
            out[:, :TOK] = high
            out[:, TOK:] = rest

    def core_copy(g):
        return links.copy("core", g, low_s.at[g, 1 - c], r0.at[g], sibling)

    def sum1(g):
        return [
            links.copy("sum1", g * 3 + i, s1.at[g, i], v1.at[g, i], peer("x", k))
            for i, k in enumerate(SHIFTS["x"])
        ]

    def sum2(g):
        return [
            links.copy(
                "sum2", g * 3 + i, acc.at[g, shifted(where, "y", k)], v2.at[g, i], peer("y", k)
            )
            for i, k in enumerate(SHIFTS["y"])
        ]

    def stage_one(g):
        core_copy(g).wait_recv()
        copies = sum1(g)
        for i, k in enumerate(SHIFTS["x"]):
            to = shifted(where, "x", k)
            value = low_s[g, c, to] + r0[g, to]
            s1[g, i] = value.reshape(32, 4 * UNIT).astype(BF16)
            copies[i].start()
        acc[g] = low_s[g, c, x] + r0[g, x]

    def stage_two(g):
        received(sum1(g))
        total = (v1[g, 0].astype(F32) + v1[g, 1].astype(F32)) + v1[g, 2].astype(F32)
        acc[g] = acc[g] + total.reshape(NY, 8, 4 * UNIT)
        start(sum2(g))

    def stage_three(g):
        received(sum2(g))
        total = acc[g, y] + ((v2[g, 0] + v2[g, 1]) + v2[g, 2])
        h = g // 2
        for block in range(4):
            columns = pl.ds(
                pl.multiple_of(block * 2 * UNIT + lax.rem(g, 2) * UNIT, UNIT), UNIT
            )
            for i in range(NZ):
                rows[h, i, :, columns] = total[i : i + 1, block * UNIT : (block + 1) * UNIT]

    def sum3(h):
        return [
            links.copy(
                "sum3", h * 7 + i, rows.at[h, shifted(where, "z", k)], v3.at[h, i], peer("z", k)
            )
            for i, k in enumerate(SHIFTS["z"])
        ]

    def dir_z(h):
        own = tiles.at[h, c, z, y, x]
        return [
            links.copy("dir_z", h * 7 + i, own, own, peer("z", k))
            for i, k in enumerate(SHIFTS["z"])
        ]

    def summed(h):
        received(sum3(h))
        low = rows[h, z]
        for i in range(NZ - 1):
            low = low + v3[h, i]
        for block in range(4):
            columns = slice(block * WIDTH + h * 512, block * WIDTH + h * 512 + 512)
            part = low[:, block * 512 : (block + 1) * 512]
            low_out[:, columns] = part
            _, _, direction = adam(part, first_ref[:, columns], second_ref[:, columns])
            for a in range(4):
                dir_rows[block * 4 + a : block * 4 + a + 1, :] = direction[
                    :, a * 128 : (a + 1) * 128
                ]
        tiles[h, c, z, y, x] = dir_rows[...].astype(BF16)
        start(dir_z(h))

    paths = ((pl.ds(0, 4), "y", "x"), (pl.ds(4, 4), "x", "y"))

    def dir_mid(h):
        copies = []
        for depth, axis, _ in paths:
            own = tiles.at[h, c, depth, y, x]
            for k in SHIFTS[axis]:
                copies.append(
                    links.copy("dir_mid", h * 6 + len(copies), own, own, peer(axis, k))
                )
        return copies

    def lines(h, p, at):
        depth = paths[p][0]
        return tiles.at[h, c, depth, :, at] if p == 0 else tiles.at[h, c, depth, at]

    def dir_last(h):
        copies = []
        for p, (_, _, axis) in enumerate(paths):
            own = lines(h, p, where[axis])
            for k in SHIFTS[axis]:
                copies.append(
                    links.copy("dir_last", h * 6 + len(copies), own, own, peer(axis, k))
                )
        return copies

    def dir_across(h):
        refs = [lines(h, p, where[paths[p][2]]) for p in range(2)]
        for p, (_, _, axis) in enumerate(paths):
            refs += [lines(h, p, shifted(where, axis, -k)) for k in SHIFTS[axis]]
        return [
            links.copy("dir_across", h * 8 + i, r, r, sibling) for i, r in enumerate(refs)
        ]

    def hand_on(h):
        for got, on in zip(dir_last(h), dir_across(h)[2:]):
            got.wait_recv()
            on.start()

    def step_of(h):
        received(dir_across(h))
        columns = slice(h * 128, (h + 1) * 128)
        step_ref[:, columns] = dot(lhs[...], tiles[h].reshape(RANK * 16, 128))

    @pl.loop(0, 2 * GROUPS)
    def _(t):
        g, i = t // 2, lax.rem(t, 2)

        @pl.when(i == 0)
        def _():
            received(across(g))
            project(g)

            @pl.when(t > 0)
            def _():
                stage_one(g - 1)

        @pl.when(i == 1)
        def _():
            @pl.when(g > 0)
            def _():
                stage_two(g - 1)

            for later in (2, 3):

                @pl.when(g == later - 2)
                def _():
                    received(mids[later])
                    open_bulk(later)

        def between():
            @pl.when((i == 1) & (g < GROUPS - 1))
            def _():
                forward(g + 1)

            @pl.when(t == 0)
            def _():
                for got, on in zip(bulk_p(), across_p()[2:]):
                    got.wait_recv()
                    on.start()

        gq_t, gk, gv, attended_t = attend_pair(
            q_s[i], k_s[i], v_s[i], gh_s[i], bias, masks, between
        )

        @pl.when(t == 0)
        def _():
            received(across_p())
            project_rank()

        gq_t = (gq_t * 0.125).astype(BF16)
        low_q = dot(np_t[...], jnp.concatenate([gq_t, gq_t], axis=1), ROWS)
        grads = jnp.concatenate([(gk * 0.125).astype(BF16), gv.astype(BF16)], axis=1)
        low_kv = dot(np_t[...], jnp.concatenate([grads, grads], axis=0))
        attended_t = attended_t.astype(BF16)
        outer = dot(gp_t[...], jnp.concatenate([attended_t, attended_t], axis=1), ROWS)
        values = (low_q, low_kv[:, :128], low_kv[:, 128:], outer)
        for block in range(4):
            columns = pl.ds(pl.multiple_of(block * UNIT + i * 128, 128), 128)
            low_s[g, :, :, :, :, columns] = values[block].reshape(NC, NX, NY, NZ, 128)

        @pl.when(i == 1)
        def _():
            core_copy(g).start()

            @pl.when(g > 0)
            def _():
                stage_three(g - 1)

            @pl.when(g == 2)
            def _():
                start(sum3(0))

        @pl.when(t == 6)
        def _():
            summed(0)

    received(dir_z(0))
    start(dir_mid(0))
    stage_one(GROUPS - 1)
    stage_two(GROUPS - 1)
    received(dir_mid(0))
    start(dir_last(0))
    start(dir_across(0)[:2])
    stage_three(GROUPS - 1)
    start(sum3(1))
    hand_on(0)
    summed(1)
    step_of(0)
    received(dir_z(1))
    start(dir_mid(1))
    received(dir_mid(1))
    start(dir_last(1))
    start(dir_across(1)[:2])
    hand_on(1)
    step_of(1)

    sent(quad + z_first + z_rank + z_rest + mid_rank)
    for copies in mids:
        sent(copies)
    sent(bulk_p() + across_p())

    @pl.loop(0, GROUPS)
    def _(g):
        sent(bulk(g) + across(g) + [core_copy(g)] + sum1(g) + sum2(g))

    for h in range(2):
        sent(sum3(h) + dir_z(h) + dir_mid(h) + dir_last(h) + dir_across(h))


def main(lengths, inputs, grad_out, gain, master, projector, first, second):
    vmem = pl.BlockSpec(memory_space=pltpu.VMEM)
    return pl.pallas_call(
        main_kernel,
        out_shape=(
            jax.ShapeDtypeStruct((64, 256), F32),
            jax.ShapeDtypeStruct((1, 4 * WIDTH), F32),
        ),
        in_specs=[pl.BlockSpec(memory_space=pltpu.SMEM)] + [vmem] * 7,
        out_specs=(vmem, vmem),
        scratch_shapes=[
            pltpu.VMEM((2, 5, NC, NZ, NY, 2, 2, 16, 128), BF16),
            pltpu.VMEM((4, 4, WIDTH), F32),
            pltpu.VMEM((4, 4, RANK), F32),
            pltpu.VMEM((4, RANK), F32),
            pltpu.VMEM((16, WIDTH), F32),
            pltpu.VMEM((16, RANK), F32),
            pltpu.VMEM((RANK, RANK), BF16),
            pltpu.VMEM((TOK, WIDTH), BF16),
            pltpu.VMEM((TOK, TOK), F32),
            pltpu.VMEM((RANK, 2 * TOK), BF16),
            pltpu.VMEM((RANK, 2 * TOK), BF16),
            pltpu.VMEM((2, TOK, 128), BF16),
            pltpu.VMEM((2, TOK, 128), BF16),
            pltpu.VMEM((2, TOK, 128), BF16),
            pltpu.VMEM((2, TOK, 128), F32),
            pltpu.VMEM((GROUPS, NC, NX, NY, NZ, 4 * UNIT), F32),
            pltpu.VMEM((GROUPS, NX, NY, NZ, 4 * UNIT), F32),
            pltpu.VMEM((GROUPS, 3, 32, 4 * UNIT), BF16),
            pltpu.VMEM((GROUPS, 3, 32, 4 * UNIT), BF16),
            pltpu.VMEM((GROUPS, NY, NZ, 4 * UNIT), F32),
            pltpu.VMEM((GROUPS, 3, NZ, 4 * UNIT), F32),
            pltpu.VMEM((2, NZ, 1, 2 * WIDTH), F32),
            pltpu.VMEM((2, NZ - 1, 1, 2 * WIDTH), F32),
            pltpu.VMEM((16, 128), F32),
            pltpu.VMEM((2, NC, NZ, NY, NX, 16, 128), BF16),
            pltpu.VMEM((64, 4 * WIDTH), BF16),
            pltpu.SemaphoreType.DMA((N_SEMS,)),
            pltpu.SemaphoreType.DMA((N_SEMS,)),
        ],
        compiler_params=pltpu.CompilerParams(
            collective_id=0, has_side_effects=True, vmem_limit_bytes=VMEM_LIMIT
        ),
        name="galore_step",
    )(lengths, inputs, grad_out, gain, master, projector, first, second)


def finish_kernel(
    step_ref, low_ref, first_ref, second_ref, master_ref, new_master, new_first, new_second
):
    first, second, _ = adam(low_ref[...], first_ref[...], second_ref[...])
    new_first[...] = first
    new_second[...] = second
    for a in range(16):
        for h in range(2):
            at = (a // 4) * WIDTH + h * 512 + (a % 4) * 128
            columns = slice(at, at + 128)
            for i in range(4):
                row = i * 16 + a
                new_master[i : i + 1, columns] = (
                    master_ref[i : i + 1, columns]
                    - learn_rate * galore_scale * step_ref[row : row + 1, h * 128 : h * 128 + 128]
                )


def finish(step, low, first, second, master):
    vmem = pl.BlockSpec(memory_space=pltpu.VMEM)
    return pl.pallas_call(
        finish_kernel,
        out_shape=(
            jax.ShapeDtypeStruct((4, 4 * WIDTH), F32),
            jax.ShapeDtypeStruct((1, 4 * WIDTH), F32),
            jax.ShapeDtypeStruct((1, 4 * WIDTH), F32),
        ),
        in_specs=[vmem] * 5,
        out_specs=(vmem, vmem, vmem),
        name="outputs",
    )(step, low, first, second, master)


def shards(
    inputs, grad_out, norm_gain, master, projector, moment_first, moment_second, doc_lengths
):
    step, low = main(
        doc_lengths, inputs, grad_out, norm_gain[None, :], master, projector,
        moment_first, moment_second,
    )
    return finish(step, low, moment_first, moment_second, master)


def solution(mesh):
    return jax.shard_map(
        shards,
        mesh=mesh,
        in_specs=(
            P("dp", None),
            P("dp", None),
            P(),
            P("dp", None),
            P("dp", None),
            P("dp", None),
            P("dp", None),
            P("dp", None),
        ),
        out_specs=(P("dp", None), P("dp", None), P("dp", None)),
        check_vma=False,
    )
```

```python
import jax
import jax.numpy as jnp
import numpy as np
from jax import lax
from jax.experimental import pallas as pl
from jax.experimental.pallas import tpu as pltpu
from jax.sharding import PartitionSpec as P

NZ, NY, NX, NC = 8, 4, 4, 2
SIZE = {"z": NZ, "y": NY, "x": NX}
SHIFTS = {"z": (4, 3, 5, 2, 6, 1, 7), "y": (2, 1, 3), "x": (2, 1, 3)}
GROUPS = 4
UNIT = 256
TOK = 384
WIDTH = 1024
RANK = 256
VMEM_LIMIT = 56 * 1024 * 1024

beta_one = 0.9
beta_two = 0.999
adam_eps = 1e-08
adam_step = 10.0
learn_rate = 0.01
galore_scale = 0.25
norm_eps = 1e-05

F32 = jnp.float32
BF16 = jnp.bfloat16
MESH = pl.DeviceIdType.MESH


def place():
    me = lax.axis_index("dp")
    c = lax.rem(me, NC)
    x = lax.rem(me // NC, NX)
    y = lax.rem(me // (NC * NX), NY)
    z = me // (NC * NX * NY)
    return {"z": z, "y": y, "x": x, "c": c}


def device_at(where, **moved):
    at = dict(where, **moved)
    return ((at["z"] * NY + at["y"]) * NX + at["x"]) * NC + at["c"]


def shifted(where, axis, by):
    n = SIZE[axis]
    return lax.rem(where[axis] + (by + n), n)


class Links:
    def __init__(self, send_sems, recv_sems):
        self.send_sems, self.recv_sems = send_sems, recv_sems
        self.bases = {}
        self.used = 0

    def reserve(self, name, count):
        self.bases[name] = self.used
        self.used += count

    def copy(self, name, i, src, dst, device):
        at = self.bases[name] + i
        return pltpu.make_async_remote_copy(
            src_ref=src,
            dst_ref=dst,
            send_sem=self.send_sems.at[at],
            recv_sem=self.recv_sems.at[at],
            device_id=(device,),
            device_id_type=MESH,
        )


N_SEMS = 232


def start(copies):
    for copy in copies:
        copy.start()


def received(copies):
    for copy in copies:
        copy.wait_recv()


def sent(copies):
    for copy in copies:
        copy.wait_send()


def greet(devices):
    barrier = pltpu.get_barrier_semaphore()
    for device in devices:
        pl.semaphore_signal(barrier, inc=1, device_id=(device,), device_id_type=MESH)
    pl.semaphore_wait(barrier, len(devices))


def dot(a, b, dims=((1,), (0,))):
    return lax.dot_general(a, b, (dims, ((), ())), preferred_element_type=F32)


ROWS = ((1,), (1,))
COLS = ((0,), (0,))


def split(value):
    high = value.astype(BF16)
    return high, (value - high.astype(F32)).astype(BF16)


def adam(low, first, second):
    new_first = beta_one * first + (1.0 - beta_one) * low
    new_second = beta_two * second + (1.0 - beta_two) * low * low
    direction = (
        new_first
        / (1.0 - beta_one**adam_step)
        / (jnp.sqrt(new_second / (1.0 - beta_two**adam_step)) + adam_eps)
    )
    return new_first, new_second, direction


def attend_pair(q, k, v, gh, bias_ref, masks, between):
    probs, highs = [], []
    left_v, right_v = [], []
    for mask in masks:
        s = dot(k, q * mask, ROWS) * 0.125 + bias_ref[...]
        e = jnp.exp(s - jnp.max(s, axis=0, keepdims=True))
        p = e * (1.0 / jnp.sum(e, axis=0, keepdims=True))
        probs.append(p)
    between()
    gh_high, gh_rest = split(gh)
    v_twice = jnp.concatenate([v, v], axis=1)
    grads, right_k, left_q = [], [], []
    for p, mask in zip(probs, masks):
        p_high, p_rest = split(p)
        gh_m, gh_r = gh_high * mask, gh_rest * mask
        gp = dot(v_twice, jnp.concatenate([gh_m, gh_r], axis=1), ROWS)
        gs = p * (gp - jnp.sum(p * gp, axis=0, keepdims=True))
        highs.append(p_high)
        left_v += [p_high, p_rest, p_high]
        right_v += [gh_m, gh_m, gh_r]
        grads += list(split(gs))
        right_k += [q * mask] * 2
        left_q += [k * mask] * 2
    gv = dot(jnp.concatenate(left_v, axis=1), jnp.concatenate(right_v, axis=0))
    gk = dot(jnp.concatenate(grads, axis=1), jnp.concatenate(right_k, axis=0))
    gq_t = dot(jnp.concatenate(left_q, axis=0), jnp.concatenate(grads, axis=0), COLS)
    by_head = jnp.concatenate([v * mask for mask in masks], axis=0)
    a_t = dot(by_head, jnp.concatenate(highs, axis=0), COLS)
    return gq_t, gk, gv, a_t


def main_kernel(
    len_ref, in_ref, gout_ref, gain_ref, master_ref, proj_ref, first_ref, second_ref,
    step_ref, low_out,
    w, quad_w, quad_p, own_p, rows_w, rows_p, order, normed, bias, np_t, gp_t,
    q_s, k_s, v_s, gh_s, low_s, r0, s1, v1, acc, v2, rows, v3, dir_rows, tiles, lhs,
    send_sems, recv_sems
):
    where = place()
    c, x, y, z = where["c"], where["x"], where["y"], where["z"]
    xh, xl = x // 2, lax.rem(x, 2)
    flip = x + 1 - 2 * xl
    sibling = device_at(where, c=1 - c)
    links = Links(send_sems, recv_sems)
    for name, count in (
        ("quad", 6), ("z0", 7), ("zp", 7), ("z1", 7), ("mid0", 6), ("midp", 6), ("mid1", 6), ("mid2", 6),
        ("x3", 3),
        ("y3", 3), ("z3", 7),
        ("bulk", 24), ("across", 32), ("bulk_p", 6), ("across_p", 8), ("core", 4),
        ("sum1", 12), ("sum2", 12), ("sum3", 14), ("dir_z", 14), ("dir_mid", 12),
        ("dir_last", 12), ("dir_across", 16),
    ):
        links.reserve(name, count)

    def peer(axis, by):
        return device_at(where, **{axis: shifted(where, axis, by)})

    greet(
        [sibling, device_at(where, x=flip, c=1 - c)]
        + [peer(axis, k) for axis in "xyz" for k in SHIFTS[axis]]
    )

    own_p[...] = proj_ref[...].astype(F32)
    mine = xl * 2 + c
    quad = []
    for i, (dx, dc) in enumerate(((0, 1), (1, 0), (1, 1))):
        to_xl = 1 - xl if dx else xl
        to_c = 1 - c if dc else c
        to = device_at(where, x=xh * 2 + to_xl, c=to_c)
        columns = pl.ds(pl.multiple_of((to_xl * 2 + to_c) * WIDTH, WIDTH), WIDTH)
        quad.append(
            links.copy("quad", 2 * i, master_ref.at[:, columns], quad_w.at[mine], to)
        )
        quad.append(links.copy("quad", 2 * i + 1, own_p, quad_p.at[mine], to))
    start(quad)
    columns = pl.ds(pl.multiple_of(mine * WIDTH, WIDTH), WIDTH)
    quad_w[mine] = master_ref[:, columns]
    quad_p[mine] = own_p[...]

    source = lax.broadcasted_iota(jnp.int32, (RANK, RANK), 0)
    place_to = lax.broadcasted_iota(jnp.int32, (RANK, RANK), 1)
    natural = (
        (place_to & 7) * 32
        + ((place_to >> 3) & 3) * 8
        + ((place_to >> 5) & 3) * 2
        + (place_to >> 7)
    )
    order[...] = (source == natural).astype(F32).astype(BF16)

    received(quad)
    for i in range(4):
        rows_w[i * 4 : i * 4 + 4, :] = quad_w[i]
        rows_p[i * 4 : i * 4 + 4, :] = quad_p[i]
    ordered = dot(rows_p[...].astype(BF16), order[...])
    w[0, 4, c, z, y, xh, xl] = jnp.where(c == 0, ordered[:, :128], ordered[:, 128:]).astype(
        BF16
    )
    for pair in range(8):
        w[pair % 2, pair // 2, c, z, y, xh, xl] = rows_w[
            :, pair * 128 : (pair + 1) * 128
        ].astype(BF16)

    def first_step(name, slots, kinds):
        copies = []
        for i, k in enumerate(SHIFTS["z"]):
            ref = w.at[kinds, slots, c, z, y, xh, xl]
            copies.append(links.copy(name, i, ref, ref, peer("z", k)))
        return copies

    z_first = first_step("z0", pl.ds(0, 1), pl.ds(0, 2))
    z_rank = first_step("zp", pl.ds(4, 1), pl.ds(0, 1))
    z_rest = first_step("z1", pl.ds(1, 2), pl.ds(0, 2))

    def other_way(name, axis, ref):
        return [
            links.copy(name, i, ref, ref, peer(axis, k)) for i, k in enumerate(SHIFTS[axis])
        ]

    x_last = other_way("x3", "x", w.at[:, 3, c, z, y, xh, xl])
    y_last = other_way("y3", "y", w.at[:, 3, c, z, y])
    z_last = other_way("z3", "z", w.at[:, 3, c, z])
    start(z_first + z_rank + x_last + z_rest)

    values = in_ref[...].astype(F32)
    scale = lax.rsqrt(jnp.mean(values * values, axis=1, keepdims=True) + norm_eps)
    normed[...] = (values * scale * gain_ref[...]).astype(BF16)
    b0 = len_ref[0, 0]
    b1 = b0 + len_ref[0, 1]
    b2 = b1 + len_ref[0, 2]
    b3 = b2 + len_ref[0, 3]

    def segment(position):
        return sum((position >= b).astype(jnp.int32) for b in (b0, b1, b2, b3))

    key = lax.broadcasted_iota(jnp.int32, (TOK, 1), 0)
    query = lax.broadcasted_iota(jnp.int32, (1, TOK), 1)
    seen = (segment(key) == segment(query)) & (query >= key)
    bias[...] = jnp.where(seen, F32(0.0), F32(-1e30))
    def middle(g):
        copies = []
        for kind, axis in ((0, "y"), (1, "x")):
            for k in SHIFTS[axis]:
                ref = w.at[kind, g, c, :, y, xh, xl]
                copies.append(links.copy("mid%d" % g, len(copies), ref, ref, peer(axis, k)))
        return copies

    depths = (pl.ds(0, 4), pl.ds(4, 4))

    def middle_p():
        copies = []
        for depth, axis in zip(depths, "yx"):
            for k in SHIFTS[axis]:
                ref = w.at[0, 4, c, depth, y, xh, xl]
                copies.append(links.copy("midp", len(copies), ref, ref, peer(axis, k)))
        return copies

    def rank_lines(p, at):
        if p == 0:
            return w.at[0, 4, c, depths[0], :, at // 2, lax.rem(at, 2)]
        return w.at[0, 4, c, depths[1], at]

    def along_x(slot, at):
        return w.at[0, slot, c, :, :, at // 2, lax.rem(at, 2)]

    def along_y(slot, at):
        return w.at[1, slot, c, :, at]

    def bulk(g):
        copies = []
        for i, k in enumerate(SHIFTS["x"]):
            ref = along_x(g, x)
            copies.append(links.copy("bulk", g * 6 + i, ref, ref, peer("x", k)))
        for i, k in enumerate(SHIFTS["y"]):
            ref = along_y(g, y)
            copies.append(links.copy("bulk", g * 6 + 3 + i, ref, ref, peer("y", k)))
        return copies

    def bulk_p():
        copies = []
        for p, axis in enumerate("xy"):
            ref = rank_lines(p, where[axis])
            for k in SHIFTS[axis]:
                copies.append(links.copy("bulk_p", len(copies), ref, ref, peer(axis, k)))
        return copies

    def across(g):
        refs = [along_x(g, x), along_y(g, y)]
        refs += [along_x(g, shifted(where, "x", -k)) for k in SHIFTS["x"]]
        refs += [along_y(g, shifted(where, "y", -k)) for k in SHIFTS["y"]]
        return [links.copy("across", g * 8 + i, r, r, sibling) for i, r in enumerate(refs)]

    def across_p():
        refs = [rank_lines(0, x), rank_lines(1, y)]
        for p, axis in enumerate("xy"):
            refs += [rank_lines(p, shifted(where, axis, -k)) for k in SHIFTS[axis]]
        return [links.copy("across_p", i, r, r, sibling) for i, r in enumerate(refs)]

    def open_bulk(g):
        start(bulk(g))
        start(across(g)[:2])

    def forward(g):
        for got, on in zip(bulk(g), across(g)[2:]):
            got.wait_recv()
            on.start()

    def across_last():
        refs = [w.at[:, 3, c, z]]
        refs += [w.at[:, 3, c, shifted(where, "z", -k)] for k in SHIFTS["z"]]
        return [links.copy("across", 24 + i, r, r, sibling) for i, r in enumerate(refs)]

    mids = [middle(g) for g in range(GROUPS - 1)]
    mid_rank = middle_p()
    received(z_first)
    start(mids[0])
    received(z_rank)
    start(mid_rank)
    received(x_last)
    start(y_last)
    received(mids[0])
    open_bulk(0)
    received(z_rest)
    start(mids[1])
    received(mid_rank)
    start(bulk_p())
    start(across_p()[:2])
    received(y_last)
    start(z_last)
    start(across_last()[:1])

    spread = lax.broadcasted_iota(jnp.int32, (RANK, 256), 1)
    source = lax.broadcasted_iota(jnp.int32, (RANK, 256), 0)
    diagonal = (spread & 15) == (lax.broadcasted_iota(jnp.int32, (RANK, 256), 0) & 15)
    own_rows = own_p[...].astype(BF16)
    for n in range(16):
        kk = n * 16 + (spread >> 4)
        pick = (source == ((kk & 127) * 2 + (kk >> 7))).astype(F32).astype(BF16)
        line = dot(own_rows, pick)
        for i in range(4):
            lhs[i * 16 : (i + 1) * 16, n * 256 : (n + 1) * 256] = jnp.where(
                diagonal[:16], line[i : i + 1, :], F32(0.0)
            ).astype(BF16)

    forward(0)
    received(mids[1])
    open_bulk(1)
    start(mids[2])

    lane = lax.broadcasted_iota(jnp.int32, (1, 128), 1)
    firsts = (lane < 64).astype(F32).astype(BF16)
    masks = (firsts, 1 - firsts)

    def weight(slot, low_x, core):
        halves = [w[a, slot, core, :, :, :, low_x].reshape(WIDTH, 128) for a in range(2)]
        return jnp.concatenate(halves, axis=1)

    def project(g):
        for src, low_x, core, out in (
            (normed, 0, 0, q_s), (normed, 0, 1, k_s), (normed, 1, 0, v_s), (gout_ref, 1, 1, gh_s)
        ):
            res = dot(src[...], weight(g, low_x, core))
            out[0] = res[:, :128].astype(out.dtype)
            out[1] = res[:, 128:].astype(out.dtype)

    def project_rank():
        both = [w[0, 4, core, :, :, :, 0].reshape(WIDTH, 128) for core in range(2)]
        proj = jnp.concatenate(both, axis=1)
        for src, out in ((normed, np_t), (gout_ref, gp_t)):
            high, rest = split(dot(src[...], proj).T)
            out[:, :TOK] = high
            out[:, TOK:] = rest

    def core_copy(g):
        return links.copy("core", g, low_s.at[g, 1 - c], r0.at[g], sibling)

    def sum1(g):
        return [
            links.copy("sum1", g * 3 + i, s1.at[g, i], v1.at[g, i], peer("x", k))
            for i, k in enumerate(SHIFTS["x"])
        ]

    def sum2(g):
        return [
            links.copy(
                "sum2", g * 3 + i, acc.at[g, shifted(where, "y", k)], v2.at[g, i], peer("y", k)
            )
            for i, k in enumerate(SHIFTS["y"])
        ]

    def stage_one(g):
        core_copy(g).wait_recv()
        copies = sum1(g)
        for i, k in enumerate(SHIFTS["x"]):
            to = shifted(where, "x", k)
            value = low_s[g, c, to] + r0[g, to]
            s1[g, i] = value.reshape(32, 4 * UNIT).astype(BF16)
            copies[i].start()
        acc[g] = low_s[g, c, x] + r0[g, x]

    def stage_two(g):
        received(sum1(g))
        total = (v1[g, 0].astype(F32) + v1[g, 1].astype(F32)) + v1[g, 2].astype(F32)
        acc[g] = acc[g] + total.reshape(NY, 8, 4 * UNIT)
        start(sum2(g))

    def stage_three(g):
        received(sum2(g))
        total = acc[g, y] + ((v2[g, 0] + v2[g, 1]) + v2[g, 2])
        h = g // 2
        for block in range(4):
            columns = pl.ds(
                pl.multiple_of(block * 2 * UNIT + lax.rem(g, 2) * UNIT, UNIT), UNIT
            )
            for i in range(NZ):
                rows[h, i, :, columns] = total[i : i + 1, block * UNIT : (block + 1) * UNIT]

    def sum3(h):
        return [
            links.copy(
                "sum3", h * 7 + i, rows.at[h, shifted(where, "z", k)], v3.at[h, i], peer("z", k)
            )
            for i, k in enumerate(SHIFTS["z"])
        ]

    def dir_z(h):
        own = tiles.at[h, c, z, y, x]
        return [
            links.copy("dir_z", h * 7 + i, own, own, peer("z", k))
            for i, k in enumerate(SHIFTS["z"])
        ]

    def summed(h):
        received(sum3(h))
        low = rows[h, z]
        for i in range(NZ - 1):
            low = low + v3[h, i]
        for block in range(4):
            columns = slice(block * WIDTH + h * 512, block * WIDTH + h * 512 + 512)
            part = low[:, block * 512 : (block + 1) * 512]
            low_out[:, columns] = part
            _, _, direction = adam(part, first_ref[:, columns], second_ref[:, columns])
            for a in range(4):
                dir_rows[block * 4 + a : block * 4 + a + 1, :] = direction[
                    :, a * 128 : (a + 1) * 128
                ]
        tiles[h, c, z, y, x] = dir_rows[...].astype(BF16)
        start(dir_z(h))

    paths = ((pl.ds(0, 4), "y", "x"), (pl.ds(4, 4), "x", "y"))

    def dir_mid(h):
        copies = []
        for depth, axis, _ in paths:
            own = tiles.at[h, c, depth, y, x]
            for k in SHIFTS[axis]:
                copies.append(
                    links.copy("dir_mid", h * 6 + len(copies), own, own, peer(axis, k))
                )
        return copies

    def lines(h, p, at):
        depth = paths[p][0]
        return tiles.at[h, c, depth, :, at] if p == 0 else tiles.at[h, c, depth, at]

    def dir_last(h):
        copies = []
        for p, (_, _, axis) in enumerate(paths):
            own = lines(h, p, where[axis])
            for k in SHIFTS[axis]:
                copies.append(
                    links.copy("dir_last", h * 6 + len(copies), own, own, peer(axis, k))
                )
        return copies

    def dir_across(h):
        refs = [lines(h, p, where[paths[p][2]]) for p in range(2)]
        for p, (_, _, axis) in enumerate(paths):
            refs += [lines(h, p, shifted(where, axis, -k)) for k in SHIFTS[axis]]
        return [
            links.copy("dir_across", h * 8 + i, r, r, sibling) for i, r in enumerate(refs)
        ]

    def hand_on(h):
        for got, on in zip(dir_last(h), dir_across(h)[2:]):
            got.wait_recv()
            on.start()

    def step_of(h):
        received(dir_across(h))
        columns = slice(h * 128, (h + 1) * 128)
        step_ref[:, columns] = dot(lhs[...], tiles[h].reshape(RANK * 16, 128))

    @pl.loop(0, 2 * GROUPS)
    def _(t):
        g, i = t // 2, lax.rem(t, 2)

        @pl.when(i == 0)
        def _():
            @pl.when(g < GROUPS - 1)
            def _():
                received(across(g))

            @pl.when(g == GROUPS - 1)
            def _():
                received(across_last())

            project(g)

            @pl.when(t > 0)
            def _():
                stage_one(g - 1)

        @pl.when(i == 1)
        def _():
            @pl.when(g > 0)
            def _():
                stage_two(g - 1)

            @pl.when(g == 0)
            def _():
                received(mids[2])
                open_bulk(2)

        def between():
            @pl.when((i == 1) & (g < GROUPS - 2))
            def _():
                forward(g + 1)

            @pl.when((i == 1) & (g == GROUPS - 2))
            def _():
                for got, on in zip(z_last, across_last()[1:]):
                    got.wait_recv()
                    on.start()

            @pl.when(t == 0)
            def _():
                for got, on in zip(bulk_p(), across_p()[2:]):
                    got.wait_recv()
                    on.start()

        gq_t, gk, gv, attended_t = attend_pair(
            q_s[i], k_s[i], v_s[i], gh_s[i], bias, masks, between
        )

        @pl.when(t == 0)
        def _():
            received(across_p())
            project_rank()

        gq_t = (gq_t * 0.125).astype(BF16)
        low_q = dot(np_t[...], jnp.concatenate([gq_t, gq_t], axis=1), ROWS)
        grads = jnp.concatenate([(gk * 0.125).astype(BF16), gv.astype(BF16)], axis=1)
        low_kv = dot(np_t[...], jnp.concatenate([grads, grads], axis=0))
        attended_t = attended_t.astype(BF16)
        outer = dot(gp_t[...], jnp.concatenate([attended_t, attended_t], axis=1), ROWS)
        values = (low_q, low_kv[:, :128], low_kv[:, 128:], outer)
        for block in range(4):
            columns = pl.ds(pl.multiple_of(block * UNIT + i * 128, 128), 128)
            low_s[g, :, :, :, :, columns] = values[block].reshape(NC, NX, NY, NZ, 128)

        @pl.when(i == 1)
        def _():
            core_copy(g).start()

            @pl.when(g > 0)
            def _():
                stage_three(g - 1)

            @pl.when(g == 2)
            def _():
                start(sum3(0))

        @pl.when(t == 6)
        def _():
            summed(0)

    stage_one(GROUPS - 1)
    received(dir_z(0))
    start(dir_mid(0))
    stage_two(GROUPS - 1)
    received(dir_mid(0))
    start(dir_last(0))
    start(dir_across(0)[:2])
    stage_three(GROUPS - 1)
    start(sum3(1))
    hand_on(0)
    summed(1)
    step_of(0)
    received(dir_z(1))
    start(dir_mid(1))
    received(dir_mid(1))
    start(dir_last(1))
    start(dir_across(1)[:2])
    hand_on(1)
    step_of(1)

    sent(quad + z_first + z_rank + z_rest + mid_rank)
    for copies in mids:
        sent(copies)
    sent(bulk_p() + across_p())

    @pl.loop(0, GROUPS)
    def _(g):
        sent([core_copy(g)] + sum1(g) + sum2(g))

        @pl.when(g < GROUPS - 1)
        def _():
            sent(bulk(g) + across(g))

    sent(x_last + y_last + z_last + across_last())

    for h in range(2):
        sent(sum3(h) + dir_z(h) + dir_mid(h) + dir_last(h) + dir_across(h))


def main(lengths, inputs, grad_out, gain, master, projector, first, second):
    vmem = pl.BlockSpec(memory_space=pltpu.VMEM)
    return pl.pallas_call(
        main_kernel,
        out_shape=(
            jax.ShapeDtypeStruct((64, 256), F32),
            jax.ShapeDtypeStruct((1, 4 * WIDTH), F32),
        ),
        in_specs=[pl.BlockSpec(memory_space=pltpu.SMEM)] + [vmem] * 7,
        out_specs=(vmem, vmem),
        scratch_shapes=[
            pltpu.VMEM((2, 5, NC, NZ, NY, 2, 2, 16, 128), BF16),
            pltpu.VMEM((4, 4, WIDTH), F32),
            pltpu.VMEM((4, 4, RANK), F32),
            pltpu.VMEM((4, RANK), F32),
            pltpu.VMEM((16, WIDTH), F32),
            pltpu.VMEM((16, RANK), F32),
            pltpu.VMEM((RANK, RANK), BF16),
            pltpu.VMEM((TOK, WIDTH), BF16),
            pltpu.VMEM((TOK, TOK), F32),
            pltpu.VMEM((RANK, 2 * TOK), BF16),
            pltpu.VMEM((RANK, 2 * TOK), BF16),
            pltpu.VMEM((2, TOK, 128), BF16),
            pltpu.VMEM((2, TOK, 128), BF16),
            pltpu.VMEM((2, TOK, 128), BF16),
            pltpu.VMEM((2, TOK, 128), F32),
            pltpu.VMEM((GROUPS, NC, NX, NY, NZ, 4 * UNIT), F32),
            pltpu.VMEM((GROUPS, NX, NY, NZ, 4 * UNIT), F32),
            pltpu.VMEM((GROUPS, 3, 32, 4 * UNIT), BF16),
            pltpu.VMEM((GROUPS, 3, 32, 4 * UNIT), BF16),
            pltpu.VMEM((GROUPS, NY, NZ, 4 * UNIT), F32),
            pltpu.VMEM((GROUPS, 3, NZ, 4 * UNIT), F32),
            pltpu.VMEM((2, NZ, 1, 2 * WIDTH), F32),
            pltpu.VMEM((2, NZ - 1, 1, 2 * WIDTH), F32),
            pltpu.VMEM((16, 128), F32),
            pltpu.VMEM((2, NC, NZ, NY, NX, 16, 128), BF16),
            pltpu.VMEM((64, 4 * WIDTH), BF16),
            pltpu.SemaphoreType.DMA((N_SEMS,)),
            pltpu.SemaphoreType.DMA((N_SEMS,)),
        ],
        compiler_params=pltpu.CompilerParams(
            collective_id=0, has_side_effects=True, vmem_limit_bytes=VMEM_LIMIT
        ),
        name="galore_step",
    )(lengths, inputs, grad_out, gain, master, projector, first, second)


def finish_kernel(
    step_ref, low_ref, first_ref, second_ref, master_ref, new_master, new_first, new_second
):
    first, second, _ = adam(low_ref[...], first_ref[...], second_ref[...])
    new_first[...] = first
    new_second[...] = second
    for a in range(16):
        for h in range(2):
            at = (a // 4) * WIDTH + h * 512 + (a % 4) * 128
            columns = slice(at, at + 128)
            for i in range(4):
                row = i * 16 + a
                new_master[i : i + 1, columns] = (
                    master_ref[i : i + 1, columns]
                    - learn_rate * galore_scale * step_ref[row : row + 1, h * 128 : h * 128 + 128]
                )


def finish(step, low, first, second, master):
    vmem = pl.BlockSpec(memory_space=pltpu.VMEM)
    return pl.pallas_call(
        finish_kernel,
        out_shape=(
            jax.ShapeDtypeStruct((4, 4 * WIDTH), F32),
            jax.ShapeDtypeStruct((1, 4 * WIDTH), F32),
            jax.ShapeDtypeStruct((1, 4 * WIDTH), F32),
        ),
        in_specs=[vmem] * 5,
        out_specs=(vmem, vmem, vmem),
        name="outputs",
    )(step, low, first, second, master)


def shards(
    inputs, grad_out, norm_gain, master, projector, moment_first, moment_second, doc_lengths
):
    step, low = main(
        doc_lengths, inputs, grad_out, norm_gain[None, :], master, projector,
        moment_first, moment_second,
    )
    return finish(step, low, moment_first, moment_second, master)


def solution(mesh):
    return jax.shard_map(
        shards,
        mesh=mesh,
        in_specs=(
            P("dp", None),
            P("dp", None),
            P(),
            P("dp", None),
            P("dp", None),
            P("dp", None),
            P("dp", None),
            P("dp", None),
        ),
        out_specs=(P("dp", None), P("dp", None), P("dp", None)),
        check_vma=False,
    )
```

```python
import jax
import jax.numpy as jnp
import numpy as np
from jax import lax
from jax.experimental import pallas as pl
from jax.experimental.pallas import tpu as pltpu
from jax.sharding import PartitionSpec as P

NZ, NY, NX, NC = 8, 4, 4, 2
SIZE = {"z": NZ, "y": NY, "x": NX}
SHIFTS = {"z": (4, 3, 5, 2, 6, 1, 7), "y": (2, 1, 3), "x": (2, 1, 3)}
GROUPS = 4
UNIT = 256
TOK = 384
WIDTH = 1024
RANK = 256
VMEM_LIMIT = 56 * 1024 * 1024

beta_one = 0.9
beta_two = 0.999
adam_eps = 1e-08
adam_step = 10.0
learn_rate = 0.01
galore_scale = 0.25
norm_eps = 1e-05

F32 = jnp.float32
BF16 = jnp.bfloat16
MESH = pl.DeviceIdType.MESH


def place():
    me = lax.axis_index("dp")
    c = lax.rem(me, NC)
    x = lax.rem(me // NC, NX)
    y = lax.rem(me // (NC * NX), NY)
    z = me // (NC * NX * NY)
    return {"z": z, "y": y, "x": x, "c": c}


def device_at(where, **moved):
    at = dict(where, **moved)
    return ((at["z"] * NY + at["y"]) * NX + at["x"]) * NC + at["c"]


def shifted(where, axis, by):
    n = SIZE[axis]
    return lax.rem(where[axis] + (by + n), n)


class Links:
    def __init__(self, send_sems, recv_sems):
        self.send_sems, self.recv_sems = send_sems, recv_sems
        self.bases = {}
        self.used = 0

    def reserve(self, name, count):
        self.bases[name] = self.used
        self.used += count

    def copy(self, name, i, src, dst, device):
        at = self.bases[name] + i
        return pltpu.make_async_remote_copy(
            src_ref=src,
            dst_ref=dst,
            send_sem=self.send_sems.at[at],
            recv_sem=self.recv_sems.at[at],
            device_id=(device,),
            device_id_type=MESH,
        )


N_SEMS = 232


def start(copies):
    for copy in copies:
        copy.start()


def received(copies):
    for copy in copies:
        copy.wait_recv()


def sent(copies):
    for copy in copies:
        copy.wait_send()


def greet(devices):
    barrier = pltpu.get_barrier_semaphore()
    for device in devices:
        pl.semaphore_signal(barrier, inc=1, device_id=(device,), device_id_type=MESH)
    pl.semaphore_wait(barrier, len(devices))


def dot(a, b, dims=((1,), (0,))):
    return lax.dot_general(a, b, (dims, ((), ())), preferred_element_type=F32)


ROWS = ((1,), (1,))
COLS = ((0,), (0,))


def split(value):
    high = value.astype(BF16)
    return high, (value - high.astype(F32)).astype(BF16)


def adam(low, first, second):
    new_first = beta_one * first + (1.0 - beta_one) * low
    new_second = beta_two * second + (1.0 - beta_two) * low * low
    direction = (
        new_first
        / (1.0 - beta_one**adam_step)
        / (jnp.sqrt(new_second / (1.0 - beta_two**adam_step)) + adam_eps)
    )
    return new_first, new_second, direction


def attend_pair(q, k, v, gh, bias_ref, masks, between):
    probs, highs = [], []
    left_v, right_v = [], []
    for mask in masks:
        s = dot(k, q * mask, ROWS) * 0.125 + bias_ref[...]
        e = jnp.exp(s - jnp.max(s, axis=0, keepdims=True))
        p = e * (1.0 / jnp.sum(e, axis=0, keepdims=True))
        probs.append(p)
    between()
    gh_high, gh_rest = split(gh)
    v_twice = jnp.concatenate([v, v], axis=1)
    grads, right_k, left_q = [], [], []
    for p, mask in zip(probs, masks):
        p_high, p_rest = split(p)
        gh_m, gh_r = gh_high * mask, gh_rest * mask
        gp = dot(v_twice, jnp.concatenate([gh_m, gh_r], axis=1), ROWS)
        gs = p * (gp - jnp.sum(p * gp, axis=0, keepdims=True))
        highs.append(p_high)
        left_v += [p_high, p_rest, p_high]
        right_v += [gh_m, gh_m, gh_r]
        grads += list(split(gs))
        right_k += [q * mask] * 2
        left_q += [k * mask] * 2
    gv = dot(jnp.concatenate(left_v, axis=1), jnp.concatenate(right_v, axis=0))
    gk = dot(jnp.concatenate(grads, axis=1), jnp.concatenate(right_k, axis=0))
    gq_t = dot(jnp.concatenate(left_q, axis=0), jnp.concatenate(grads, axis=0), COLS)
    by_head = jnp.concatenate([v * mask for mask in masks], axis=0)
    a_t = dot(by_head, jnp.concatenate(highs, axis=0), COLS)
    return gq_t, gk, gv, a_t


def main_kernel(
    len_ref, in_ref, gout_ref, gain_ref, master_ref, proj_ref, first_ref, second_ref,
    step_ref, low_out,
    w, quad_w, quad_p, own_p, rows_w, rows_p, order, normed, bias, np_t, gp_t,
    q_s, k_s, v_s, gh_s, low_s, r0, s1, v1, acc, v2, rows, v3, dir_rows, tiles, lhs,
    send_sems, recv_sems
):
    where = place()
    c, x, y, z = where["c"], where["x"], where["y"], where["z"]
    xh, xl = x // 2, lax.rem(x, 2)
    flip = x + 1 - 2 * xl
    sibling = device_at(where, c=1 - c)
    links = Links(send_sems, recv_sems)
    for name, count in (
        ("quad", 6), ("z0", 7), ("zp", 7), ("z1", 7), ("mid0", 6), ("midp", 6), ("mid1", 6), ("mid2", 6),
        ("x3", 3),
        ("y3", 3), ("z3", 7),
        ("bulk", 24), ("across", 32), ("bulk_p", 6), ("across_p", 8), ("core", 4),
        ("sum1", 12), ("sum2", 12), ("sum3", 14), ("dir_z", 14), ("dir_mid", 12),
        ("dir_last", 12), ("dir_across", 16),
    ):
        links.reserve(name, count)

    def peer(axis, by):
        return device_at(where, **{axis: shifted(where, axis, by)})

    greet(
        [sibling, device_at(where, x=flip, c=1 - c)]
        + [peer(axis, k) for axis in "xyz" for k in SHIFTS[axis]]
    )

    own_p[...] = proj_ref[...].astype(F32)
    mine = xl * 2 + c
    quad = []
    for i, (dx, dc) in enumerate(((0, 1), (1, 0), (1, 1))):
        to_xl = 1 - xl if dx else xl
        to_c = 1 - c if dc else c
        to = device_at(where, x=xh * 2 + to_xl, c=to_c)
        columns = pl.ds(pl.multiple_of((to_xl * 2 + to_c) * WIDTH, WIDTH), WIDTH)
        quad.append(
            links.copy("quad", 2 * i, master_ref.at[:, columns], quad_w.at[mine], to)
        )
        quad.append(links.copy("quad", 2 * i + 1, own_p, quad_p.at[mine], to))
    start(quad)
    columns = pl.ds(pl.multiple_of(mine * WIDTH, WIDTH), WIDTH)
    quad_w[mine] = master_ref[:, columns]
    quad_p[mine] = own_p[...]

    source = lax.broadcasted_iota(jnp.int32, (RANK, RANK), 0)
    place_to = lax.broadcasted_iota(jnp.int32, (RANK, RANK), 1)
    natural = (
        (place_to & 7) * 32
        + ((place_to >> 3) & 3) * 8
        + ((place_to >> 5) & 3) * 2
        + (place_to >> 7)
    )
    order[...] = (source == natural).astype(F32).astype(BF16)

    received(quad)
    for i in range(4):
        rows_w[i * 4 : i * 4 + 4, :] = quad_w[i]
        rows_p[i * 4 : i * 4 + 4, :] = quad_p[i]
    ordered = dot(rows_p[...].astype(BF16), order[...])
    w[0, 4, c, z, y, xh, xl] = jnp.where(c == 0, ordered[:, :128], ordered[:, 128:]).astype(
        BF16
    )
    for pair in range(8):
        w[pair % 2, pair // 2, c, z, y, xh, xl] = rows_w[
            :, pair * 128 : (pair + 1) * 128
        ].astype(BF16)

    def first_step(name, slots, kinds):
        copies = []
        for i, k in enumerate(SHIFTS["z"]):
            ref = w.at[kinds, slots, c, z, y, xh, xl]
            copies.append(links.copy(name, i, ref, ref, peer("z", k)))
        return copies

    z_first = first_step("z0", pl.ds(0, 1), pl.ds(0, 2))
    z_rank = first_step("zp", pl.ds(4, 1), pl.ds(0, 1))
    z_rest = first_step("z1", pl.ds(1, 2), pl.ds(0, 2))

    def other_way(name, axis, ref):
        return [
            links.copy(name, i, ref, ref, peer(axis, k)) for i, k in enumerate(SHIFTS[axis])
        ]

    x_last = other_way("x3", "x", w.at[:, 3, c, z, y, xh, xl])
    y_last = other_way("y3", "y", w.at[:, 3, c, z, y])
    z_last = other_way("z3", "z", w.at[:, 3, c, z])
    start(z_first + z_rank + x_last + z_rest)

    values = in_ref[...].astype(F32)
    scale = lax.rsqrt(jnp.mean(values * values, axis=1, keepdims=True) + norm_eps)
    normed[...] = (values * scale * gain_ref[...]).astype(BF16)
    b0 = len_ref[0, 0]
    b1 = b0 + len_ref[0, 1]
    b2 = b1 + len_ref[0, 2]
    b3 = b2 + len_ref[0, 3]

    def segment(position):
        return sum((position >= b).astype(jnp.int32) for b in (b0, b1, b2, b3))

    key = lax.broadcasted_iota(jnp.int32, (TOK, 1), 0)
    query = lax.broadcasted_iota(jnp.int32, (1, TOK), 1)
    seen = (segment(key) == segment(query)) & (query >= key)
    bias[...] = jnp.where(seen, F32(0.0), F32(-1e30))
    def middle(g):
        copies = []
        for kind, axis in ((0, "y"), (1, "x")):
            for k in SHIFTS[axis]:
                ref = w.at[kind, g, c, :, y, xh, xl]
                copies.append(links.copy("mid%d" % g, len(copies), ref, ref, peer(axis, k)))
        return copies

    depths = (pl.ds(0, 4), pl.ds(4, 4))

    def middle_p():
        copies = []
        for depth, axis in zip(depths, "yx"):
            for k in SHIFTS[axis]:
                ref = w.at[0, 4, c, depth, y, xh, xl]
                copies.append(links.copy("midp", len(copies), ref, ref, peer(axis, k)))
        return copies

    def rank_lines(p, at):
        if p == 0:
            return w.at[0, 4, c, depths[0], :, at // 2, lax.rem(at, 2)]
        return w.at[0, 4, c, depths[1], at]

    def along_x(slot, at):
        return w.at[0, slot, c, :, :, at // 2, lax.rem(at, 2)]

    def along_y(slot, at):
        return w.at[1, slot, c, :, at]

    def bulk(g):
        copies = []
        for i, k in enumerate(SHIFTS["x"]):
            ref = along_x(g, x)
            copies.append(links.copy("bulk", g * 6 + i, ref, ref, peer("x", k)))
        for i, k in enumerate(SHIFTS["y"]):
            ref = along_y(g, y)
            copies.append(links.copy("bulk", g * 6 + 3 + i, ref, ref, peer("y", k)))
        return copies

    def bulk_p():
        copies = []
        for p, axis in enumerate("xy"):
            ref = rank_lines(p, where[axis])
            for k in SHIFTS[axis]:
                copies.append(links.copy("bulk_p", len(copies), ref, ref, peer(axis, k)))
        return copies

    def across(g):
        refs = [along_x(g, x), along_y(g, y)]
        refs += [along_x(g, shifted(where, "x", -k)) for k in SHIFTS["x"]]
        refs += [along_y(g, shifted(where, "y", -k)) for k in SHIFTS["y"]]
        return [links.copy("across", g * 8 + i, r, r, sibling) for i, r in enumerate(refs)]

    def across_p():
        refs = [rank_lines(0, x), rank_lines(1, y)]
        for p, axis in enumerate("xy"):
            refs += [rank_lines(p, shifted(where, axis, -k)) for k in SHIFTS[axis]]
        return [links.copy("across_p", i, r, r, sibling) for i, r in enumerate(refs)]

    def open_bulk(g):
        start(bulk(g))
        start(across(g)[:2])

    def forward(g):
        for got, on in zip(bulk(g), across(g)[2:]):
            got.wait_recv()
            on.start()

    def across_last():
        refs = [w.at[:, 3, c, z]]
        refs += [w.at[:, 3, c, shifted(where, "z", -k)] for k in SHIFTS["z"]]
        return [links.copy("across", 24 + i, r, r, sibling) for i, r in enumerate(refs)]

    mids = [middle(g) for g in range(GROUPS - 1)]
    mid_rank = middle_p()
    received(z_first)
    start(mids[0])
    received(z_rank)
    start(mid_rank)
    received(x_last)
    start(y_last)
    received(mids[0])
    open_bulk(0)
    received(z_rest)
    start(mids[1])
    received(mid_rank)
    start(bulk_p())
    start(across_p()[:2])
    received(y_last)
    start(z_last)
    start(across_last()[:1])

    spread = lax.broadcasted_iota(jnp.int32, (RANK, 256), 1)
    source = lax.broadcasted_iota(jnp.int32, (RANK, 256), 0)
    diagonal = (spread & 15) == (lax.broadcasted_iota(jnp.int32, (RANK, 256), 0) & 15)
    own_rows = own_p[...].astype(BF16)
    for n in range(16):
        kk = n * 16 + (spread >> 4)
        pick = (source == ((kk & 127) * 2 + (kk >> 7))).astype(F32).astype(BF16)
        line = dot(own_rows, pick)
        for i in range(4):
            columns = slice(n % 8 * 256, n % 8 * 256 + 256)
            lhs[n // 8, i * 16 : (i + 1) * 16, columns] = jnp.where(
                diagonal[:16], line[i : i + 1, :], F32(0.0)
            ).astype(BF16)

    forward(0)
    received(mids[1])
    open_bulk(1)
    start(mids[2])

    lane = lax.broadcasted_iota(jnp.int32, (1, 128), 1)
    firsts = (lane < 64).astype(F32).astype(BF16)
    masks = (firsts, 1 - firsts)

    def weight(slot, low_x, core):
        halves = [w[a, slot, core, :, :, :, low_x].reshape(WIDTH, 128) for a in range(2)]
        return jnp.concatenate(halves, axis=1)

    def project(g):
        for src, low_x, core, out in (
            (normed, 0, 0, q_s), (normed, 0, 1, k_s), (normed, 1, 0, v_s), (gout_ref, 1, 1, gh_s)
        ):
            res = dot(src[...], weight(g, low_x, core))
            out[0] = res[:, :128].astype(out.dtype)
            out[1] = res[:, 128:].astype(out.dtype)

    def project_rank():
        both = [w[0, 4, core, :, :, :, 0].reshape(WIDTH, 128) for core in range(2)]
        proj = jnp.concatenate(both, axis=1)
        for src, out in ((normed, np_t), (gout_ref, gp_t)):
            high, rest = split(dot(src[...], proj).T)
            out[:, :TOK] = high
            out[:, TOK:] = rest

    def core_copy(g):
        return links.copy("core", g, low_s.at[g, 1 - c], r0.at[g], sibling)

    def sum1(g):
        return [
            links.copy("sum1", g * 3 + i, s1.at[g, i], v1.at[g, i], peer("x", k))
            for i, k in enumerate(SHIFTS["x"])
        ]

    def sum2(g):
        return [
            links.copy(
                "sum2", g * 3 + i, acc.at[g, shifted(where, "y", k)], v2.at[g, i], peer("y", k)
            )
            for i, k in enumerate(SHIFTS["y"])
        ]

    def stage_one(g):
        core_copy(g).wait_recv()
        copies = sum1(g)
        for i, k in enumerate(SHIFTS["x"]):
            to = shifted(where, "x", k)
            value = low_s[g, c, to] + r0[g, to]
            s1[g, i] = value.reshape(32, 4 * UNIT).astype(BF16)
            copies[i].start()
        acc[g] = low_s[g, c, x] + r0[g, x]

    def stage_two(g):
        received(sum1(g))
        total = (v1[g, 0].astype(F32) + v1[g, 1].astype(F32)) + v1[g, 2].astype(F32)
        acc[g] = acc[g] + total.reshape(NY, 8, 4 * UNIT)
        start(sum2(g))

    def stage_three(g):
        received(sum2(g))
        total = acc[g, y] + ((v2[g, 0] + v2[g, 1]) + v2[g, 2])
        h = g // 2
        for block in range(4):
            columns = pl.ds(
                pl.multiple_of(block * 2 * UNIT + lax.rem(g, 2) * UNIT, UNIT), UNIT
            )
            for i in range(NZ):
                rows[h, i, :, columns] = total[i : i + 1, block * UNIT : (block + 1) * UNIT]

    def sum3(h):
        return [
            links.copy(
                "sum3", h * 7 + i, rows.at[h, shifted(where, "z", k)], v3.at[h, i], peer("z", k)
            )
            for i, k in enumerate(SHIFTS["z"])
        ]

    def dir_z(h):
        own = tiles.at[h, c, z, y, x]
        return [
            links.copy("dir_z", h * 7 + i, own, own, peer("z", k))
            for i, k in enumerate(SHIFTS["z"])
        ]

    def summed(h):
        received(sum3(h))
        low = rows[h, z]
        for i in range(NZ - 1):
            low = low + v3[h, i]
        for block in range(4):
            columns = slice(block * WIDTH + h * 512, block * WIDTH + h * 512 + 512)
            part = low[:, block * 512 : (block + 1) * 512]
            low_out[:, columns] = part
            _, _, direction = adam(part, first_ref[:, columns], second_ref[:, columns])
            for a in range(4):
                dir_rows[block * 4 + a : block * 4 + a + 1, :] = direction[
                    :, a * 128 : (a + 1) * 128
                ]
        tiles[h, c, z, y, x] = dir_rows[...].astype(BF16)
        start(dir_z(h))

    paths = ((pl.ds(0, 4), "y", "x"), (pl.ds(4, 4), "x", "y"))

    def dir_mid(h):
        copies = []
        for depth, axis, _ in paths:
            own = tiles.at[h, c, depth, y, x]
            for k in SHIFTS[axis]:
                copies.append(
                    links.copy("dir_mid", h * 6 + len(copies), own, own, peer(axis, k))
                )
        return copies

    def lines(h, p, at):
        depth = paths[p][0]
        return tiles.at[h, c, depth, :, at] if p == 0 else tiles.at[h, c, depth, at]

    def dir_last(h):
        copies = []
        for p, (_, _, axis) in enumerate(paths):
            own = lines(h, p, where[axis])
            for k in SHIFTS[axis]:
                copies.append(
                    links.copy("dir_last", h * 6 + len(copies), own, own, peer(axis, k))
                )
        return copies

    def dir_across(h):
        refs = [lines(h, p, where[paths[p][2]]) for p in range(2)]
        for p, (_, _, axis) in enumerate(paths):
            refs += [lines(h, p, shifted(where, axis, -k)) for k in SHIFTS[axis]]
        return [
            links.copy("dir_across", h * 8 + i, r, r, sibling) for i, r in enumerate(refs)
        ]

    def hand_on(h):
        for got, on in zip(dir_last(h), dir_across(h)[2:]):
            got.wait_recv()
            on.start()

    def step_of(h):
        columns = slice(h * 128, (h + 1) * 128)
        own = dot(lhs[c], tiles[h, c].reshape(RANK * 8, 128))
        received(dir_across(h))
        step_ref[:, columns] = own + dot(lhs[1 - c], tiles[h, 1 - c].reshape(RANK * 8, 128))

    @pl.loop(0, 2 * GROUPS)
    def _(t):
        g, i = t // 2, lax.rem(t, 2)

        @pl.when(i == 0)
        def _():
            @pl.when(g < GROUPS - 1)
            def _():
                received(across(g))

            @pl.when(g == GROUPS - 1)
            def _():
                received(across_last())

            project(g)

        @pl.when(i == 1)
        def _():
            @pl.when(g == 0)
            def _():
                received(mids[2])
                open_bulk(2)

        def between():
            @pl.when((i == 0) & (g > 0))
            def _():
                stage_one(g - 1)

            @pl.when((i == 1) & (g < GROUPS - 2))
            def _():
                forward(g + 1)

            @pl.when((i == 1) & (g == GROUPS - 2))
            def _():
                for got, on in zip(z_last, across_last()[1:]):
                    got.wait_recv()
                    on.start()

            @pl.when(t == 0)
            def _():
                for got, on in zip(bulk_p(), across_p()[2:]):
                    got.wait_recv()
                    on.start()

        gq_t, gk, gv, attended_t = attend_pair(
            q_s[i], k_s[i], v_s[i], gh_s[i], bias, masks, between
        )

        @pl.when(t == 0)
        def _():
            received(across_p())
            project_rank()

        gq_t = (gq_t * 0.125).astype(BF16)
        low_q = dot(np_t[...], jnp.concatenate([gq_t, gq_t], axis=1), ROWS)
        grads = jnp.concatenate([(gk * 0.125).astype(BF16), gv.astype(BF16)], axis=1)
        low_kv = dot(np_t[...], jnp.concatenate([grads, grads], axis=0))
        attended_t = attended_t.astype(BF16)
        outer = dot(gp_t[...], jnp.concatenate([attended_t, attended_t], axis=1), ROWS)
        values = (low_q, low_kv[:, :128], low_kv[:, 128:], outer)
        for block in range(4):
            columns = pl.ds(pl.multiple_of(block * UNIT + i * 128, 128), 128)
            low_s[g, :, :, :, :, columns] = values[block].reshape(NC, NX, NY, NZ, 128)

        @pl.when(i == 1)
        def _():
            core_copy(g).start()

            @pl.when(g > 0)
            def _():
                stage_two(g - 1)

        @pl.when((i == 0) & (g > 1))
        def _():
            stage_three(g - 2)

            @pl.when(g == 3)
            def _():
                start(sum3(0))

    stage_one(GROUPS - 1)
    stage_three(GROUPS - 2)
    summed(0)
    stage_two(GROUPS - 1)
    stage_three(GROUPS - 1)
    start(sum3(1))
    received(dir_z(0))
    start(dir_mid(0))
    received(dir_mid(0))
    start(dir_last(0))
    start(dir_across(0)[:2])
    summed(1)
    hand_on(0)
    received(dir_z(1))
    start(dir_mid(1))
    step_of(0)
    received(dir_mid(1))
    start(dir_last(1))
    start(dir_across(1)[:2])
    hand_on(1)
    step_of(1)

    sent(quad + z_first + z_rank + z_rest + mid_rank)
    for copies in mids:
        sent(copies)
    sent(bulk_p() + across_p())

    @pl.loop(0, GROUPS)
    def _(g):
        sent([core_copy(g)] + sum1(g) + sum2(g))

        @pl.when(g < GROUPS - 1)
        def _():
            sent(bulk(g) + across(g))

    sent(x_last + y_last + z_last + across_last())

    for h in range(2):
        sent(sum3(h) + dir_z(h) + dir_mid(h) + dir_last(h) + dir_across(h))


def main(lengths, inputs, grad_out, gain, master, projector, first, second):
    vmem = pl.BlockSpec(memory_space=pltpu.VMEM)
    return pl.pallas_call(
        main_kernel,
        out_shape=(
            jax.ShapeDtypeStruct((64, 256), F32),
            jax.ShapeDtypeStruct((1, 4 * WIDTH), F32),
        ),
        in_specs=[pl.BlockSpec(memory_space=pltpu.SMEM)] + [vmem] * 7,
        out_specs=(vmem, vmem),
        scratch_shapes=[
            pltpu.VMEM((2, 5, NC, NZ, NY, 2, 2, 16, 128), BF16),
            pltpu.VMEM((4, 4, WIDTH), F32),
            pltpu.VMEM((4, 4, RANK), F32),
            pltpu.VMEM((4, RANK), F32),
            pltpu.VMEM((16, WIDTH), F32),
            pltpu.VMEM((16, RANK), F32),
            pltpu.VMEM((RANK, RANK), BF16),
            pltpu.VMEM((TOK, WIDTH), BF16),
            pltpu.VMEM((TOK, TOK), F32),
            pltpu.VMEM((RANK, 2 * TOK), BF16),
            pltpu.VMEM((RANK, 2 * TOK), BF16),
            pltpu.VMEM((2, TOK, 128), BF16),
            pltpu.VMEM((2, TOK, 128), BF16),
            pltpu.VMEM((2, TOK, 128), BF16),
            pltpu.VMEM((2, TOK, 128), F32),
            pltpu.VMEM((GROUPS, NC, NX, NY, NZ, 4 * UNIT), F32),
            pltpu.VMEM((GROUPS, NX, NY, NZ, 4 * UNIT), F32),
            pltpu.VMEM((GROUPS, 3, 32, 4 * UNIT), BF16),
            pltpu.VMEM((GROUPS, 3, 32, 4 * UNIT), BF16),
            pltpu.VMEM((GROUPS, NY, NZ, 4 * UNIT), F32),
            pltpu.VMEM((GROUPS, 3, NZ, 4 * UNIT), F32),
            pltpu.VMEM((2, NZ, 1, 2 * WIDTH), F32),
            pltpu.VMEM((2, NZ - 1, 1, 2 * WIDTH), F32),
            pltpu.VMEM((16, 128), F32),
            pltpu.VMEM((2, NC, NZ, NY, NX, 16, 128), BF16),
            pltpu.VMEM((NC, 64, 2 * WIDTH), BF16),
            pltpu.SemaphoreType.DMA((N_SEMS,)),
            pltpu.SemaphoreType.DMA((N_SEMS,)),
        ],
        compiler_params=pltpu.CompilerParams(
            collective_id=0, has_side_effects=True, vmem_limit_bytes=VMEM_LIMIT
        ),
        name="galore_step",
    )(lengths, inputs, grad_out, gain, master, projector, first, second)


def finish_kernel(
    step_ref, low_ref, first_ref, second_ref, master_ref, new_master, new_first, new_second
):
    first, second, _ = adam(low_ref[...], first_ref[...], second_ref[...])
    new_first[...] = first
    new_second[...] = second
    for a in range(16):
        for h in range(2):
            at = (a // 4) * WIDTH + h * 512 + (a % 4) * 128
            columns = slice(at, at + 128)
            for i in range(4):
                row = i * 16 + a
                new_master[i : i + 1, columns] = (
                    master_ref[i : i + 1, columns]
                    - learn_rate * galore_scale * step_ref[row : row + 1, h * 128 : h * 128 + 128]
                )


def finish(step, low, first, second, master):
    vmem = pl.BlockSpec(memory_space=pltpu.VMEM)
    return pl.pallas_call(
        finish_kernel,
        out_shape=(
            jax.ShapeDtypeStruct((4, 4 * WIDTH), F32),
            jax.ShapeDtypeStruct((1, 4 * WIDTH), F32),
            jax.ShapeDtypeStruct((1, 4 * WIDTH), F32),
        ),
        in_specs=[vmem] * 5,
        out_specs=(vmem, vmem, vmem),
        name="outputs",
    )(step, low, first, second, master)


def shards(
    inputs, grad_out, norm_gain, master, projector, moment_first, moment_second, doc_lengths
):
    step, low = main(
        doc_lengths, inputs, grad_out, norm_gain[None, :], master, projector,
        moment_first, moment_second,
    )
    return finish(step, low, moment_first, moment_second, master)


def solution(mesh):
    return jax.shard_map(
        shards,
        mesh=mesh,
        in_specs=(
            P("dp", None),
            P("dp", None),
            P(),
            P("dp", None),
            P("dp", None),
            P("dp", None),
            P("dp", None),
            P("dp", None),
        ),
        out_specs=(P("dp", None), P("dp", None), P("dp", None)),
        check_vma=False,
    )
```

```python
import jax
import jax.numpy as jnp
import numpy as np
from jax import lax
from jax.experimental import pallas as pl
from jax.experimental.pallas import tpu as pltpu
from jax.sharding import PartitionSpec as P

NZ, NY, NX, NC = 8, 4, 4, 2
SIZE = {"z": NZ, "y": NY, "x": NX}
SHIFTS = {"z": (4, 3, 5, 2, 6, 1, 7), "y": (2, 1, 3), "x": (2, 1, 3)}
GROUPS = 4
UNIT = 256
TOK = 384
WIDTH = 1024
RANK = 256
VMEM_LIMIT = 56 * 1024 * 1024

beta_one = 0.9
beta_two = 0.999
adam_eps = 1e-08
adam_step = 10.0
learn_rate = 0.01
galore_scale = 0.25
norm_eps = 1e-05

F32 = jnp.float32
BF16 = jnp.bfloat16
MESH = pl.DeviceIdType.MESH


def place():
    me = lax.axis_index("dp")
    c = lax.rem(me, NC)
    x = lax.rem(me // NC, NX)
    y = lax.rem(me // (NC * NX), NY)
    z = me // (NC * NX * NY)
    return {"z": z, "y": y, "x": x, "c": c}


def device_at(where, **moved):
    at = dict(where, **moved)
    return ((at["z"] * NY + at["y"]) * NX + at["x"]) * NC + at["c"]


def shifted(where, axis, by):
    n = SIZE[axis]
    return lax.rem(where[axis] + (by + n), n)


class Links:
    def __init__(self, send_sems, recv_sems):
        self.send_sems, self.recv_sems = send_sems, recv_sems
        self.bases = {}
        self.used = 0

    def reserve(self, name, count):
        self.bases[name] = self.used
        self.used += count

    def copy(self, name, i, src, dst, device):
        at = self.bases[name] + i
        return pltpu.make_async_remote_copy(
            src_ref=src,
            dst_ref=dst,
            send_sem=self.send_sems.at[at],
            recv_sem=self.recv_sems.at[at],
            device_id=(device,),
            device_id_type=MESH,
        )


N_SEMS = 272


def start(copies):
    for copy in copies:
        copy.start()


def received(copies):
    for copy in copies:
        copy.wait_recv()


def sent(copies):
    for copy in copies:
        copy.wait_send()


def greet(devices):
    barrier = pltpu.get_barrier_semaphore()
    for device in devices:
        pl.semaphore_signal(barrier, inc=1, device_id=(device,), device_id_type=MESH)
    pl.semaphore_wait(barrier, len(devices))


def dot(a, b, dims=((1,), (0,))):
    return lax.dot_general(a, b, (dims, ((), ())), preferred_element_type=F32)


ROWS = ((1,), (1,))
COLS = ((0,), (0,))


def split(value):
    high = value.astype(BF16)
    return high, (value - high.astype(F32)).astype(BF16)


def adam(low, first, second):
    new_first = beta_one * first + (1.0 - beta_one) * low
    new_second = beta_two * second + (1.0 - beta_two) * low * low
    direction = (
        new_first
        / (1.0 - beta_one**adam_step)
        / (jnp.sqrt(new_second / (1.0 - beta_two**adam_step)) + adam_eps)
    )
    return new_first, new_second, direction


def attend_pair(q, k, v, gh, bias_ref, masks, between):
    probs, highs = [], []
    left_v, right_v = [], []
    for mask in masks:
        s = dot(k, q * mask, ROWS) * 0.125 + bias_ref[...]
        e = jnp.exp(s - jnp.max(s, axis=0, keepdims=True))
        p = e * (1.0 / jnp.sum(e, axis=0, keepdims=True))
        probs.append(p)
    between()
    gh_high, gh_rest = split(gh)
    v_twice = jnp.concatenate([v, v], axis=1)
    grads, right_k, left_q = [], [], []
    for p, mask in zip(probs, masks):
        p_high, p_rest = split(p)
        gh_m, gh_r = gh_high * mask, gh_rest * mask
        gp = dot(v_twice, jnp.concatenate([gh_m, gh_r], axis=1), ROWS)
        gs = p * (gp - jnp.sum(p * gp, axis=0, keepdims=True))
        highs.append(p_high)
        left_v += [p_high, p_rest]
        right_v += [
            jnp.concatenate([gh_m, gh_r], axis=1),
            jnp.concatenate([gh_m, jnp.zeros_like(gh_m)], axis=1),
        ]
        grads += list(split(gs))
        right_k += [q * mask] * 2
        left_q += [k * mask] * 2
    gv = dot(jnp.concatenate(left_v, axis=1), jnp.concatenate(right_v, axis=0))
    gv = gv[:, :128] + gv[:, 128:]
    gk = dot(jnp.concatenate(grads, axis=1), jnp.concatenate(right_k, axis=0))
    gq_t = dot(jnp.concatenate(left_q, axis=0), jnp.concatenate(grads, axis=0), COLS)
    by_head = jnp.concatenate([v * mask for mask in masks], axis=0)
    a_t = dot(by_head, jnp.concatenate(highs, axis=0), COLS)
    return gq_t, gk, gv, a_t


def main_kernel(
    len_ref, in_ref, gout_ref, gain_ref, master_ref, proj_ref, first_ref, second_ref,
    step_ref, low_out,
    w, quad_w, quad_p, own_p, rows_w, rows_p, order, normed, bias, np_t, gp_t,
    q_s, k_s, v_s, gh_s, low_s, r0, s1, v1, acc, v2, rows, v3, dir_rows, tiles, lhs,
    send_sems, recv_sems
):
    where = place()
    c, x, y, z = where["c"], where["x"], where["y"], where["z"]
    xh, xl = x // 2, lax.rem(x, 2)
    flip = x + 1 - 2 * xl
    sibling = device_at(where, c=1 - c)
    links = Links(send_sems, recv_sems)
    for name, count in (
        ("quad", 6), ("z0", 7), ("zp", 7), ("z1", 7), ("midp", 6), ("mid1", 6), ("mid2", 6),
        ("x3", 3),
        ("y3", 3), ("z3", 7),
        ("bulk", 24), ("across", 32), ("bulkp", 6), ("acrossp", 8), ("mida", 6), ("bulka", 6), ("acrossa", 8),
        ("midb", 6), ("bulkb", 6), ("acrossb", 8), ("core", 4),
        ("sum1", 12), ("sum2", 12), ("sum3", 14), ("dir_z", 14), ("dir_mid", 12),
        ("dir_last", 12), ("dir_across", 16),
    ):
        links.reserve(name, count)

    def peer(axis, by):
        return device_at(where, **{axis: shifted(where, axis, by)})

    greet(
        [sibling, device_at(where, x=flip, c=1 - c)]
        + [peer(axis, k) for axis in "xyz" for k in SHIFTS[axis]]
    )

    own_p[...] = proj_ref[...].astype(F32)
    mine = xl * 2 + c
    quad = []
    for i, (dx, dc) in enumerate(((0, 1), (1, 0), (1, 1))):
        to_xl = 1 - xl if dx else xl
        to_c = 1 - c if dc else c
        to = device_at(where, x=xh * 2 + to_xl, c=to_c)
        columns = pl.ds(pl.multiple_of((to_xl * 2 + to_c) * WIDTH, WIDTH), WIDTH)
        quad.append(
            links.copy("quad", 2 * i, master_ref.at[:, columns], quad_w.at[mine], to)
        )
        quad.append(links.copy("quad", 2 * i + 1, own_p, quad_p.at[mine], to))
    start(quad)
    columns = pl.ds(pl.multiple_of(mine * WIDTH, WIDTH), WIDTH)
    quad_w[mine] = master_ref[:, columns]
    quad_p[mine] = own_p[...]

    source = lax.broadcasted_iota(jnp.int32, (RANK, RANK), 0)
    place_to = lax.broadcasted_iota(jnp.int32, (RANK, RANK), 1)
    natural = (
        (place_to & 7) * 32
        + ((place_to >> 3) & 3) * 8
        + ((place_to >> 5) & 3) * 2
        + (place_to >> 7)
    )
    order[...] = (source == natural).astype(F32).astype(BF16)

    received(quad)
    for i in range(4):
        rows_w[i * 4 : i * 4 + 4, :] = quad_w[i]
        rows_p[i * 4 : i * 4 + 4, :] = quad_p[i]
    ordered = dot(rows_p[...].astype(BF16), order[...])
    w[0, 4, c, z, y, xh, xl] = jnp.where(c == 0, ordered[:, :128], ordered[:, 128:]).astype(
        BF16
    )
    for pair in range(8):
        w[pair % 2, pair // 2, c, z, y, xh, xl] = rows_w[
            :, pair * 128 : (pair + 1) * 128
        ].astype(BF16)

    def first_step(name, slots, kinds):
        copies = []
        for i, k in enumerate(SHIFTS["z"]):
            ref = w.at[kinds, slots, c, z, y, xh, xl]
            copies.append(links.copy(name, i, ref, ref, peer("z", k)))
        return copies

    z_first = first_step("z0", pl.ds(0, 1), pl.ds(0, 2))
    z_rank = first_step("zp", pl.ds(4, 1), pl.ds(0, 1))
    z_rest = first_step("z1", pl.ds(1, 2), pl.ds(0, 2))

    def other_way(name, axis, ref):
        return [
            links.copy(name, i, ref, ref, peer(axis, k)) for i, k in enumerate(SHIFTS[axis])
        ]

    x_last = other_way("x3", "x", w.at[:, 3, c, z, y, xh, xl])
    y_last = other_way("y3", "y", w.at[:, 3, c, z, y])
    z_last = other_way("z3", "z", w.at[:, 3, c, z])
    start(z_first + z_rank + x_last + z_rest)

    values = in_ref[...].astype(F32)
    scale = lax.rsqrt(jnp.mean(values * values, axis=1, keepdims=True) + norm_eps)
    normed[...] = (values * scale * gain_ref[...]).astype(BF16)
    b0 = len_ref[0, 0]
    b1 = b0 + len_ref[0, 1]
    b2 = b1 + len_ref[0, 2]
    b3 = b2 + len_ref[0, 3]

    def segment(position):
        return sum((position >= b).astype(jnp.int32) for b in (b0, b1, b2, b3))

    key = lax.broadcasted_iota(jnp.int32, (TOK, 1), 0)
    query = lax.broadcasted_iota(jnp.int32, (1, TOK), 1)
    seen = (segment(key) == segment(query)) & (query >= key)
    bias[...] = jnp.where(seen, F32(0.0), F32(-1e30))
    def middle(g):
        copies = []
        for kind, axis in ((0, "y"), (1, "x")):
            for k in SHIFTS[axis]:
                ref = w.at[kind, g, c, :, y, xh, xl]
                copies.append(links.copy("mid%d" % g, len(copies), ref, ref, peer(axis, k)))
        return copies

    depths = (pl.ds(0, 4), pl.ds(4, 4))

    units = {"a": (0, 0), "b": (1, 0), "p": (0, 4)}

    def unit_lines(unit, p, at):
        kind, slot = units[unit]
        if p == 0:
            return w.at[kind, slot, c, depths[0], :, at // 2, lax.rem(at, 2)]
        return w.at[kind, slot, c, depths[1], at]

    def unit_middle(unit):
        kind, slot = units[unit]
        copies = []
        for depth, axis in zip(depths, "yx"):
            for k in SHIFTS[axis]:
                ref = w.at[kind, slot, c, depth, y, xh, xl]
                copies.append(links.copy("mid" + unit, len(copies), ref, ref, peer(axis, k)))
        return copies

    def unit_bulk(unit):
        copies = []
        for p, axis in enumerate("xy"):
            ref = unit_lines(unit, p, where[axis])
            for k in SHIFTS[axis]:
                copies.append(links.copy("bulk" + unit, len(copies), ref, ref, peer(axis, k)))
        return copies

    def unit_across(unit):
        refs = [unit_lines(unit, 0, x), unit_lines(unit, 1, y)]
        for p, axis in enumerate("xy"):
            refs += [unit_lines(unit, p, shifted(where, axis, -k)) for k in SHIFTS[axis]]
        return [links.copy("across" + unit, i, r, r, sibling) for i, r in enumerate(refs)]

    def open_unit(unit):
        start(unit_bulk(unit))
        start(unit_across(unit)[:2])

    def forward_unit(unit):
        for got, on in zip(unit_bulk(unit), unit_across(unit)[2:]):
            got.wait_recv()
            on.start()

    def along_x(slot, at):
        return w.at[0, slot, c, :, :, at // 2, lax.rem(at, 2)]

    def along_y(slot, at):
        return w.at[1, slot, c, :, at]

    def bulk(g):
        copies = []
        for i, k in enumerate(SHIFTS["x"]):
            ref = along_x(g, x)
            copies.append(links.copy("bulk", g * 6 + i, ref, ref, peer("x", k)))
        for i, k in enumerate(SHIFTS["y"]):
            ref = along_y(g, y)
            copies.append(links.copy("bulk", g * 6 + 3 + i, ref, ref, peer("y", k)))
        return copies

    def across(g):
        refs = [along_x(g, x), along_y(g, y)]
        refs += [along_x(g, shifted(where, "x", -k)) for k in SHIFTS["x"]]
        refs += [along_y(g, shifted(where, "y", -k)) for k in SHIFTS["y"]]
        return [links.copy("across", g * 8 + i, r, r, sibling) for i, r in enumerate(refs)]

    def open_bulk(g):
        start(bulk(g))
        start(across(g)[:2])

    def forward(g):
        for got, on in zip(bulk(g), across(g)[2:]):
            got.wait_recv()
            on.start()

    def across_last():
        refs = [w.at[:, 3, c, z]]
        refs += [w.at[:, 3, c, shifted(where, "z", -k)] for k in SHIFTS["z"]]
        return [links.copy("across", 24 + i, r, r, sibling) for i, r in enumerate(refs)]

    mids = {g: middle(g) for g in (1, 2)}
    unit_mids = {unit: unit_middle(unit) for unit in units}
    received(z_first)
    start(unit_mids["a"])
    start(unit_mids["b"])
    received(z_rank)
    start(unit_mids["p"])
    received(x_last)
    start(y_last)
    received(unit_mids["a"])
    open_unit("a")
    received(unit_mids["b"])
    open_unit("b")
    received(z_rest)
    start(mids[1])
    received(unit_mids["p"])
    open_unit("p")
    received(y_last)
    start(z_last)
    start(across_last()[:1])

    spread = lax.broadcasted_iota(jnp.int32, (RANK, 256), 1)
    source = lax.broadcasted_iota(jnp.int32, (RANK, 256), 0)
    diagonal = (spread & 15) == (lax.broadcasted_iota(jnp.int32, (RANK, 256), 0) & 15)
    own_rows = own_p[...].astype(BF16)
    for n in range(16):
        kk = n * 16 + (spread >> 4)
        pick = (source == ((kk & 127) * 2 + (kk >> 7))).astype(F32).astype(BF16)
        line = dot(own_rows, pick)
        for i in range(4):
            columns = slice(n % 8 * 256, n % 8 * 256 + 256)
            lhs[n // 8, i * 16 : (i + 1) * 16, columns] = jnp.where(
                diagonal[:16], line[i : i + 1, :], F32(0.0)
            ).astype(BF16)

    forward_unit("a")
    received(mids[1])
    open_bulk(1)
    start(mids[2])

    lane = lax.broadcasted_iota(jnp.int32, (1, 128), 1)
    firsts = (lane < 64).astype(F32).astype(BF16)
    masks = (firsts, 1 - firsts)

    def weight(slot, low_x, core):
        halves = [w[a, slot, core, :, :, :, low_x].reshape(WIDTH, 128) for a in range(2)]
        return jnp.concatenate(halves, axis=1)

    def project(g):
        for src, low_x, core, out in (
            (normed, 0, 0, q_s), (normed, 0, 1, k_s), (normed, 1, 0, v_s), (gout_ref, 1, 1, gh_s)
        ):
            res = dot(src[...], weight(g, low_x, core))
            out[0] = res[:, :128].astype(out.dtype)
            out[1] = res[:, 128:].astype(out.dtype)

    def project_unit(u):
        for src, low_x, core, out in (
            (normed, 0, 0, q_s), (normed, 0, 1, k_s), (normed, 1, 0, v_s), (gout_ref, 1, 1, gh_s)
        ):
            res = dot(src[...], w[u, 0, core, :, :, :, low_x].reshape(WIDTH, 128))
            out[u] = res.astype(out.dtype)

    def project_rank():
        both = [w[0, 4, core, :, :, :, 0].reshape(WIDTH, 128) for core in range(2)]
        proj = jnp.concatenate(both, axis=1)
        for src, out in ((normed, np_t), (gout_ref, gp_t)):
            high, rest = split(dot(src[...], proj).T)
            out[:, :TOK] = high
            out[:, TOK:] = rest

    def core_copy(g):
        return links.copy("core", g, low_s.at[g, 1 - c], r0.at[g], sibling)

    def sum1(g):
        return [
            links.copy("sum1", g * 3 + i, s1.at[g, i], v1.at[g, i], peer("x", k))
            for i, k in enumerate(SHIFTS["x"])
        ]

    def sum2(g):
        return [
            links.copy(
                "sum2", g * 3 + i, acc.at[g, shifted(where, "y", k)], v2.at[g, i], peer("y", k)
            )
            for i, k in enumerate(SHIFTS["y"])
        ]

    def stage_one(g):
        core_copy(g).wait_recv()
        copies = sum1(g)
        for i, k in enumerate(SHIFTS["x"]):
            to = shifted(where, "x", k)
            value = low_s[g, c, to] + r0[g, to]
            s1[g, i] = value.reshape(32, 4 * UNIT).astype(BF16)
            copies[i].start()
        acc[g] = low_s[g, c, x] + r0[g, x]

    def stage_two(g):
        received(sum1(g))
        total = (v1[g, 0].astype(F32) + v1[g, 1].astype(F32)) + v1[g, 2].astype(F32)
        acc[g] = acc[g] + total.reshape(NY, 8, 4 * UNIT)
        start(sum2(g))

    def stage_three(g):
        received(sum2(g))
        total = acc[g, y] + ((v2[g, 0] + v2[g, 1]) + v2[g, 2])
        h = g // 2
        for block in range(4):
            columns = pl.ds(
                pl.multiple_of(block * 2 * UNIT + lax.rem(g, 2) * UNIT, UNIT), UNIT
            )
            for i in range(NZ):
                rows[h, i, :, columns] = total[i : i + 1, block * UNIT : (block + 1) * UNIT]

    def sum3(h):
        return [
            links.copy(
                "sum3", h * 7 + i, rows.at[h, shifted(where, "z", k)], v3.at[h, i], peer("z", k)
            )
            for i, k in enumerate(SHIFTS["z"])
        ]

    def dir_z(h):
        own = tiles.at[h, c, z, y, x]
        return [
            links.copy("dir_z", h * 7 + i, own, own, peer("z", k))
            for i, k in enumerate(SHIFTS["z"])
        ]

    def summed(h):
        received(sum3(h))
        low = rows[h, z]
        for i in range(NZ - 1):
            low = low + v3[h, i]
        for block in range(4):
            columns = slice(block * WIDTH + h * 512, block * WIDTH + h * 512 + 512)
            part = low[:, block * 512 : (block + 1) * 512]
            low_out[:, columns] = part
            _, _, direction = adam(part, first_ref[:, columns], second_ref[:, columns])
            for a in range(4):
                dir_rows[block * 4 + a : block * 4 + a + 1, :] = direction[
                    :, a * 128 : (a + 1) * 128
                ]
        tiles[h, c, z, y, x] = dir_rows[...].astype(BF16)
        start(dir_z(h))

    paths = ((pl.ds(0, 4), "y", "x"), (pl.ds(4, 4), "x", "y"))

    def dir_mid(h):
        copies = []
        for depth, axis, _ in paths:
            own = tiles.at[h, c, depth, y, x]
            for k in SHIFTS[axis]:
                copies.append(
                    links.copy("dir_mid", h * 6 + len(copies), own, own, peer(axis, k))
                )
        return copies

    def lines(h, p, at):
        depth = paths[p][0]
        return tiles.at[h, c, depth, :, at] if p == 0 else tiles.at[h, c, depth, at]

    def dir_last(h):
        copies = []
        for p, (_, _, axis) in enumerate(paths):
            own = lines(h, p, where[axis])
            for k in SHIFTS[axis]:
                copies.append(
                    links.copy("dir_last", h * 6 + len(copies), own, own, peer(axis, k))
                )
        return copies

    def dir_across(h):
        refs = [lines(h, p, where[paths[p][2]]) for p in range(2)]
        for p, (_, _, axis) in enumerate(paths):
            refs += [lines(h, p, shifted(where, axis, -k)) for k in SHIFTS[axis]]
        return [
            links.copy("dir_across", h * 8 + i, r, r, sibling) for i, r in enumerate(refs)
        ]

    def hand_on(h):
        for got, on in zip(dir_last(h), dir_across(h)[2:]):
            got.wait_recv()
            on.start()

    def step_of(h):
        columns = slice(h * 128, (h + 1) * 128)
        own = dot(lhs[c], tiles[h, c].reshape(RANK * 8, 128))
        received(dir_across(h))
        step_ref[:, columns] = own + dot(lhs[1 - c], tiles[h, 1 - c].reshape(RANK * 8, 128))

    @pl.loop(0, 2 * GROUPS)
    def _(t):
        g, i = t // 2, lax.rem(t, 2)

        @pl.when(i == 0)
        def _():
            @pl.when(g == 0)
            def _():
                received(unit_across("a"))
                project_unit(0)

            @pl.when((g > 0) & (g < GROUPS - 1))
            def _():
                received(across(g))

            @pl.when(g == GROUPS - 1)
            def _():
                received(across_last())

            @pl.when(g > 0)
            def _():
                project(g)

        @pl.when(i == 1)
        def _():
            @pl.when(g == 0)
            def _():
                received(unit_across("b"))
                project_unit(1)
                received(mids[2])
                open_bulk(2)

        def between():
            @pl.when((i == 0) & (g > 0))
            def _():
                stage_one(g - 1)

            @pl.when((i == 1) & (g < GROUPS - 2))
            def _():
                forward(g + 1)

            @pl.when((i == 1) & (g == GROUPS - 2))
            def _():
                for got, on in zip(z_last, across_last()[1:]):
                    got.wait_recv()
                    on.start()

            @pl.when(t == 0)
            def _():
                forward_unit("b")
                forward_unit("p")

        gq_t, gk, gv, attended_t = attend_pair(
            q_s[i], k_s[i], v_s[i], gh_s[i], bias, masks, between
        )

        @pl.when(t == 0)
        def _():
            received(unit_across("p"))
            project_rank()

        gq_t = (gq_t * 0.125).astype(BF16)
        low_q = dot(np_t[...], jnp.concatenate([gq_t, gq_t], axis=1), ROWS)
        grads = jnp.concatenate([(gk * 0.125).astype(BF16), gv.astype(BF16)], axis=1)
        low_kv = dot(np_t[...], jnp.concatenate([grads, grads], axis=0))
        attended_t = attended_t.astype(BF16)
        outer = dot(gp_t[...], jnp.concatenate([attended_t, attended_t], axis=1), ROWS)
        values = (low_q, low_kv[:, :128], low_kv[:, 128:], outer)
        for block in range(4):
            columns = pl.ds(pl.multiple_of(block * UNIT + i * 128, 128), 128)
            low_s[g, :, :, :, :, columns] = values[block].reshape(NC, NX, NY, NZ, 128)

        @pl.when(i == 1)
        def _():
            core_copy(g).start()

            @pl.when(g > 0)
            def _():
                stage_two(g - 1)

        @pl.when((i == 0) & (g > 1))
        def _():
            stage_three(g - 2)

            @pl.when(g == 3)
            def _():
                start(sum3(0))

    stage_one(GROUPS - 1)
    stage_three(GROUPS - 2)
    summed(0)
    stage_two(GROUPS - 1)
    stage_three(GROUPS - 1)
    start(sum3(1))
    received(dir_z(0))
    start(dir_mid(0))
    received(dir_mid(0))
    start(dir_last(0))
    start(dir_across(0)[:2])
    summed(1)
    hand_on(0)
    received(dir_z(1))
    start(dir_mid(1))
    step_of(0)
    received(dir_mid(1))
    start(dir_last(1))
    start(dir_across(1)[:2])
    hand_on(1)
    step_of(1)

    sent(quad + z_first + z_rank + z_rest + mids[1] + mids[2])
    for unit in units:
        sent(unit_mids[unit] + unit_bulk(unit) + unit_across(unit))

    @pl.loop(0, GROUPS)
    def _(g):
        sent([core_copy(g)] + sum1(g) + sum2(g))

        @pl.when((g > 0) & (g < GROUPS - 1))
        def _():
            sent(bulk(g) + across(g))

    sent(x_last + y_last + z_last + across_last())

    for h in range(2):
        sent(sum3(h) + dir_z(h) + dir_mid(h) + dir_last(h) + dir_across(h))


def main(lengths, inputs, grad_out, gain, master, projector, first, second):
    vmem = pl.BlockSpec(memory_space=pltpu.VMEM)
    return pl.pallas_call(
        main_kernel,
        out_shape=(
            jax.ShapeDtypeStruct((64, 256), F32),
            jax.ShapeDtypeStruct((1, 4 * WIDTH), F32),
        ),
        in_specs=[pl.BlockSpec(memory_space=pltpu.SMEM)] + [vmem] * 7,
        out_specs=(vmem, vmem),
        scratch_shapes=[
            pltpu.VMEM((2, 5, NC, NZ, NY, 2, 2, 16, 128), BF16),
            pltpu.VMEM((4, 4, WIDTH), F32),
            pltpu.VMEM((4, 4, RANK), F32),
            pltpu.VMEM((4, RANK), F32),
            pltpu.VMEM((16, WIDTH), F32),
            pltpu.VMEM((16, RANK), F32),
            pltpu.VMEM((RANK, RANK), BF16),
            pltpu.VMEM((TOK, WIDTH), BF16),
            pltpu.VMEM((TOK, TOK), F32),
            pltpu.VMEM((RANK, 2 * TOK), BF16),
            pltpu.VMEM((RANK, 2 * TOK), BF16),
            pltpu.VMEM((2, TOK, 128), BF16),
            pltpu.VMEM((2, TOK, 128), BF16),
            pltpu.VMEM((2, TOK, 128), BF16),
            pltpu.VMEM((2, TOK, 128), F32),
            pltpu.VMEM((GROUPS, NC, NX, NY, NZ, 4 * UNIT), F32),
            pltpu.VMEM((GROUPS, NX, NY, NZ, 4 * UNIT), F32),
            pltpu.VMEM((GROUPS, 3, 32, 4 * UNIT), BF16),
            pltpu.VMEM((GROUPS, 3, 32, 4 * UNIT), BF16),
            pltpu.VMEM((GROUPS, NY, NZ, 4 * UNIT), F32),
            pltpu.VMEM((GROUPS, 3, NZ, 4 * UNIT), F32),
            pltpu.VMEM((2, NZ, 1, 2 * WIDTH), F32),
            pltpu.VMEM((2, NZ - 1, 1, 2 * WIDTH), F32),
            pltpu.VMEM((16, 128), F32),
            pltpu.VMEM((2, NC, NZ, NY, NX, 16, 128), BF16),
            pltpu.VMEM((NC, 64, 2 * WIDTH), BF16),
            pltpu.SemaphoreType.DMA((N_SEMS,)),
            pltpu.SemaphoreType.DMA((N_SEMS,)),
        ],
        compiler_params=pltpu.CompilerParams(
            collective_id=0, has_side_effects=True, vmem_limit_bytes=VMEM_LIMIT
        ),
        name="galore_step",
    )(lengths, inputs, grad_out, gain, master, projector, first, second)


def finish_kernel(
    step_ref, low_ref, first_ref, second_ref, master_ref, new_master, new_first, new_second
):
    first, second, _ = adam(low_ref[...], first_ref[...], second_ref[...])
    new_first[...] = first
    new_second[...] = second
    for a in range(16):
        for h in range(2):
            at = (a // 4) * WIDTH + h * 512 + (a % 4) * 128
            columns = slice(at, at + 128)
            for i in range(4):
                row = i * 16 + a
                new_master[i : i + 1, columns] = (
                    master_ref[i : i + 1, columns]
                    - learn_rate * galore_scale * step_ref[row : row + 1, h * 128 : h * 128 + 128]
                )


def finish(step, low, first, second, master):
    vmem = pl.BlockSpec(memory_space=pltpu.VMEM)
    return pl.pallas_call(
        finish_kernel,
        out_shape=(
            jax.ShapeDtypeStruct((4, 4 * WIDTH), F32),
            jax.ShapeDtypeStruct((1, 4 * WIDTH), F32),
            jax.ShapeDtypeStruct((1, 4 * WIDTH), F32),
        ),
        in_specs=[vmem] * 5,
        out_specs=(vmem, vmem, vmem),
        name="outputs",
    )(step, low, first, second, master)


def shards(
    inputs, grad_out, norm_gain, master, projector, moment_first, moment_second, doc_lengths
):
    step, low = main(
        doc_lengths, inputs, grad_out, norm_gain[None, :], master, projector,
        moment_first, moment_second,
    )
    return finish(step, low, moment_first, moment_second, master)


def solution(mesh):
    return jax.shard_map(
        shards,
        mesh=mesh,
        in_specs=(
            P("dp", None),
            P("dp", None),
            P(),
            P("dp", None),
            P("dp", None),
            P("dp", None),
            P("dp", None),
            P("dp", None),
        ),
        out_specs=(P("dp", None), P("dp", None), P("dp", None)),
        check_vma=False,
    )
```

```python
import jax
import jax.numpy as jnp
import numpy as np
from jax import lax
from jax.experimental import pallas as pl
from jax.experimental.pallas import tpu as pltpu
from jax.sharding import PartitionSpec as P

NZ, NY, NX, NC = 8, 4, 4, 2
SIZE = {"z": NZ, "y": NY, "x": NX}
SHIFTS = {"z": (4, 3, 5, 2, 6, 1, 7), "y": (2, 1, 3), "x": (2, 1, 3)}
GROUPS = 4
UNIT = 256
TOK = 384
WIDTH = 1024
RANK = 256
VMEM_LIMIT = 56 * 1024 * 1024

beta_one = 0.9
beta_two = 0.999
adam_eps = 1e-08
adam_step = 10.0
learn_rate = 0.01
galore_scale = 0.25
norm_eps = 1e-05

F32 = jnp.float32
BF16 = jnp.bfloat16
MESH = pl.DeviceIdType.MESH


def place():
    me = lax.axis_index("dp")
    c = lax.rem(me, NC)
    x = lax.rem(me // NC, NX)
    y = lax.rem(me // (NC * NX), NY)
    z = me // (NC * NX * NY)
    return {"z": z, "y": y, "x": x, "c": c}


def device_at(where, **moved):
    at = dict(where, **moved)
    return ((at["z"] * NY + at["y"]) * NX + at["x"]) * NC + at["c"]


def shifted(where, axis, by):
    n = SIZE[axis]
    return lax.rem(where[axis] + (by + n), n)


class Links:
    def __init__(self, send_sems, recv_sems):
        self.send_sems, self.recv_sems = send_sems, recv_sems
        self.bases = {}
        self.used = 0

    def reserve(self, name, count):
        self.bases[name] = self.used
        self.used += count

    def copy(self, name, i, src, dst, device):
        at = self.bases[name] + i
        return pltpu.make_async_remote_copy(
            src_ref=src,
            dst_ref=dst,
            send_sem=self.send_sems.at[at],
            recv_sem=self.recv_sems.at[at],
            device_id=(device,),
            device_id_type=MESH,
        )


N_SEMS = 232


def start(copies):
    for copy in copies:
        copy.start()


def received(copies):
    for copy in copies:
        copy.wait_recv()


def sent(copies):
    for copy in copies:
        copy.wait_send()


def greet(devices):
    barrier = pltpu.get_barrier_semaphore()
    for device in devices:
        pl.semaphore_signal(barrier, inc=1, device_id=(device,), device_id_type=MESH)
    pl.semaphore_wait(barrier, len(devices))


def dot(a, b, dims=((1,), (0,))):
    return lax.dot_general(a, b, (dims, ((), ())), preferred_element_type=F32)


ROWS = ((1,), (1,))
COLS = ((0,), (0,))


def split(value):
    high = value.astype(BF16)
    return high, (value - high.astype(F32)).astype(BF16)


def adam(low, first, second):
    new_first = beta_one * first + (1.0 - beta_one) * low
    new_second = beta_two * second + (1.0 - beta_two) * low * low
    direction = (
        new_first
        / (1.0 - beta_one**adam_step)
        / (jnp.sqrt(new_second / (1.0 - beta_two**adam_step)) + adam_eps)
    )
    return new_first, new_second, direction


def attend_pair(q, k, v, gh, bias_ref, masks, between):
    probs, highs = [], []
    left_v, right_v = [], []
    for mask in masks:
        s = dot(k, q * mask, ROWS) * 0.125 + bias_ref[...]
        e = jnp.exp(s - jnp.max(s, axis=0, keepdims=True))
        p = e * (1.0 / jnp.sum(e, axis=0, keepdims=True))
        probs.append(p)
    between()
    gh_high, gh_rest = split(gh)
    v_twice = jnp.concatenate([v, v], axis=1)
    grads, right_k, left_q = [], [], []
    for p, mask in zip(probs, masks):
        p_high, p_rest = split(p)
        gh_m, gh_r = gh_high * mask, gh_rest * mask
        gp = dot(v_twice, jnp.concatenate([gh_m, gh_r], axis=1), ROWS)
        gs = p * (gp - jnp.sum(p * gp, axis=0, keepdims=True))
        highs.append(p_high)
        left_v += [p_high, p_rest]
        right_v += [
            jnp.concatenate([gh_m, gh_r], axis=1),
            jnp.concatenate([gh_m, jnp.zeros_like(gh_m)], axis=1),
        ]
        grads += list(split(gs))
        right_k += [q * mask] * 2
        left_q += [k * mask] * 2
    gv = dot(jnp.concatenate(left_v, axis=1), jnp.concatenate(right_v, axis=0))
    gv = gv[:, :128] + gv[:, 128:]
    gk = dot(jnp.concatenate(grads, axis=1), jnp.concatenate(right_k, axis=0))
    gq_t = dot(jnp.concatenate(left_q, axis=0), jnp.concatenate(grads, axis=0), COLS)
    by_head = jnp.concatenate([v * mask for mask in masks], axis=0)
    a_t = dot(by_head, jnp.concatenate(highs, axis=0), COLS)
    return gq_t, gk, gv, a_t


def main_kernel(
    len_ref, in_ref, gout_ref, gain_ref, master_ref, proj_ref, first_ref, second_ref,
    step_ref, low_out,
    w, quad_w, quad_p, own_p, rows_w, rows_p, order, normed, bias, np_t, gp_t,
    q_s, k_s, v_s, gh_s, low_s, r0, s1, v1, acc, v2, rows, v3, dir_rows, tiles, lhs,
    send_sems, recv_sems
):
    where = place()
    c, x, y, z = where["c"], where["x"], where["y"], where["z"]
    xh, xl = x // 2, lax.rem(x, 2)
    flip = x + 1 - 2 * xl
    sibling = device_at(where, c=1 - c)
    links = Links(send_sems, recv_sems)
    for name, count in (
        ("quad", 6), ("z0", 7), ("zp", 7), ("z1", 7), ("mid0", 6), ("midp", 6), ("mid1", 6), ("mid2", 6),
        ("x3", 3),
        ("y3", 3), ("z3", 7),
        ("bulk", 24), ("across", 32), ("bulk_p", 6), ("across_p", 8), ("core", 4),
        ("sum1", 12), ("sum2", 12), ("sum3", 14), ("dir_z", 14), ("dir_mid", 12),
        ("dir_last", 12), ("dir_across", 16),
    ):
        links.reserve(name, count)

    def peer(axis, by):
        return device_at(where, **{axis: shifted(where, axis, by)})

    greet(
        [sibling, device_at(where, x=flip, c=1 - c)]
        + [peer(axis, k) for axis in "xyz" for k in SHIFTS[axis]]
    )

    own_p[...] = proj_ref[...].astype(F32)
    mine = xl * 2 + c
    quad = []
    for i, (dx, dc) in enumerate(((0, 1), (1, 0), (1, 1))):
        to_xl = 1 - xl if dx else xl
        to_c = 1 - c if dc else c
        to = device_at(where, x=xh * 2 + to_xl, c=to_c)
        columns = pl.ds(pl.multiple_of((to_xl * 2 + to_c) * WIDTH, WIDTH), WIDTH)
        quad.append(
            links.copy("quad", 2 * i, master_ref.at[:, columns], quad_w.at[mine], to)
        )
        quad.append(links.copy("quad", 2 * i + 1, own_p, quad_p.at[mine], to))
    start(quad)
    columns = pl.ds(pl.multiple_of(mine * WIDTH, WIDTH), WIDTH)
    quad_w[mine] = master_ref[:, columns]
    quad_p[mine] = own_p[...]

    source = lax.broadcasted_iota(jnp.int32, (RANK, RANK), 0)
    place_to = lax.broadcasted_iota(jnp.int32, (RANK, RANK), 1)
    natural = (
        (place_to & 7) * 32
        + ((place_to >> 3) & 3) * 8
        + ((place_to >> 5) & 3) * 2
        + (place_to >> 7)
    )
    order[...] = (source == natural).astype(F32).astype(BF16)

    received(quad)
    for i in range(4):
        rows_w[i * 4 : i * 4 + 4, :] = quad_w[i]
        rows_p[i * 4 : i * 4 + 4, :] = quad_p[i]
    ordered = dot(rows_p[...].astype(BF16), order[...])
    w[0, 4, c, z, y, xh, xl] = jnp.where(c == 0, ordered[:, :128], ordered[:, 128:]).astype(
        BF16
    )
    for pair in range(8):
        w[pair % 2, pair // 2, c, z, y, xh, xl] = rows_w[
            :, pair * 128 : (pair + 1) * 128
        ].astype(BF16)

    def first_step(name, slots, kinds):
        copies = []
        for i, k in enumerate(SHIFTS["z"]):
            ref = w.at[kinds, slots, c, z, y, xh, xl]
            copies.append(links.copy(name, i, ref, ref, peer("z", k)))
        return copies

    z_first = first_step("z0", pl.ds(0, 1), pl.ds(0, 2))
    z_rank = first_step("zp", pl.ds(4, 1), pl.ds(0, 1))
    z_rest = first_step("z1", pl.ds(1, 2), pl.ds(0, 2))

    def other_way(name, axis, ref):
        return [
            links.copy(name, i, ref, ref, peer(axis, k)) for i, k in enumerate(SHIFTS[axis])
        ]

    x_last = other_way("x3", "x", w.at[:, 3, c, z, y, xh, xl])
    y_last = other_way("y3", "y", w.at[:, 3, c, z, y])
    z_last = other_way("z3", "z", w.at[:, 3, c, z])
    start(z_first + z_rank + x_last + z_rest)

    values = in_ref[...].astype(F32)
    scale = lax.rsqrt(jnp.mean(values * values, axis=1, keepdims=True) + norm_eps)
    normed[...] = (values * scale * gain_ref[...]).astype(BF16)
    b0 = len_ref[0, 0]
    b1 = b0 + len_ref[0, 1]
    b2 = b1 + len_ref[0, 2]
    b3 = b2 + len_ref[0, 3]

    def segment(position):
        return sum((position >= b).astype(jnp.int32) for b in (b0, b1, b2, b3))

    key = lax.broadcasted_iota(jnp.int32, (TOK, 1), 0)
    query = lax.broadcasted_iota(jnp.int32, (1, TOK), 1)
    seen = (segment(key) == segment(query)) & (query >= key)
    bias[...] = jnp.where(seen, F32(0.0), F32(-1e30))
    def middle(g):
        copies = []
        for kind, axis in ((0, "y"), (1, "x")):
            for k in SHIFTS[axis]:
                ref = w.at[kind, g, c, :, y, xh, xl]
                copies.append(links.copy("mid%d" % g, len(copies), ref, ref, peer(axis, k)))
        return copies

    depths = (pl.ds(0, 4), pl.ds(4, 4))

    def middle_p():
        copies = []
        for depth, axis in zip(depths, "yx"):
            for k in SHIFTS[axis]:
                ref = w.at[0, 4, c, depth, y, xh, xl]
                copies.append(links.copy("midp", len(copies), ref, ref, peer(axis, k)))
        return copies

    def rank_lines(p, at):
        if p == 0:
            return w.at[0, 4, c, depths[0], :, at // 2, lax.rem(at, 2)]
        return w.at[0, 4, c, depths[1], at]

    def along_x(slot, at):
        return w.at[0, slot, c, :, :, at // 2, lax.rem(at, 2)]

    def along_y(slot, at):
        return w.at[1, slot, c, :, at]

    def bulk(g):
        copies = []
        for i, k in enumerate(SHIFTS["x"]):
            ref = along_x(g, x)
            copies.append(links.copy("bulk", g * 6 + i, ref, ref, peer("x", k)))
        for i, k in enumerate(SHIFTS["y"]):
            ref = along_y(g, y)
            copies.append(links.copy("bulk", g * 6 + 3 + i, ref, ref, peer("y", k)))
        return copies

    def bulk_p():
        copies = []
        for p, axis in enumerate("xy"):
            ref = rank_lines(p, where[axis])
            for k in SHIFTS[axis]:
                copies.append(links.copy("bulk_p", len(copies), ref, ref, peer(axis, k)))
        return copies

    def across(g):
        refs = [along_x(g, x), along_y(g, y)]
        refs += [along_x(g, shifted(where, "x", -k)) for k in SHIFTS["x"]]
        refs += [along_y(g, shifted(where, "y", -k)) for k in SHIFTS["y"]]
        return [links.copy("across", g * 8 + i, r, r, sibling) for i, r in enumerate(refs)]

    def across_p():
        refs = [rank_lines(0, x), rank_lines(1, y)]
        for p, axis in enumerate("xy"):
            refs += [rank_lines(p, shifted(where, axis, -k)) for k in SHIFTS[axis]]
        return [links.copy("across_p", i, r, r, sibling) for i, r in enumerate(refs)]

    def open_bulk(g):
        start(bulk(g))
        start(across(g)[:2])

    def forward(g):
        for got, on in zip(bulk(g), across(g)[2:]):
            got.wait_recv()
            on.start()

    def across_last():
        refs = [w.at[:, 3, c, z]]
        refs += [w.at[:, 3, c, shifted(where, "z", -k)] for k in SHIFTS["z"]]
        return [links.copy("across", 24 + i, r, r, sibling) for i, r in enumerate(refs)]

    mids = [middle(g) for g in range(GROUPS - 1)]
    mid_rank = middle_p()
    received(z_first)
    start(mids[0])
    received(z_rank)
    start(mid_rank)
    received(x_last)
    start(y_last)
    received(mids[0])
    open_bulk(0)
    received(z_rest)
    start(mids[1])
    received(mid_rank)
    start(bulk_p())
    start(across_p()[:2])
    received(y_last)
    start(z_last)
    start(across_last()[:1])

    spread = lax.broadcasted_iota(jnp.int32, (RANK, 256), 1)
    source = lax.broadcasted_iota(jnp.int32, (RANK, 256), 0)
    diagonal = (spread & 15) == (lax.broadcasted_iota(jnp.int32, (RANK, 256), 0) & 15)
    own_rows = own_p[...].astype(BF16)
    for n in range(16):
        kk = n * 16 + (spread >> 4)
        pick = (source == ((kk & 127) * 2 + (kk >> 7))).astype(F32).astype(BF16)
        line = dot(own_rows, pick)
        for i in range(4):
            columns = slice(n % 8 * 256, n % 8 * 256 + 256)
            lhs[n // 8, i * 16 : (i + 1) * 16, columns] = jnp.where(
                diagonal[:16], line[i : i + 1, :], F32(0.0)
            ).astype(BF16)

    forward(0)
    received(mids[1])
    open_bulk(1)
    start(mids[2])

    lane = lax.broadcasted_iota(jnp.int32, (1, 128), 1)
    firsts = (lane < 64).astype(F32).astype(BF16)
    masks = (firsts, 1 - firsts)

    def weight(slot, low_x, core):
        halves = [w[a, slot, core, :, :, :, low_x].reshape(WIDTH, 128) for a in range(2)]
        return jnp.concatenate(halves, axis=1)

    def project(g):
        for src, low_x, core, out in (
            (normed, 0, 0, q_s), (normed, 0, 1, k_s), (normed, 1, 0, v_s), (gout_ref, 1, 1, gh_s)
        ):
            res = dot(src[...], weight(g, low_x, core))
            out[0] = res[:, :128].astype(out.dtype)
            out[1] = res[:, 128:].astype(out.dtype)

    def project_rank():
        both = [w[0, 4, core, :, :, :, 0].reshape(WIDTH, 128) for core in range(2)]
        proj = jnp.concatenate(both, axis=1)
        for src, out in ((normed, np_t), (gout_ref, gp_t)):
            high, rest = split(dot(src[...], proj).T)
            out[:, :TOK] = high
            out[:, TOK:] = rest

    def core_copy(g):
        return links.copy("core", g, low_s.at[g, 1 - c], r0.at[g], sibling)

    def sum1(g):
        return [
            links.copy("sum1", g * 3 + i, s1.at[g, i], v1.at[g, i], peer("x", k))
            for i, k in enumerate(SHIFTS["x"])
        ]

    def sum2(g):
        return [
            links.copy(
                "sum2", g * 3 + i, acc.at[g, shifted(where, "y", k)], v2.at[g, i], peer("y", k)
            )
            for i, k in enumerate(SHIFTS["y"])
        ]

    def stage_one(g):
        core_copy(g).wait_recv()
        copies = sum1(g)
        for i, k in enumerate(SHIFTS["x"]):
            to = shifted(where, "x", k)
            value = low_s[g, c, to] + r0[g, to]
            s1[g, i] = value.reshape(32, 4 * UNIT).astype(BF16)
            copies[i].start()
        acc[g] = low_s[g, c, x] + r0[g, x]

    def stage_two(g):
        received(sum1(g))
        total = (v1[g, 0].astype(F32) + v1[g, 1].astype(F32)) + v1[g, 2].astype(F32)
        acc[g] = acc[g] + total.reshape(NY, 8, 4 * UNIT)
        start(sum2(g))

    def stage_three(g):
        received(sum2(g))
        total = acc[g, y] + ((v2[g, 0] + v2[g, 1]) + v2[g, 2])
        h = g // 2
        for block in range(4):
            columns = pl.ds(
                pl.multiple_of(block * 2 * UNIT + lax.rem(g, 2) * UNIT, UNIT), UNIT
            )
            for i in range(NZ):
                rows[h, i, :, columns] = total[i : i + 1, block * UNIT : (block + 1) * UNIT]

    def sum3(h):
        return [
            links.copy(
                "sum3", h * 7 + i, rows.at[h, shifted(where, "z", k)], v3.at[h, i], peer("z", k)
            )
            for i, k in enumerate(SHIFTS["z"])
        ]

    def dir_z(h):
        own = tiles.at[h, c, z, y, x]
        return [
            links.copy("dir_z", h * 7 + i, own, own, peer("z", k))
            for i, k in enumerate(SHIFTS["z"])
        ]

    def summed(h):
        received(sum3(h))
        low = rows[h, z]
        for i in range(NZ - 1):
            low = low + v3[h, i]
        for block in range(4):
            columns = slice(block * WIDTH + h * 512, block * WIDTH + h * 512 + 512)
            part = low[:, block * 512 : (block + 1) * 512]
            low_out[:, columns] = part
            _, _, direction = adam(part, first_ref[:, columns], second_ref[:, columns])
            for a in range(4):
                dir_rows[block * 4 + a : block * 4 + a + 1, :] = direction[
                    :, a * 128 : (a + 1) * 128
                ]
        tiles[h, c, z, y, x] = dir_rows[...].astype(BF16)
        start(dir_z(h))

    paths = ((pl.ds(0, 4), "y", "x"), (pl.ds(4, 4), "x", "y"))

    def dir_mid(h):
        copies = []
        for depth, axis, _ in paths:
            own = tiles.at[h, c, depth, y, x]
            for k in SHIFTS[axis]:
                copies.append(
                    links.copy("dir_mid", h * 6 + len(copies), own, own, peer(axis, k))
                )
        return copies

    def lines(h, p, at):
        depth = paths[p][0]
        return tiles.at[h, c, depth, :, at] if p == 0 else tiles.at[h, c, depth, at]

    def dir_last(h):
        copies = []
        for p, (_, _, axis) in enumerate(paths):
            own = lines(h, p, where[axis])
            for k in SHIFTS[axis]:
                copies.append(
                    links.copy("dir_last", h * 6 + len(copies), own, own, peer(axis, k))
                )
        return copies

    def dir_across(h):
        refs = [lines(h, p, where[paths[p][2]]) for p in range(2)]
        for p, (_, _, axis) in enumerate(paths):
            refs += [lines(h, p, shifted(where, axis, -k)) for k in SHIFTS[axis]]
        return [
            links.copy("dir_across", h * 8 + i, r, r, sibling) for i, r in enumerate(refs)
        ]

    def hand_on(h):
        for got, on in zip(dir_last(h), dir_across(h)[2:]):
            got.wait_recv()
            on.start()

    def step_of(h):
        columns = slice(h * 128, (h + 1) * 128)
        own = dot(lhs[c], tiles[h, c].reshape(RANK * 8, 128))
        received(dir_across(h))
        step_ref[:, columns] = own + dot(lhs[1 - c], tiles[h, 1 - c].reshape(RANK * 8, 128))

    @pl.loop(0, 2 * GROUPS)
    def _(t):
        g, i = t // 2, lax.rem(t, 2)

        @pl.when(i == 0)
        def _():
            @pl.when(g < GROUPS - 1)
            def _():
                received(across(g))

            @pl.when(g == GROUPS - 1)
            def _():
                received(across_last())

            project(g)

        @pl.when(i == 1)
        def _():
            @pl.when(g == 0)
            def _():
                received(mids[2])
                open_bulk(2)

        def between():
            @pl.when((i == 0) & (g > 0))
            def _():
                stage_one(g - 1)

            @pl.when((i == 1) & (g < GROUPS - 2))
            def _():
                forward(g + 1)

            @pl.when((i == 1) & (g == GROUPS - 2))
            def _():
                for got, on in zip(z_last, across_last()[1:]):
                    got.wait_recv()
                    on.start()

            @pl.when(t == 0)
            def _():
                for got, on in zip(bulk_p(), across_p()[2:]):
                    got.wait_recv()
                    on.start()

        gq_t, gk, gv, attended_t = attend_pair(
            q_s[i], k_s[i], v_s[i], gh_s[i], bias, masks, between
        )

        @pl.when(t == 0)
        def _():
            received(across_p())
            project_rank()

        gq_t = (gq_t * 0.125).astype(BF16)
        low_q = dot(np_t[...], jnp.concatenate([gq_t, gq_t], axis=1), ROWS)
        grads = jnp.concatenate([(gk * 0.125).astype(BF16), gv.astype(BF16)], axis=1)
        low_kv = dot(np_t[...], jnp.concatenate([grads, grads], axis=0))
        attended_t = attended_t.astype(BF16)
        outer = dot(gp_t[...], jnp.concatenate([attended_t, attended_t], axis=1), ROWS)
        values = (low_q, low_kv[:, :128], low_kv[:, 128:], outer)
        for block in range(4):
            columns = pl.ds(pl.multiple_of(block * UNIT + i * 128, 128), 128)
            low_s[g, :, :, :, :, columns] = values[block].reshape(NC, NX, NY, NZ, 128)

        @pl.when(i == 1)
        def _():
            core_copy(g).start()

            @pl.when(g > 0)
            def _():
                stage_two(g - 1)

        @pl.when((i == 0) & (g > 1))
        def _():
            stage_three(g - 2)

            @pl.when(g == 3)
            def _():
                start(sum3(0))

    stage_one(GROUPS - 1)
    stage_three(GROUPS - 2)
    stage_two(GROUPS - 1)
    summed(0)
    stage_three(GROUPS - 1)
    start(sum3(1))
    received(dir_z(0))
    start(dir_mid(0))
    received(dir_mid(0))
    start(dir_last(0))
    start(dir_across(0)[:2])
    summed(1)
    hand_on(0)
    received(dir_z(1))
    start(dir_mid(1))
    step_of(0)
    received(dir_mid(1))
    start(dir_last(1))
    start(dir_across(1)[:2])
    hand_on(1)
    step_of(1)

    sent(quad + z_first + z_rank + z_rest + mid_rank)
    for copies in mids:
        sent(copies)
    sent(bulk_p() + across_p())

    @pl.loop(0, GROUPS)
    def _(g):
        sent([core_copy(g)] + sum1(g) + sum2(g))

        @pl.when(g < GROUPS - 1)
        def _():
            sent(bulk(g) + across(g))

    sent(x_last + y_last + z_last + across_last())

    for h in range(2):
        sent(sum3(h) + dir_z(h) + dir_mid(h) + dir_last(h) + dir_across(h))


def main(lengths, inputs, grad_out, gain, master, projector, first, second):
    vmem = pl.BlockSpec(memory_space=pltpu.VMEM)
    return pl.pallas_call(
        main_kernel,
        out_shape=(
            jax.ShapeDtypeStruct((64, 256), F32),
            jax.ShapeDtypeStruct((1, 4 * WIDTH), F32),
        ),
        in_specs=[pl.BlockSpec(memory_space=pltpu.SMEM)] + [vmem] * 7,
        out_specs=(vmem, vmem),
        scratch_shapes=[
            pltpu.VMEM((2, 5, NC, NZ, NY, 2, 2, 16, 128), BF16),
            pltpu.VMEM((4, 4, WIDTH), F32),
            pltpu.VMEM((4, 4, RANK), F32),
            pltpu.VMEM((4, RANK), F32),
            pltpu.VMEM((16, WIDTH), F32),
            pltpu.VMEM((16, RANK), F32),
            pltpu.VMEM((RANK, RANK), BF16),
            pltpu.VMEM((TOK, WIDTH), BF16),
            pltpu.VMEM((TOK, TOK), F32),
            pltpu.VMEM((RANK, 2 * TOK), BF16),
            pltpu.VMEM((RANK, 2 * TOK), BF16),
            pltpu.VMEM((2, TOK, 128), BF16),
            pltpu.VMEM((2, TOK, 128), BF16),
            pltpu.VMEM((2, TOK, 128), BF16),
            pltpu.VMEM((2, TOK, 128), F32),
            pltpu.VMEM((GROUPS, NC, NX, NY, NZ, 4 * UNIT), F32),
            pltpu.VMEM((GROUPS, NX, NY, NZ, 4 * UNIT), F32),
            pltpu.VMEM((GROUPS, 3, 32, 4 * UNIT), BF16),
            pltpu.VMEM((GROUPS, 3, 32, 4 * UNIT), BF16),
            pltpu.VMEM((GROUPS, NY, NZ, 4 * UNIT), F32),
            pltpu.VMEM((GROUPS, 3, NZ, 4 * UNIT), F32),
            pltpu.VMEM((2, NZ, 1, 2 * WIDTH), F32),
            pltpu.VMEM((2, NZ - 1, 1, 2 * WIDTH), F32),
            pltpu.VMEM((16, 128), F32),
            pltpu.VMEM((2, NC, NZ, NY, NX, 16, 128), BF16),
            pltpu.VMEM((NC, 64, 2 * WIDTH), BF16),
            pltpu.SemaphoreType.DMA((N_SEMS,)),
            pltpu.SemaphoreType.DMA((N_SEMS,)),
        ],
        compiler_params=pltpu.CompilerParams(
            collective_id=0, has_side_effects=True, vmem_limit_bytes=VMEM_LIMIT
        ),
        name="galore_step",
    )(lengths, inputs, grad_out, gain, master, projector, first, second)


def finish_kernel(
    step_ref, low_ref, first_ref, second_ref, master_ref, new_master, new_first, new_second
):
    first, second, _ = adam(low_ref[...], first_ref[...], second_ref[...])
    new_first[...] = first
    new_second[...] = second
    for a in range(16):
        for h in range(2):
            at = (a // 4) * WIDTH + h * 512 + (a % 4) * 128
            columns = slice(at, at + 128)
            for i in range(4):
                row = i * 16 + a
                new_master[i : i + 1, columns] = (
                    master_ref[i : i + 1, columns]
                    - learn_rate * galore_scale * step_ref[row : row + 1, h * 128 : h * 128 + 128]
                )


def finish(step, low, first, second, master):
    vmem = pl.BlockSpec(memory_space=pltpu.VMEM)
    return pl.pallas_call(
        finish_kernel,
        out_shape=(
            jax.ShapeDtypeStruct((4, 4 * WIDTH), F32),
            jax.ShapeDtypeStruct((1, 4 * WIDTH), F32),
            jax.ShapeDtypeStruct((1, 4 * WIDTH), F32),
        ),
        in_specs=[vmem] * 5,
        out_specs=(vmem, vmem, vmem),
        name="outputs",
    )(step, low, first, second, master)


def shards(
    inputs, grad_out, norm_gain, master, projector, moment_first, moment_second, doc_lengths
):
    step, low = main(
        doc_lengths, inputs, grad_out, norm_gain[None, :], master, projector,
        moment_first, moment_second,
    )
    return finish(step, low, moment_first, moment_second, master)


def solution(mesh):
    return jax.shard_map(
        shards,
        mesh=mesh,
        in_specs=(
            P("dp", None),
            P("dp", None),
            P(),
            P("dp", None),
            P("dp", None),
            P("dp", None),
            P("dp", None),
            P("dp", None),
        ),
        out_specs=(P("dp", None), P("dp", None), P("dp", None)),
        check_vma=False,
    )
```

```python
import jax
import jax.numpy as jnp
import numpy as np
from jax import lax
from jax.experimental import pallas as pl
from jax.experimental.pallas import tpu as pltpu
from jax.sharding import PartitionSpec as P

NZ, NY, NX, NC = 8, 4, 4, 2
SIZE = {"z": NZ, "y": NY, "x": NX}
SHIFTS = {"z": (4, 3, 5, 2, 6, 1, 7), "y": (2, 1, 3), "x": (2, 1, 3)}
GROUPS = 4
UNIT = 256
TOK = 384
WIDTH = 1024
RANK = 256
VMEM_LIMIT = 56 * 1024 * 1024

beta_one = 0.9
beta_two = 0.999
adam_eps = 1e-08
adam_step = 10.0
learn_rate = 0.01
galore_scale = 0.25
norm_eps = 1e-05

F32 = jnp.float32
BF16 = jnp.bfloat16
MESH = pl.DeviceIdType.MESH


def place():
    me = lax.axis_index("dp")
    c = lax.rem(me, NC)
    x = lax.rem(me // NC, NX)
    y = lax.rem(me // (NC * NX), NY)
    z = me // (NC * NX * NY)
    return {"z": z, "y": y, "x": x, "c": c}


def device_at(where, **moved):
    at = dict(where, **moved)
    return ((at["z"] * NY + at["y"]) * NX + at["x"]) * NC + at["c"]


def shifted(where, axis, by):
    n = SIZE[axis]
    return lax.rem(where[axis] + (by + n), n)


class Links:
    def __init__(self, send_sems, recv_sems):
        self.send_sems, self.recv_sems = send_sems, recv_sems
        self.bases = {}
        self.used = 0

    def reserve(self, name, count):
        self.bases[name] = self.used
        self.used += count

    def copy(self, name, i, src, dst, device):
        at = self.bases[name] + i
        return pltpu.make_async_remote_copy(
            src_ref=src,
            dst_ref=dst,
            send_sem=self.send_sems.at[at],
            recv_sem=self.recv_sems.at[at],
            device_id=(device,),
            device_id_type=MESH,
        )


N_SEMS = 232


def start(copies):
    for copy in copies:
        copy.start()


def received(copies):
    for copy in copies:
        copy.wait_recv()


def sent(copies):
    for copy in copies:
        copy.wait_send()


def greet(devices):
    barrier = pltpu.get_barrier_semaphore()
    for device in devices:
        pl.semaphore_signal(barrier, inc=1, device_id=(device,), device_id_type=MESH)
    pl.semaphore_wait(barrier, len(devices))


def dot(a, b, dims=((1,), (0,))):
    return lax.dot_general(a, b, (dims, ((), ())), preferred_element_type=F32)


ROWS = ((1,), (1,))
COLS = ((0,), (0,))


def split(value):
    high = value.astype(BF16)
    return high, (value - high.astype(F32)).astype(BF16)


def adam(low, first, second):
    new_first = beta_one * first + (1.0 - beta_one) * low
    new_second = beta_two * second + (1.0 - beta_two) * low * low
    direction = (
        new_first
        / (1.0 - beta_one**adam_step)
        / (jnp.sqrt(new_second / (1.0 - beta_two**adam_step)) + adam_eps)
    )
    return new_first, new_second, direction


def attend_pair(q, k, v, gh, bias_ref, masks, between):
    probs, highs = [], []
    left_v, right_v = [], []
    for mask in masks:
        s = dot(k, q * mask, ROWS) * 0.125 + bias_ref[...]
        e = jnp.exp(s - jnp.max(s, axis=0, keepdims=True))
        p = e * (1.0 / jnp.sum(e, axis=0, keepdims=True))
        probs.append(p)
    between()
    gh_high, gh_rest = split(gh)
    v_twice = jnp.concatenate([v, v], axis=1)
    grads, right_k, left_q = [], [], []
    for p, mask in zip(probs, masks):
        p_high, p_rest = split(p)
        gh_m, gh_r = gh_high * mask, gh_rest * mask
        gp = dot(v_twice, jnp.concatenate([gh_m, gh_r], axis=1), ROWS)
        gs = p * (gp - jnp.sum(p * gp, axis=0, keepdims=True))
        highs.append(p_high)
        left_v += [p_high, p_rest]
        right_v += [
            jnp.concatenate([gh_m, gh_r], axis=1),
            jnp.concatenate([gh_m, jnp.zeros_like(gh_m)], axis=1),
        ]
        grads += list(split(gs))
        right_k += [q * mask] * 2
        left_q += [k * mask] * 2
    gv = dot(jnp.concatenate(left_v, axis=1), jnp.concatenate(right_v, axis=0))
    gv = gv[:, :128] + gv[:, 128:]
    gk = dot(jnp.concatenate(grads, axis=1), jnp.concatenate(right_k, axis=0))
    gq_t = dot(jnp.concatenate(left_q, axis=0), jnp.concatenate(grads, axis=0), COLS)
    by_head = jnp.concatenate([v * mask for mask in masks], axis=0)
    a_t = dot(by_head, jnp.concatenate(highs, axis=0), COLS)
    return gq_t, gk, gv, a_t


def main_kernel(
    len_ref, in_ref, gout_ref, gain_ref, master_ref, proj_ref, first_ref, second_ref,
    step_ref, low_out,
    w, quad_w, quad_p, own_p, rows_w, rows_p, order, normed, bias, np_t, gp_t,
    q_s, k_s, v_s, gh_s, low_s, r0, s1, v1, acc, v2, rows, v3, dir_rows, tiles, lhs,
    send_sems, recv_sems
):
    where = place()
    c, x, y, z = where["c"], where["x"], where["y"], where["z"]
    xh, xl = x // 2, lax.rem(x, 2)
    flip = x + 1 - 2 * xl
    sibling = device_at(where, c=1 - c)
    links = Links(send_sems, recv_sems)
    for name, count in (
        ("quad", 6), ("z0", 7), ("zp", 7), ("z1", 7), ("mid0", 6), ("midp", 6), ("mid1", 6), ("mid2", 6),
        ("x3", 3),
        ("y3", 3), ("z3", 7),
        ("bulk", 24), ("across", 32), ("bulk_p", 6), ("across_p", 8), ("core", 4),
        ("sum1", 12), ("sum2", 12), ("sum3", 14), ("dir_z", 14), ("dir_mid", 12),
        ("dir_last", 12), ("dir_across", 16),
    ):
        links.reserve(name, count)

    def peer(axis, by):
        return device_at(where, **{axis: shifted(where, axis, by)})

    greet(
        [sibling, device_at(where, x=flip, c=1 - c)]
        + [peer(axis, k) for axis in "xyz" for k in SHIFTS[axis]]
    )

    own_p[...] = proj_ref[...].astype(F32)
    mine = xl * 2 + c
    quad = []
    for i, (dx, dc) in enumerate(((0, 1), (1, 0), (1, 1))):
        to_xl = 1 - xl if dx else xl
        to_c = 1 - c if dc else c
        to = device_at(where, x=xh * 2 + to_xl, c=to_c)
        columns = pl.ds(pl.multiple_of((to_xl * 2 + to_c) * WIDTH, WIDTH), WIDTH)
        quad.append(
            links.copy("quad", 2 * i, master_ref.at[:, columns], quad_w.at[mine], to)
        )
        quad.append(links.copy("quad", 2 * i + 1, own_p, quad_p.at[mine], to))
    start(quad)
    columns = pl.ds(pl.multiple_of(mine * WIDTH, WIDTH), WIDTH)
    quad_w[mine] = master_ref[:, columns]
    quad_p[mine] = own_p[...]

    source = lax.broadcasted_iota(jnp.int32, (RANK, RANK), 0)
    place_to = lax.broadcasted_iota(jnp.int32, (RANK, RANK), 1)
    natural = (
        (place_to & 7) * 32
        + ((place_to >> 3) & 3) * 8
        + ((place_to >> 5) & 3) * 2
        + (place_to >> 7)
    )
    order[...] = (source == natural).astype(F32).astype(BF16)

    received(quad)
    for i in range(4):
        rows_w[i * 4 : i * 4 + 4, :] = quad_w[i]
        rows_p[i * 4 : i * 4 + 4, :] = quad_p[i]
    ordered = dot(rows_p[...].astype(BF16), order[...])
    w[0, 4, c, z, y, xh, xl] = jnp.where(c == 0, ordered[:, :128], ordered[:, 128:]).astype(
        BF16
    )
    for pair in range(8):
        w[pair % 2, pair // 2, c, z, y, xh, xl] = rows_w[
            :, pair * 128 : (pair + 1) * 128
        ].astype(BF16)

    def first_step(name, slots, kinds):
        copies = []
        for i, k in enumerate(SHIFTS["z"]):
            ref = w.at[kinds, slots, c, z, y, xh, xl]
            copies.append(links.copy(name, i, ref, ref, peer("z", k)))
        return copies

    z_first = first_step("z0", pl.ds(0, 1), pl.ds(0, 2))
    z_rank = first_step("zp", pl.ds(4, 1), pl.ds(0, 1))
    z_rest = first_step("z1", pl.ds(1, 2), pl.ds(0, 2))

    def other_way(name, axis, ref):
        return [
            links.copy(name, i, ref, ref, peer(axis, k)) for i, k in enumerate(SHIFTS[axis])
        ]

    x_last = other_way("x3", "x", w.at[:, 3, c, z, y, xh, xl])
    y_last = other_way("y3", "y", w.at[:, 3, c, z, y])
    z_last = other_way("z3", "z", w.at[:, 3, c, z])
    start(z_first + z_rank + x_last + z_rest)

    values = in_ref[...].astype(F32)
    scale = lax.rsqrt(jnp.mean(values * values, axis=1, keepdims=True) + norm_eps)
    normed[...] = (values * scale * gain_ref[...]).astype(BF16)
    b0 = len_ref[0, 0]
    b1 = b0 + len_ref[0, 1]
    b2 = b1 + len_ref[0, 2]
    b3 = b2 + len_ref[0, 3]

    def segment(position):
        return sum((position >= b).astype(jnp.int32) for b in (b0, b1, b2, b3))

    key = lax.broadcasted_iota(jnp.int32, (TOK, 1), 0)
    query = lax.broadcasted_iota(jnp.int32, (1, TOK), 1)
    seen = (segment(key) == segment(query)) & (query >= key)
    bias[...] = jnp.where(seen, F32(0.0), F32(-1e30))
    def middle(g):
        copies = []
        for kind, axis in ((0, "y"), (1, "x")):
            for k in SHIFTS[axis]:
                ref = w.at[kind, g, c, :, y, xh, xl]
                copies.append(links.copy("mid%d" % g, len(copies), ref, ref, peer(axis, k)))
        return copies

    depths = (pl.ds(0, 4), pl.ds(4, 4))

    def middle_p():
        copies = []
        for depth, axis in zip(depths, "yx"):
            for k in SHIFTS[axis]:
                ref = w.at[0, 4, c, depth, y, xh, xl]
                copies.append(links.copy("midp", len(copies), ref, ref, peer(axis, k)))
        return copies

    def rank_lines(p, at):
        if p == 0:
            return w.at[0, 4, c, depths[0], :, at // 2, lax.rem(at, 2)]
        return w.at[0, 4, c, depths[1], at]

    def along_x(slot, at):
        return w.at[0, slot, c, :, :, at // 2, lax.rem(at, 2)]

    def along_y(slot, at):
        return w.at[1, slot, c, :, at]

    def bulk(g):
        copies = []
        for i, k in enumerate(SHIFTS["x"]):
            ref = along_x(g, x)
            copies.append(links.copy("bulk", g * 6 + i, ref, ref, peer("x", k)))
        for i, k in enumerate(SHIFTS["y"]):
            ref = along_y(g, y)
            copies.append(links.copy("bulk", g * 6 + 3 + i, ref, ref, peer("y", k)))
        return copies

    def bulk_p():
        copies = []
        for p, axis in enumerate("xy"):
            ref = rank_lines(p, where[axis])
            for k in SHIFTS[axis]:
                copies.append(links.copy("bulk_p", len(copies), ref, ref, peer(axis, k)))
        return copies

    def across(g):
        refs = [along_x(g, x), along_y(g, y)]
        refs += [along_x(g, shifted(where, "x", -k)) for k in SHIFTS["x"]]
        refs += [along_y(g, shifted(where, "y", -k)) for k in SHIFTS["y"]]
        return [links.copy("across", g * 8 + i, r, r, sibling) for i, r in enumerate(refs)]

    def across_p():
        refs = [rank_lines(0, x), rank_lines(1, y)]
        for p, axis in enumerate("xy"):
            refs += [rank_lines(p, shifted(where, axis, -k)) for k in SHIFTS[axis]]
        return [links.copy("across_p", i, r, r, sibling) for i, r in enumerate(refs)]

    def open_bulk(g):
        start(bulk(g))
        start(across(g)[:2])

    def forward(g):
        for got, on in zip(bulk(g), across(g)[2:]):
            got.wait_recv()
            on.start()

    def across_last():
        refs = [w.at[:, 3, c, z]]
        refs += [w.at[:, 3, c, shifted(where, "z", -k)] for k in SHIFTS["z"]]
        return [links.copy("across", 24 + i, r, r, sibling) for i, r in enumerate(refs)]

    mids = [middle(g) for g in range(GROUPS - 1)]
    mid_rank = middle_p()
    received(z_first)
    start(mids[0])
    received(z_rank)
    start(mid_rank)
    received(x_last)
    start(y_last)
    received(mids[0])
    open_bulk(0)
    received(z_rest)
    start(mids[1])
    received(mid_rank)
    start(bulk_p())
    start(across_p()[:2])
    received(y_last)
    start(z_last)
    start(across_last()[:1])

    spread = lax.broadcasted_iota(jnp.int32, (RANK, 256), 1)
    source = lax.broadcasted_iota(jnp.int32, (RANK, 256), 0)
    diagonal = (spread & 15) == (lax.broadcasted_iota(jnp.int32, (RANK, 256), 0) & 15)
    own_rows = own_p[...].astype(BF16)
    for n in range(16):
        kk = n * 16 + (spread >> 4)
        pick = (source == ((kk & 127) * 2 + (kk >> 7))).astype(F32).astype(BF16)
        line = dot(own_rows, pick)
        for i in range(4):
            columns = slice(n % 8 * 256, n % 8 * 256 + 256)
            lhs[n // 8, i * 16 : (i + 1) * 16, columns] = jnp.where(
                diagonal[:16], line[i : i + 1, :], F32(0.0)
            ).astype(BF16)

    forward(0)
    received(mids[1])
    open_bulk(1)
    start(mids[2])

    lane = lax.broadcasted_iota(jnp.int32, (1, 128), 1)
    firsts = (lane < 64).astype(F32).astype(BF16)
    masks = (firsts, 1 - firsts)

    def weight(slot, low_x, core):
        halves = [w[a, slot, core, :, :, :, low_x].reshape(WIDTH, 128) for a in range(2)]
        return jnp.concatenate(halves, axis=1)

    def project(g):
        for src, low_x, core, out in (
            (normed, 0, 0, q_s), (normed, 0, 1, k_s), (normed, 1, 0, v_s), (gout_ref, 1, 1, gh_s)
        ):
            res = dot(src[...], weight(g, low_x, core))
            out[0] = res[:, :128].astype(out.dtype)
            out[1] = res[:, 128:].astype(out.dtype)

    def project_rank():
        both = [w[0, 4, core, :, :, :, 0].reshape(WIDTH, 128) for core in range(2)]
        proj = jnp.concatenate(both, axis=1)
        for src, out in ((normed, np_t), (gout_ref, gp_t)):
            high, rest = split(dot(src[...], proj).T)
            out[:, :TOK] = high
            out[:, TOK:] = rest

    def core_copy(g):
        return links.copy("core", g, low_s.at[g, 1 - c], r0.at[g], sibling)

    def sum1(g):
        return [
            links.copy("sum1", g * 3 + i, s1.at[g, i], v1.at[g, i], peer("x", k))
            for i, k in enumerate(SHIFTS["x"])
        ]

    def sum2(g):
        return [
            links.copy(
                "sum2", g * 3 + i, acc.at[g, shifted(where, "y", k)], v2.at[g, i], peer("y", k)
            )
            for i, k in enumerate(SHIFTS["y"])
        ]

    def stage_one(g):
        core_copy(g).wait_recv()
        copies = sum1(g)
        for i, k in enumerate(SHIFTS["x"]):
            to = shifted(where, "x", k)
            value = low_s[g, c, to] + r0[g, to]
            s1[g, i] = value.reshape(32, 4 * UNIT).astype(BF16)
            copies[i].start()
        acc[g] = low_s[g, c, x] + r0[g, x]

    def stage_two(g):
        received(sum1(g))
        total = (v1[g, 0].astype(F32) + v1[g, 1].astype(F32)) + v1[g, 2].astype(F32)
        acc[g] = acc[g] + total.reshape(NY, 8, 4 * UNIT)
        start(sum2(g))

    def stage_three(g):
        received(sum2(g))
        total = acc[g, y] + ((v2[g, 0] + v2[g, 1]) + v2[g, 2])
        h = g // 2
        for block in range(4):
            columns = pl.ds(
                pl.multiple_of(block * 2 * UNIT + lax.rem(g, 2) * UNIT, UNIT), UNIT
            )
            for i in range(NZ):
                rows[h, i, :, columns] = total[i : i + 1, block * UNIT : (block + 1) * UNIT]

    def sum3(h):
        return [
            links.copy(
                "sum3", h * 7 + i, rows.at[h, shifted(where, "z", k)], v3.at[h, i], peer("z", k)
            )
            for i, k in enumerate(SHIFTS["z"])
        ]

    def dir_z(h):
        own = tiles.at[h, c, z, y, x]
        return [
            links.copy("dir_z", h * 7 + i, own, own, peer("z", k))
            for i, k in enumerate(SHIFTS["z"])
        ]

    def summed(h):
        received(sum3(h))
        low = rows[h, z]
        for i in range(NZ - 1):
            low = low + v3[h, i]
        for block in range(4):
            columns = slice(block * WIDTH + h * 512, block * WIDTH + h * 512 + 512)
            part = low[:, block * 512 : (block + 1) * 512]
            low_out[:, columns] = part
            _, _, direction = adam(part, first_ref[:, columns], second_ref[:, columns])
            for a in range(4):
                dir_rows[block * 4 + a : block * 4 + a + 1, :] = direction[
                    :, a * 128 : (a + 1) * 128
                ]
        tiles[h, c, z, y, x] = dir_rows[...].astype(BF16)
        start(dir_z(h))

    paths = ((pl.ds(0, 4), "y", "x"), (pl.ds(4, 4), "x", "y"))

    def dir_mid(h):
        copies = []
        for depth, axis, _ in paths:
            own = tiles.at[h, c, depth, y, x]
            for k in SHIFTS[axis]:
                copies.append(
                    links.copy("dir_mid", h * 6 + len(copies), own, own, peer(axis, k))
                )
        return copies

    def lines(h, p, at):
        depth = paths[p][0]
        return tiles.at[h, c, depth, :, at] if p == 0 else tiles.at[h, c, depth, at]

    def dir_last(h):
        copies = []
        for p, (_, _, axis) in enumerate(paths):
            own = lines(h, p, where[axis])
            for k in SHIFTS[axis]:
                copies.append(
                    links.copy("dir_last", h * 6 + len(copies), own, own, peer(axis, k))
                )
        return copies

    def dir_across(h):
        refs = [lines(h, p, where[paths[p][2]]) for p in range(2)]
        for p, (_, _, axis) in enumerate(paths):
            refs += [lines(h, p, shifted(where, axis, -k)) for k in SHIFTS[axis]]
        return [
            links.copy("dir_across", h * 8 + i, r, r, sibling) for i, r in enumerate(refs)
        ]

    def hand_on(h):
        for got, on in zip(dir_last(h), dir_across(h)[2:]):
            got.wait_recv()
            on.start()

    def step_of(h):
        columns = slice(h * 128, (h + 1) * 128)
        own = dot(lhs[c], tiles[h, c].reshape(RANK * 8, 128))
        received(dir_across(h))
        step_ref[:, columns] = own + dot(lhs[1 - c], tiles[h, 1 - c].reshape(RANK * 8, 128))

    @pl.loop(0, 2 * GROUPS)
    def _(t):
        g, i = t // 2, lax.rem(t, 2)

        @pl.when(i == 0)
        def _():
            @pl.when(g < GROUPS - 1)
            def _():
                received(across(g))

            @pl.when(g == GROUPS - 1)
            def _():
                received(across_last())

            project(g)

        @pl.when(i == 1)
        def _():
            @pl.when(g == 0)
            def _():
                received(mids[2])
                open_bulk(2)

            @pl.when(g == 1)
            def _():
                forward(2)

        def between():
            @pl.when((i == 0) & (g > 0))
            def _():
                stage_one(g - 1)

            @pl.when((i == 1) & (g == 0))
            def _():
                forward(1)

            @pl.when((i == 0) & (g == GROUPS - 2))
            def _():
                for got, on in zip(z_last, across_last()[1:]):
                    got.wait_recv()
                    on.start()

            @pl.when(t == 0)
            def _():
                for got, on in zip(bulk_p(), across_p()[2:]):
                    got.wait_recv()
                    on.start()

        gq_t, gk, gv, attended_t = attend_pair(
            q_s[i], k_s[i], v_s[i], gh_s[i], bias, masks, between
        )

        @pl.when(t == 0)
        def _():
            received(across_p())
            project_rank()

        gq_t = (gq_t * 0.125).astype(BF16)
        low_q = dot(np_t[...], jnp.concatenate([gq_t, gq_t], axis=1), ROWS)
        grads = jnp.concatenate([(gk * 0.125).astype(BF16), gv.astype(BF16)], axis=1)
        low_kv = dot(np_t[...], jnp.concatenate([grads, grads], axis=0))
        attended_t = attended_t.astype(BF16)
        outer = dot(gp_t[...], jnp.concatenate([attended_t, attended_t], axis=1), ROWS)
        values = (low_q, low_kv[:, :128], low_kv[:, 128:], outer)
        for block in range(4):
            columns = pl.ds(pl.multiple_of(block * UNIT + i * 128, 128), 128)
            low_s[g, :, :, :, :, columns] = values[block].reshape(NC, NX, NY, NZ, 128)

        @pl.when(i == 1)
        def _():
            core_copy(g).start()

            @pl.when(g > 0)
            def _():
                stage_two(g - 1)

        @pl.when((i == 0) & (g > 1))
        def _():
            stage_three(g - 2)

            @pl.when(g == 3)
            def _():
                start(sum3(0))

    stage_one(GROUPS - 1)
    stage_three(GROUPS - 2)
    stage_two(GROUPS - 1)
    summed(0)
    stage_three(GROUPS - 1)
    start(sum3(1))
    received(dir_z(0))
    start(dir_mid(0))
    received(dir_mid(0))
    start(dir_last(0))
    start(dir_across(0)[:2])
    summed(1)
    hand_on(0)
    received(dir_z(1))
    start(dir_mid(1))
    step_of(0)
    received(dir_mid(1))
    start(dir_last(1))
    start(dir_across(1)[:2])
    hand_on(1)
    step_of(1)

    sent(quad + z_first + z_rank + z_rest + mid_rank)
    for copies in mids:
        sent(copies)
    sent(bulk_p() + across_p())

    @pl.loop(0, GROUPS)
    def _(g):
        sent([core_copy(g)] + sum1(g) + sum2(g))

        @pl.when(g < GROUPS - 1)
        def _():
            sent(bulk(g) + across(g))

    sent(x_last + y_last + z_last + across_last())

    for h in range(2):
        sent(sum3(h) + dir_z(h) + dir_mid(h) + dir_last(h) + dir_across(h))


def main(lengths, inputs, grad_out, gain, master, projector, first, second):
    vmem = pl.BlockSpec(memory_space=pltpu.VMEM)
    return pl.pallas_call(
        main_kernel,
        out_shape=(
            jax.ShapeDtypeStruct((64, 256), F32),
            jax.ShapeDtypeStruct((1, 4 * WIDTH), F32),
        ),
        in_specs=[pl.BlockSpec(memory_space=pltpu.SMEM)] + [vmem] * 7,
        out_specs=(vmem, vmem),
        scratch_shapes=[
            pltpu.VMEM((2, 5, NC, NZ, NY, 2, 2, 16, 128), BF16),
            pltpu.VMEM((4, 4, WIDTH), F32),
            pltpu.VMEM((4, 4, RANK), F32),
            pltpu.VMEM((4, RANK), F32),
            pltpu.VMEM((16, WIDTH), F32),
            pltpu.VMEM((16, RANK), F32),
            pltpu.VMEM((RANK, RANK), BF16),
            pltpu.VMEM((TOK, WIDTH), BF16),
            pltpu.VMEM((TOK, TOK), F32),
            pltpu.VMEM((RANK, 2 * TOK), BF16),
            pltpu.VMEM((RANK, 2 * TOK), BF16),
            pltpu.VMEM((2, TOK, 128), BF16),
            pltpu.VMEM((2, TOK, 128), BF16),
            pltpu.VMEM((2, TOK, 128), BF16),
            pltpu.VMEM((2, TOK, 128), F32),
            pltpu.VMEM((GROUPS, NC, NX, NY, NZ, 4 * UNIT), F32),
            pltpu.VMEM((GROUPS, NX, NY, NZ, 4 * UNIT), F32),
            pltpu.VMEM((GROUPS, 3, 32, 4 * UNIT), BF16),
            pltpu.VMEM((GROUPS, 3, 32, 4 * UNIT), BF16),
            pltpu.VMEM((GROUPS, NY, NZ, 4 * UNIT), F32),
            pltpu.VMEM((GROUPS, 3, NZ, 4 * UNIT), F32),
            pltpu.VMEM((2, NZ, 1, 2 * WIDTH), F32),
            pltpu.VMEM((2, NZ - 1, 1, 2 * WIDTH), F32),
            pltpu.VMEM((16, 128), F32),
            pltpu.VMEM((2, NC, NZ, NY, NX, 16, 128), BF16),
            pltpu.VMEM((NC, 64, 2 * WIDTH), BF16),
            pltpu.SemaphoreType.DMA((N_SEMS,)),
            pltpu.SemaphoreType.DMA((N_SEMS,)),
        ],
        compiler_params=pltpu.CompilerParams(
            collective_id=0, has_side_effects=True, vmem_limit_bytes=VMEM_LIMIT
        ),
        name="galore_step",
    )(lengths, inputs, grad_out, gain, master, projector, first, second)


def finish_kernel(
    step_ref, low_ref, first_ref, second_ref, master_ref, new_master, new_first, new_second
):
    first, second, _ = adam(low_ref[...], first_ref[...], second_ref[...])
    new_first[...] = first
    new_second[...] = second
    for a in range(16):
        for h in range(2):
            at = (a // 4) * WIDTH + h * 512 + (a % 4) * 128
            columns = slice(at, at + 128)
            for i in range(4):
                row = i * 16 + a
                new_master[i : i + 1, columns] = (
                    master_ref[i : i + 1, columns]
                    - learn_rate * galore_scale * step_ref[row : row + 1, h * 128 : h * 128 + 128]
                )


def finish(step, low, first, second, master):
    vmem = pl.BlockSpec(memory_space=pltpu.VMEM)
    return pl.pallas_call(
        finish_kernel,
        out_shape=(
            jax.ShapeDtypeStruct((4, 4 * WIDTH), F32),
            jax.ShapeDtypeStruct((1, 4 * WIDTH), F32),
            jax.ShapeDtypeStruct((1, 4 * WIDTH), F32),
        ),
        in_specs=[vmem] * 5,
        out_specs=(vmem, vmem, vmem),
        name="outputs",
    )(step, low, first, second, master)


def shards(
    inputs, grad_out, norm_gain, master, projector, moment_first, moment_second, doc_lengths
):
    step, low = main(
        doc_lengths, inputs, grad_out, norm_gain[None, :], master, projector,
        moment_first, moment_second,
    )
    return finish(step, low, moment_first, moment_second, master)


def solution(mesh):
    return jax.shard_map(
        shards,
        mesh=mesh,
        in_specs=(
            P("dp", None),
            P("dp", None),
            P(),
            P("dp", None),
            P("dp", None),
            P("dp", None),
            P("dp", None),
            P("dp", None),
        ),
        out_specs=(P("dp", None), P("dp", None), P("dp", None)),
        check_vma=False,
    )
```

```python
import jax
import jax.numpy as jnp
import numpy as np
from jax import lax
from jax.experimental import pallas as pl
from jax.experimental.pallas import tpu as pltpu
from jax.sharding import PartitionSpec as P

NZ, NY, NX, NC = 8, 4, 4, 2
SIZE = {"z": NZ, "y": NY, "x": NX}
SHIFTS = {"z": (4, 3, 5, 2, 6, 1, 7), "y": (2, 1, 3), "x": (2, 1, 3)}
GROUPS = 4
UNIT = 256
TOK = 384
WIDTH = 1024
RANK = 256
VMEM_LIMIT = 56 * 1024 * 1024

beta_one = 0.9
beta_two = 0.999
adam_eps = 1e-08
adam_step = 10.0
learn_rate = 0.01
galore_scale = 0.25
norm_eps = 1e-05

F32 = jnp.float32
BF16 = jnp.bfloat16
MESH = pl.DeviceIdType.MESH


def place():
    me = lax.axis_index("dp")
    c = lax.rem(me, NC)
    x = lax.rem(me // NC, NX)
    y = lax.rem(me // (NC * NX), NY)
    z = me // (NC * NX * NY)
    return {"z": z, "y": y, "x": x, "c": c}


def device_at(where, **moved):
    at = dict(where, **moved)
    return ((at["z"] * NY + at["y"]) * NX + at["x"]) * NC + at["c"]


def shifted(where, axis, by):
    n = SIZE[axis]
    return lax.rem(where[axis] + (by + n), n)


class Links:
    def __init__(self, send_sems, recv_sems):
        self.send_sems, self.recv_sems = send_sems, recv_sems
        self.bases = {}
        self.used = 0

    def reserve(self, name, count):
        self.bases[name] = self.used
        self.used += count

    def copy(self, name, i, src, dst, device):
        at = self.bases[name] + i
        return pltpu.make_async_remote_copy(
            src_ref=src,
            dst_ref=dst,
            send_sem=self.send_sems.at[at],
            recv_sem=self.recv_sems.at[at],
            device_id=(device,),
            device_id_type=MESH,
        )


N_SEMS = 232


def start(copies):
    for copy in copies:
        copy.start()


def received(copies):
    for copy in copies:
        copy.wait_recv()


def sent(copies):
    for copy in copies:
        copy.wait_send()


def greet(devices):
    barrier = pltpu.get_barrier_semaphore()
    for device in devices:
        pl.semaphore_signal(barrier, inc=1, device_id=(device,), device_id_type=MESH)
    pl.semaphore_wait(barrier, len(devices))


def dot(a, b, dims=((1,), (0,))):
    return lax.dot_general(a, b, (dims, ((), ())), preferred_element_type=F32)


ROWS = ((1,), (1,))
COLS = ((0,), (0,))


def split(value):
    high = value.astype(BF16)
    return high, (value - high.astype(F32)).astype(BF16)


def adam(low, first, second):
    new_first = beta_one * first + (1.0 - beta_one) * low
    new_second = beta_two * second + (1.0 - beta_two) * low * low
    direction = (
        new_first
        / (1.0 - beta_one**adam_step)
        / (jnp.sqrt(new_second / (1.0 - beta_two**adam_step)) + adam_eps)
    )
    return new_first, new_second, direction


def attend_pair(q, k, v, gh, bias_ref, masks, between):
    probs, highs = [], []
    left_v, right_v = [], []
    for mask in masks:
        s = dot(k, q * mask, ROWS) * 0.125 + bias_ref[...]
        e = jnp.exp(s - jnp.max(s, axis=0, keepdims=True))
        p = e * (1.0 / jnp.sum(e, axis=0, keepdims=True))
        probs.append(p)
    between()
    gh_high, gh_rest = split(gh)
    v_twice = jnp.concatenate([v, v], axis=1)
    grads, right_k, left_q = [], [], []
    for p, mask in zip(probs, masks):
        p_high, p_rest = split(p)
        gh_m, gh_r = gh_high * mask, gh_rest * mask
        gp = dot(v_twice, jnp.concatenate([gh_m, gh_r], axis=1), ROWS)
        gs = p * (gp - jnp.sum(p * gp, axis=0, keepdims=True))
        highs.append(p_high)
        left_v += [p_high, p_rest]
        right_v += [
            jnp.concatenate([gh_m, gh_r], axis=1),
            jnp.concatenate([gh_m, jnp.zeros_like(gh_m)], axis=1),
        ]
        grads += list(split(gs))
        right_k += [q * mask] * 2
        left_q += [k * mask] * 2
    gv = dot(jnp.concatenate(left_v, axis=1), jnp.concatenate(right_v, axis=0))
    gv = gv[:, :128] + gv[:, 128:]
    gk = dot(jnp.concatenate(grads, axis=1), jnp.concatenate(right_k, axis=0))
    gq_t = dot(jnp.concatenate(left_q, axis=0), jnp.concatenate(grads, axis=0), COLS)
    by_head = jnp.concatenate([v * mask for mask in masks], axis=0)
    a_t = dot(by_head, jnp.concatenate(highs, axis=0), COLS)
    return gq_t, gk, gv, a_t


def main_kernel(
    len_ref, in_ref, gout_ref, gain_ref, master_ref, proj_ref, first_ref, second_ref,
    step_ref, low_out,
    w, quad_w, quad_p, own_p, rows_w, rows_p, order, normed, bias, np_t, gp_t,
    q_s, k_s, v_s, gh_s, low_s, r0, s1, v1, acc, v2, rows, v3, dir_rows, tiles, lhs,
    send_sems, recv_sems
):
    where = place()
    c, x, y, z = where["c"], where["x"], where["y"], where["z"]
    xh, xl = x // 2, lax.rem(x, 2)
    flip = x + 1 - 2 * xl
    sibling = device_at(where, c=1 - c)
    links = Links(send_sems, recv_sems)
    for name, count in (
        ("quad", 6), ("z0", 7), ("zp", 7), ("z1", 7), ("mid0", 6), ("midp", 6), ("mid1", 6), ("mid2", 6),
        ("x3", 3),
        ("y3", 3), ("z3", 7),
        ("bulk", 24), ("across", 32), ("bulk_p", 6), ("across_p", 8), ("core", 4),
        ("sum1", 12), ("sum2", 12), ("sum3", 14), ("dir_z", 14), ("dir_mid", 12),
        ("dir_last", 12), ("dir_across", 16),
    ):
        links.reserve(name, count)

    def peer(axis, by):
        return device_at(where, **{axis: shifted(where, axis, by)})

    greet(
        [sibling, device_at(where, x=flip, c=1 - c)]
        + [peer(axis, k) for axis in "xyz" for k in SHIFTS[axis]]
    )

    own_p[...] = proj_ref[...].astype(F32)
    mine = xl * 2 + c
    quad = []
    for i, (dx, dc) in enumerate(((0, 1), (1, 0), (1, 1))):
        to_xl = 1 - xl if dx else xl
        to_c = 1 - c if dc else c
        to = device_at(where, x=xh * 2 + to_xl, c=to_c)
        columns = pl.ds(pl.multiple_of((to_xl * 2 + to_c) * WIDTH, WIDTH), WIDTH)
        quad.append(
            links.copy("quad", 2 * i, master_ref.at[:, columns], quad_w.at[mine], to)
        )
        quad.append(links.copy("quad", 2 * i + 1, own_p, quad_p.at[mine], to))
    start(quad)
    columns = pl.ds(pl.multiple_of(mine * WIDTH, WIDTH), WIDTH)
    quad_w[mine] = master_ref[:, columns]
    quad_p[mine] = own_p[...]

    source = lax.broadcasted_iota(jnp.int32, (RANK, RANK), 0)
    place_to = lax.broadcasted_iota(jnp.int32, (RANK, RANK), 1)
    natural = (
        (place_to & 7) * 32
        + ((place_to >> 3) & 3) * 8
        + ((place_to >> 5) & 3) * 2
        + (place_to >> 7)
    )
    order[...] = (source == natural).astype(F32).astype(BF16)

    received(quad)
    for i in range(4):
        rows_w[i * 4 : i * 4 + 4, :] = quad_w[i]
        rows_p[i * 4 : i * 4 + 4, :] = quad_p[i]
    ordered = dot(rows_p[...].astype(BF16), order[...])
    w[0, 4, c, z, y, xh, xl] = jnp.where(c == 0, ordered[:, :128], ordered[:, 128:]).astype(
        BF16
    )
    for pair in range(8):
        w[pair % 2, pair // 2, c, z, y, xh, xl] = rows_w[
            :, pair * 128 : (pair + 1) * 128
        ].astype(BF16)

    def first_step(name, slots, kinds):
        copies = []
        for i, k in enumerate(SHIFTS["z"]):
            ref = w.at[kinds, slots, c, z, y, xh, xl]
            copies.append(links.copy(name, i, ref, ref, peer("z", k)))
        return copies

    z_first = first_step("z0", pl.ds(0, 1), pl.ds(0, 2))
    z_rank = first_step("zp", pl.ds(4, 1), pl.ds(0, 1))
    z_rest = first_step("z1", pl.ds(1, 2), pl.ds(0, 2))

    def other_way(name, axis, ref):
        return [
            links.copy(name, i, ref, ref, peer(axis, k)) for i, k in enumerate(SHIFTS[axis])
        ]

    x_last = other_way("x3", "x", w.at[:, 3, c, z, y, xh, xl])
    y_last = other_way("y3", "y", w.at[:, 3, c, z, y])
    z_last = other_way("z3", "z", w.at[:, 3, c, z])
    start(z_first + z_rank + x_last + z_rest)

    values = in_ref[...].astype(F32)
    scale = lax.rsqrt(jnp.mean(values * values, axis=1, keepdims=True) + norm_eps)
    normed[...] = (values * scale * gain_ref[...]).astype(BF16)
    b0 = len_ref[0, 0]
    b1 = b0 + len_ref[0, 1]
    b2 = b1 + len_ref[0, 2]
    b3 = b2 + len_ref[0, 3]

    def segment(position):
        return sum((position >= b).astype(jnp.int32) for b in (b0, b1, b2, b3))

    key = lax.broadcasted_iota(jnp.int32, (TOK, 1), 0)
    query = lax.broadcasted_iota(jnp.int32, (1, TOK), 1)
    seen = (segment(key) == segment(query)) & (query >= key)
    bias[...] = jnp.where(seen, F32(0.0), F32(-1e30))
    def middle(g):
        copies = []
        for kind, axis in ((0, "y"), (1, "x")):
            for k in SHIFTS[axis]:
                ref = w.at[kind, g, c, :, y, xh, xl]
                copies.append(links.copy("mid%d" % g, len(copies), ref, ref, peer(axis, k)))
        return copies

    depths = (pl.ds(0, 4), pl.ds(4, 4))

    def middle_p():
        copies = []
        for depth, axis in zip(depths, "yx"):
            for k in SHIFTS[axis]:
                ref = w.at[0, 4, c, depth, y, xh, xl]
                copies.append(links.copy("midp", len(copies), ref, ref, peer(axis, k)))
        return copies

    def rank_lines(p, at):
        if p == 0:
            return w.at[0, 4, c, depths[0], :, at // 2, lax.rem(at, 2)]
        return w.at[0, 4, c, depths[1], at]

    def along_x(slot, at):
        return w.at[0, slot, c, :, :, at // 2, lax.rem(at, 2)]

    def along_y(slot, at):
        return w.at[1, slot, c, :, at]

    def bulk(g):
        copies = []
        for i, k in enumerate(SHIFTS["x"]):
            ref = along_x(g, x)
            copies.append(links.copy("bulk", g * 6 + i, ref, ref, peer("x", k)))
        for i, k in enumerate(SHIFTS["y"]):
            ref = along_y(g, y)
            copies.append(links.copy("bulk", g * 6 + 3 + i, ref, ref, peer("y", k)))
        return copies

    def bulk_p():
        copies = []
        for p, axis in enumerate("xy"):
            ref = rank_lines(p, where[axis])
            for k in SHIFTS[axis]:
                copies.append(links.copy("bulk_p", len(copies), ref, ref, peer(axis, k)))
        return copies

    def across(g):
        refs = [along_x(g, x), along_y(g, y)]
        refs += [along_x(g, shifted(where, "x", -k)) for k in SHIFTS["x"]]
        refs += [along_y(g, shifted(where, "y", -k)) for k in SHIFTS["y"]]
        return [links.copy("across", g * 8 + i, r, r, sibling) for i, r in enumerate(refs)]

    def across_p():
        refs = [rank_lines(0, x), rank_lines(1, y)]
        for p, axis in enumerate("xy"):
            refs += [rank_lines(p, shifted(where, axis, -k)) for k in SHIFTS[axis]]
        return [links.copy("across_p", i, r, r, sibling) for i, r in enumerate(refs)]

    def open_bulk(g):
        start(bulk(g))
        start(across(g)[:2])

    def forward(g):
        for got, on in zip(bulk(g), across(g)[2:]):
            got.wait_recv()
            on.start()

    def across_last():
        refs = [w.at[:, 3, c, z]]
        refs += [w.at[:, 3, c, shifted(where, "z", -k)] for k in SHIFTS["z"]]
        return [links.copy("across", 24 + i, r, r, sibling) for i, r in enumerate(refs)]

    mids = [middle(g) for g in range(GROUPS - 1)]
    mid_rank = middle_p()
    received(z_first)
    start(mids[0])
    received(z_rank)
    start(mid_rank)
    received(x_last)
    start(y_last)
    received(mids[0])
    open_bulk(0)
    received(z_rest)
    start(mids[1])
    received(mid_rank)
    start(bulk_p())
    start(across_p()[:2])
    received(y_last)
    start(z_last)
    start(across_last()[:1])

    spread = lax.broadcasted_iota(jnp.int32, (RANK, 256), 1)
    source = lax.broadcasted_iota(jnp.int32, (RANK, 256), 0)
    diagonal = (spread & 15) == (lax.broadcasted_iota(jnp.int32, (RANK, 256), 0) & 15)
    own_rows = own_p[...].astype(BF16)
    for n in range(16):
        kk = n * 16 + (spread >> 4)
        pick = (source == ((kk & 127) * 2 + (kk >> 7))).astype(F32).astype(BF16)
        line = dot(own_rows, pick)
        for i in range(4):
            columns = slice(n % 8 * 256, n % 8 * 256 + 256)
            lhs[n // 8, i * 16 : (i + 1) * 16, columns] = jnp.where(
                diagonal[:16], line[i : i + 1, :], F32(0.0)
            ).astype(BF16)

    received(mids[1])
    open_bulk(1)
    start(mids[2])
    forward(0)

    lane = lax.broadcasted_iota(jnp.int32, (1, 128), 1)
    firsts = (lane < 64).astype(F32).astype(BF16)
    masks = (firsts, 1 - firsts)

    def weight(slot, low_x, core):
        halves = [w[a, slot, core, :, :, :, low_x].reshape(WIDTH, 128) for a in range(2)]
        return jnp.concatenate(halves, axis=1)

    def project(g):
        for src, low_x, core, out in (
            (normed, 0, 0, q_s), (normed, 0, 1, k_s), (normed, 1, 0, v_s), (gout_ref, 1, 1, gh_s)
        ):
            res = dot(src[...], weight(g, low_x, core))
            out[0] = res[:, :128].astype(out.dtype)
            out[1] = res[:, 128:].astype(out.dtype)

    def project_rank():
        both = [w[0, 4, core, :, :, :, 0].reshape(WIDTH, 128) for core in range(2)]
        proj = jnp.concatenate(both, axis=1)
        for src, out in ((normed, np_t), (gout_ref, gp_t)):
            high, rest = split(dot(src[...], proj).T)
            out[:, :TOK] = high
            out[:, TOK:] = rest

    def core_copy(g):
        return links.copy("core", g, low_s.at[g, 1 - c], r0.at[g], sibling)

    def sum1(g):
        return [
            links.copy("sum1", g * 3 + i, s1.at[g, i], v1.at[g, i], peer("x", k))
            for i, k in enumerate(SHIFTS["x"])
        ]

    def sum2(g):
        return [
            links.copy(
                "sum2", g * 3 + i, acc.at[g, shifted(where, "y", k)], v2.at[g, i], peer("y", k)
            )
            for i, k in enumerate(SHIFTS["y"])
        ]

    def stage_one(g):
        core_copy(g).wait_recv()
        copies = sum1(g)
        for i, k in enumerate(SHIFTS["x"]):
            to = shifted(where, "x", k)
            value = low_s[g, c, to] + r0[g, to]
            s1[g, i] = value.reshape(32, 4 * UNIT).astype(BF16)
            copies[i].start()
        acc[g] = low_s[g, c, x] + r0[g, x]

    def stage_two(g):
        received(sum1(g))
        total = (v1[g, 0].astype(F32) + v1[g, 1].astype(F32)) + v1[g, 2].astype(F32)
        acc[g] = acc[g] + total.reshape(NY, 8, 4 * UNIT)
        start(sum2(g))

    def stage_three(g):
        received(sum2(g))
        total = acc[g, y] + ((v2[g, 0] + v2[g, 1]) + v2[g, 2])
        h = g // 2
        for block in range(4):
            columns = pl.ds(
                pl.multiple_of(block * 2 * UNIT + lax.rem(g, 2) * UNIT, UNIT), UNIT
            )
            for i in range(NZ):
                rows[h, i, :, columns] = total[i : i + 1, block * UNIT : (block + 1) * UNIT]

    def sum3(h):
        return [
            links.copy(
                "sum3", h * 7 + i, rows.at[h, shifted(where, "z", k)], v3.at[h, i], peer("z", k)
            )
            for i, k in enumerate(SHIFTS["z"])
        ]

    def dir_z(h):
        own = tiles.at[h, c, z, y, x]
        return [
            links.copy("dir_z", h * 7 + i, own, own, peer("z", k))
            for i, k in enumerate(SHIFTS["z"])
        ]

    def summed(h):
        received(sum3(h))
        low = rows[h, z]
        for i in range(NZ - 1):
            low = low + v3[h, i]
        for block in range(4):
            columns = slice(block * WIDTH + h * 512, block * WIDTH + h * 512 + 512)
            part = low[:, block * 512 : (block + 1) * 512]
            low_out[:, columns] = part
            _, _, direction = adam(part, first_ref[:, columns], second_ref[:, columns])
            for a in range(4):
                dir_rows[block * 4 + a : block * 4 + a + 1, :] = direction[
                    :, a * 128 : (a + 1) * 128
                ]
        tiles[h, c, z, y, x] = dir_rows[...].astype(BF16)
        start(dir_z(h))

    paths = ((pl.ds(0, 4), "y", "x"), (pl.ds(4, 4), "x", "y"))

    def dir_mid(h):
        copies = []
        for depth, axis, _ in paths:
            own = tiles.at[h, c, depth, y, x]
            for k in SHIFTS[axis]:
                copies.append(
                    links.copy("dir_mid", h * 6 + len(copies), own, own, peer(axis, k))
                )
        return copies

    def lines(h, p, at):
        depth = paths[p][0]
        return tiles.at[h, c, depth, :, at] if p == 0 else tiles.at[h, c, depth, at]

    def dir_last(h):
        copies = []
        for p, (_, _, axis) in enumerate(paths):
            own = lines(h, p, where[axis])
            for k in SHIFTS[axis]:
                copies.append(
                    links.copy("dir_last", h * 6 + len(copies), own, own, peer(axis, k))
                )
        return copies

    def dir_across(h):
        refs = [lines(h, p, where[paths[p][2]]) for p in range(2)]
        for p, (_, _, axis) in enumerate(paths):
            refs += [lines(h, p, shifted(where, axis, -k)) for k in SHIFTS[axis]]
        return [
            links.copy("dir_across", h * 8 + i, r, r, sibling) for i, r in enumerate(refs)
        ]

    def hand_on(h):
        for got, on in zip(dir_last(h), dir_across(h)[2:]):
            got.wait_recv()
            on.start()

    def step_of(h):
        columns = slice(h * 128, (h + 1) * 128)
        own = dot(lhs[c], tiles[h, c].reshape(RANK * 8, 128))
        received(dir_across(h))
        step_ref[:, columns] = own + dot(lhs[1 - c], tiles[h, 1 - c].reshape(RANK * 8, 128))

    @pl.loop(0, 2 * GROUPS)
    def _(t):
        g, i = t // 2, lax.rem(t, 2)

        @pl.when(i == 0)
        def _():
            @pl.when(g < GROUPS - 1)
            def _():
                received(across(g))

            @pl.when(g == GROUPS - 1)
            def _():
                received(across_last())

            project(g)

        @pl.when(i == 1)
        def _():
            @pl.when(g == 0)
            def _():
                received(mids[2])
                open_bulk(2)

        def between():
            @pl.when((i == 0) & (g > 0))
            def _():
                stage_one(g - 1)

            @pl.when((i == 1) & (g < GROUPS - 2))
            def _():
                forward(g + 1)

            @pl.when((i == 1) & (g == GROUPS - 2))
            def _():
                for got, on in zip(z_last, across_last()[1:]):
                    got.wait_recv()
                    on.start()

            @pl.when(t == 0)
            def _():
                for got, on in zip(bulk_p(), across_p()[2:]):
                    got.wait_recv()
                    on.start()

        gq_t, gk, gv, attended_t = attend_pair(
            q_s[i], k_s[i], v_s[i], gh_s[i], bias, masks, between
        )

        @pl.when(t == 0)
        def _():
            received(across_p())
            project_rank()

        gq_t = (gq_t * 0.125).astype(BF16)
        low_q = dot(np_t[...], jnp.concatenate([gq_t, gq_t], axis=1), ROWS)
        grads = jnp.concatenate([(gk * 0.125).astype(BF16), gv.astype(BF16)], axis=1)
        low_kv = dot(np_t[...], jnp.concatenate([grads, grads], axis=0))
        attended_t = attended_t.astype(BF16)
        outer = dot(gp_t[...], jnp.concatenate([attended_t, attended_t], axis=1), ROWS)
        values = (low_q, low_kv[:, :128], low_kv[:, 128:], outer)
        for block in range(4):
            columns = pl.ds(pl.multiple_of(block * UNIT + i * 128, 128), 128)
            low_s[g, :, :, :, :, columns] = values[block].reshape(NC, NX, NY, NZ, 128)

        @pl.when(i == 1)
        def _():
            core_copy(g).start()

            @pl.when(g > 0)
            def _():
                stage_two(g - 1)

        @pl.when((i == 0) & (g > 1))
        def _():
            stage_three(g - 2)

            @pl.when(g == 3)
            def _():
                start(sum3(0))

    stage_one(GROUPS - 1)
    stage_three(GROUPS - 2)
    stage_two(GROUPS - 1)
    summed(0)
    stage_three(GROUPS - 1)
    start(sum3(1))
    received(dir_z(0))
    start(dir_mid(0))
    received(dir_mid(0))
    start(dir_last(0))
    start(dir_across(0)[:2])
    summed(1)
    hand_on(0)
    received(dir_z(1))
    start(dir_mid(1))
    step_of(0)
    received(dir_mid(1))
    start(dir_last(1))
    start(dir_across(1)[:2])
    hand_on(1)
    step_of(1)

    sent(quad + z_first + z_rank + z_rest + mid_rank)
    for copies in mids:
        sent(copies)
    sent(bulk_p() + across_p())

    @pl.loop(0, GROUPS)
    def _(g):
        sent([core_copy(g)] + sum1(g) + sum2(g))

        @pl.when(g < GROUPS - 1)
        def _():
            sent(bulk(g) + across(g))

    sent(x_last + y_last + z_last + across_last())

    for h in range(2):
        sent(sum3(h) + dir_z(h) + dir_mid(h) + dir_last(h) + dir_across(h))


def main(lengths, inputs, grad_out, gain, master, projector, first, second):
    vmem = pl.BlockSpec(memory_space=pltpu.VMEM)
    return pl.pallas_call(
        main_kernel,
        out_shape=(
            jax.ShapeDtypeStruct((64, 256), F32),
            jax.ShapeDtypeStruct((1, 4 * WIDTH), F32),
        ),
        in_specs=[pl.BlockSpec(memory_space=pltpu.SMEM)] + [vmem] * 7,
        out_specs=(vmem, vmem),
        scratch_shapes=[
            pltpu.VMEM((2, 5, NC, NZ, NY, 2, 2, 16, 128), BF16),
            pltpu.VMEM((4, 4, WIDTH), F32),
            pltpu.VMEM((4, 4, RANK), F32),
            pltpu.VMEM((4, RANK), F32),
            pltpu.VMEM((16, WIDTH), F32),
            pltpu.VMEM((16, RANK), F32),
            pltpu.VMEM((RANK, RANK), BF16),
            pltpu.VMEM((TOK, WIDTH), BF16),
            pltpu.VMEM((TOK, TOK), F32),
            pltpu.VMEM((RANK, 2 * TOK), BF16),
            pltpu.VMEM((RANK, 2 * TOK), BF16),
            pltpu.VMEM((2, TOK, 128), BF16),
            pltpu.VMEM((2, TOK, 128), BF16),
            pltpu.VMEM((2, TOK, 128), BF16),
            pltpu.VMEM((2, TOK, 128), F32),
            pltpu.VMEM((GROUPS, NC, NX, NY, NZ, 4 * UNIT), F32),
            pltpu.VMEM((GROUPS, NX, NY, NZ, 4 * UNIT), F32),
            pltpu.VMEM((GROUPS, 3, 32, 4 * UNIT), BF16),
            pltpu.VMEM((GROUPS, 3, 32, 4 * UNIT), BF16),
            pltpu.VMEM((GROUPS, NY, NZ, 4 * UNIT), F32),
            pltpu.VMEM((GROUPS, 3, NZ, 4 * UNIT), F32),
            pltpu.VMEM((2, NZ, 1, 2 * WIDTH), F32),
            pltpu.VMEM((2, NZ - 1, 1, 2 * WIDTH), F32),
            pltpu.VMEM((16, 128), F32),
            pltpu.VMEM((2, NC, NZ, NY, NX, 16, 128), BF16),
            pltpu.VMEM((NC, 64, 2 * WIDTH), BF16),
            pltpu.SemaphoreType.DMA((N_SEMS,)),
            pltpu.SemaphoreType.DMA((N_SEMS,)),
        ],
        compiler_params=pltpu.CompilerParams(
            collective_id=0, has_side_effects=True, vmem_limit_bytes=VMEM_LIMIT
        ),
        name="galore_step",
    )(lengths, inputs, grad_out, gain, master, projector, first, second)


def finish_kernel(
    step_ref, low_ref, first_ref, second_ref, master_ref, new_master, new_first, new_second
):
    first, second, _ = adam(low_ref[...], first_ref[...], second_ref[...])
    new_first[...] = first
    new_second[...] = second
    for a in range(16):
        for h in range(2):
            at = (a // 4) * WIDTH + h * 512 + (a % 4) * 128
            columns = slice(at, at + 128)
            for i in range(4):
                row = i * 16 + a
                new_master[i : i + 1, columns] = (
                    master_ref[i : i + 1, columns]
                    - learn_rate * galore_scale * step_ref[row : row + 1, h * 128 : h * 128 + 128]
                )


def finish(step, low, first, second, master):
    vmem = pl.BlockSpec(memory_space=pltpu.VMEM)
    return pl.pallas_call(
        finish_kernel,
        out_shape=(
            jax.ShapeDtypeStruct((4, 4 * WIDTH), F32),
            jax.ShapeDtypeStruct((1, 4 * WIDTH), F32),
            jax.ShapeDtypeStruct((1, 4 * WIDTH), F32),
        ),
        in_specs=[vmem] * 5,
        out_specs=(vmem, vmem, vmem),
        name="outputs",
    )(step, low, first, second, master)


def shards(
    inputs, grad_out, norm_gain, master, projector, moment_first, moment_second, doc_lengths
):
    step, low = main(
        doc_lengths, inputs, grad_out, norm_gain[None, :], master, projector,
        moment_first, moment_second,
    )
    return finish(step, low, moment_first, moment_second, master)


def solution(mesh):
    return jax.shard_map(
        shards,
        mesh=mesh,
        in_specs=(
            P("dp", None),
            P("dp", None),
            P(),
            P("dp", None),
            P("dp", None),
            P("dp", None),
            P("dp", None),
            P("dp", None),
        ),
        out_specs=(P("dp", None), P("dp", None), P("dp", None)),
        check_vma=False,
    )
```
